32 devices in a mesh: item: 4 (over z), pair: 8 (over y, x, core).
Axes of the slice: x: 2, y: 2, z: 4, core: 2. Of those that a mesh axis runs over, the one named last changes fastest.
Arguments:
- pair_act: bfloat16 [4, 384, 384, 128], P('item', 'pair'), may hold values from -6 to 6
- targets: float32 [4, 384, 384], P('item', 'pair'), may hold values from -6 to 6
- pair_mask: int32 [4, 384, 384], P('item', 'pair'), may hold values from 0 to 1
- tri_proj: float32 [1, 128, 640], P(None, 'item'), may hold values from -0.5 to 0.5
- tri_out: float32 [1, 128, 128], P(None, 'item'), may hold values from -0.5 to 0.5
- attention_proj: float32 [1, 128, 512], P(None, 'item'), may hold values from -0.5 to 0.5
- bias_proj: float32 [1, 128, 4], P(None, 'item'), may hold values from -0.5 to 0.5
- output_proj: float32 [1, 128, 128], P(None, 'item'), may hold values from -1.5 to 1.5
- expand_proj: float32 [1, 128, 1024], P(None, 'item'), may hold values from -0.5 to 0.5
- shrink_proj: float32 [1, 512, 128], P(None, 'item'), may hold values from -0.25 to 0.25
- vectors: float32 [5, 128], P(None, 'item'), may hold values from -1 to 3
- first_tri: float32 [1, 128, 640], P(None, 'item'), may hold values from -1.1920929e-06 to 1.1920929e-06
- first_tri_out: float32 [1, 128, 128], P(None, 'item'), may hold values from -1.1920929e-06 to 1.1920929e-06
- first_attention: float32 [1, 128, 512], P(None, 'item'), may hold values from -1.1920929e-06 to 1.1920929e-06
- first_bias: float32 [1, 128, 4], P(None, 'item'), may hold values from -1.1920929e-06 to 1.1920929e-06
- first_output: float32 [1, 128, 128], P(None, 'item'), may hold values from -1.1920929e-06 to 1.1920929e-06
- first_expand: float32 [1, 128, 1024], P(None, 'item'), may hold values from -1.1920929e-06 to 1.1920929e-06
- first_shrink: float32 [1, 512, 128], P(None, 'item'), may hold values from -1.1920929e-06 to 1.1920929e-06
- first_vectors: float32 [5, 128], P(None, 'item'), may hold values from -5.340576e-05 to 5.340576e-05
- second_tri: float32 [1, 128, 640], P(None, 'item'), may hold values from 2.7e-15 to 1.06e-14
- second_tri_out: float32 [1, 128, 128], P(None, 'item'), may hold values from 2.7e-15 to 1.06e-14
- second_attention: float32 [1, 128, 512], P(None, 'item'), may hold values from 2.7e-15 to 1.06e-14
- second_bias: float32 [1, 128, 4], P(None, 'item'), may hold values from 2.7e-15 to 1.06e-14
- second_output: float32 [1, 128, 128], P(None, 'item'), may hold values from 2.7e-15 to 1.06e-14
- second_expand: float32 [1, 128, 1024], P(None, 'item'), may hold values from 2.7e-15 to 1.06e-14
- second_shrink: float32 [1, 512, 128], P(None, 'item'), may hold values from 2.7e-15 to 1.06e-14
- second_vectors: float32 [5, 128], P(None, 'item'), may hold values from 7.8125e-12 to 3.125e-11
Outputs:
- loss_sum: float32 [], replicated
- pair_count: float32 [], replicated
- grad_norm: float32 [], replicated
- new_tri: float32 [1, 128, 640], P(None, 'item')
- new_tri_out: float32 [1, 128, 128], P(None, 'item')
- new_attention: float32 [1, 128, 512], P(None, 'item')
- new_bias: float32 [1, 128, 4], P(None, 'item')
- new_output: float32 [1, 128, 128], P(None, 'item')
- new_expand: float32 [1, 128, 1024], P(None, 'item')
- new_shrink: float32 [1, 512, 128], P(None, 'item')
- new_vectors: float32 [5, 128], P(None, 'item')
- moment_tri: float32 [1, 128, 640], P(None, 'item')
- moment_tri_out: float32 [1, 128, 128], P(None, 'item')
- moment_attention: float32 [1, 128, 512], P(None, 'item')
- moment_bias: float32 [1, 128, 4], P(None, 'item')
- moment_output: float32 [1, 128, 128], P(None, 'item')
- moment_expand: float32 [1, 128, 1024], P(None, 'item')
- moment_shrink: float32 [1, 512, 128], P(None, 'item')
- moment_vectors: float32 [5, 128], P(None, 'item')
- square_tri: float32 [1, 128, 640], P(None, 'item')
- square_tri_out: float32 [1, 128, 128], P(None, 'item')
- square_attention: float32 [1, 128, 512], P(None, 'item')
- square_bias: float32 [1, 128, 4], P(None, 'item')
- square_output: float32 [1, 128, 128], P(None, 'item')
- square_expand: float32 [1, 128, 1024], P(None, 'item')
- square_shrink: float32 [1, 512, 128], P(None, 'item')
- square_vectors: float32 [5, 128], P(None, 'item')
The draws below stay inside these ranges and needn't reach their ends.
All inputs are finite; a program needn't handle non-finite values.
Results may differ from the reference program's by a relative error of at most 0.015.
Values may be sent and summed in bfloat16 or wider, within the bound.
No kernel may reach another device: no remote copies, remote signals or barrier semaphores. Data moves between devices by JAX's collectives and lax.ppermute only.
A program may use at most 640 MiB of HBM per device.

```python
import math
import jax
import jax.numpy as jnp
from jax import lax

C = 128
H = 4
DH = 32
F = 512
L = 1
STEP = 10
N = 384
CROPS = 4


def draw_pair_mask(key, part):
    key = jax.random.fold_in(key, 11)
    rows = lax.broadcasted_iota(jnp.int32, (CROPS, N, N), 1)
    crops = lax.broadcasted_iota(jnp.int32, (CROPS, N, N), 0)
    chance = (100 + 200 * rows // (N - 1)) * (CROPS - 1 + 2 * crops) // (CROPS - 1)
    return (jax.random.randint(key, (CROPS, N, N), 0, 1000) < chance).astype(jnp.int32)


def draw_vectors(key, part):
    key = jax.random.fold_in(key, 23)
    first, second = jax.random.split(key)
    lane = lax.broadcasted_iota(jnp.float32, (4 * L, C), 1) / (C - 1)
    gains = (0.5 + lane) * jax.random.uniform(first, (4 * L, C), jnp.float32, 0.8, 1.25)
    readout = jnp.clip(jax.random.normal(second, (1, C), jnp.float32), -4.0, 4.0) * C ** (-0.5)
    return jnp.concatenate([gains, readout], axis=0)


def shard_levels(stream_key, extent, shards, low, high):
    def one(axis_at, blocks):
        heights = jax.random.uniform(jax.random.fold_in(jax.random.fold_in(stream_key, 6), axis_at), (blocks,), jnp.float32, low / len(shards), high / len(shards))
        return jnp.repeat(jnp.exp(heights), extent[axis_at] // blocks).reshape((-1,) + (1,) * (len(extent) - axis_at - 1))

    loudness = one(*shards[0])
    for cut in shards[1:]:
        loudness = loudness * one(*cut)
    return loudness


def normal_values(stream_key, shape, scale, limit, cuts=(), dtype=jnp.bfloat16):
    loudness = shard_levels(stream_key, shape, cuts, -0.22, 0.18) if cuts else 1.0
    entries = jax.random.normal(stream_key, shape, jnp.float32) * scale * loudness
    return jnp.minimum(jnp.maximum(entries, -limit), limit).astype(dtype)


def setup_inputs(seed: int = 0) -> dict:
    key_list = jax.random.split(jax.random.key(seed), 28)
    return {
        "pair_act": normal_values(key_list[0], (CROPS, N, N, C), 1.0, 6.0, ((0, 4), (1, 8))),
        "targets": normal_values(key_list[1], (CROPS, N, N), 1.0, 6.0, ((0, 4), (1, 8)), jnp.float32),
        "pair_mask": draw_pair_mask(jax.random.fold_in(key_list[27], 71), 0),
        "tri_proj": normal_values(key_list[3], (L, C, 5 * C), C ** -0.5, 0.5, ((1, 4),), jnp.float32),
        "tri_out": normal_values(key_list[4], (L, C, C), C ** -0.5, 0.5, ((1, 4),), jnp.float32),
        "attention_proj": normal_values(key_list[5], (L, C, 4 * C), C ** -0.5, 0.5, ((1, 4),), jnp.float32),
        "bias_proj": normal_values(key_list[6], (L, C, H), C ** -0.5, 0.5, ((1, 4),), jnp.float32),
        "output_proj": normal_values(key_list[7], (L, C, C), (C // 8) ** -0.5, 1.5, ((1, 4),), jnp.float32),
        "expand_proj": normal_values(key_list[8], (L, C, 2 * F), C ** -0.5, 0.5, ((1, 4),), jnp.float32),
        "shrink_proj": normal_values(key_list[9], (L, F, C), F ** -0.5, 0.25, ((1, 4),), jnp.float32),
        "vectors": draw_vectors(jax.random.fold_in(key_list[27], 71), 0),
        "first_tri": normal_values(key_list[11], (L, C, 5 * C), (2e-7), 1.1920928955078125e-06, ((1, 4),), jnp.float32),
        "first_tri_out": normal_values(key_list[12], (L, C, C), (2e-7), 1.1920928955078125e-06, ((1, 4),), jnp.float32),
        "first_attention": normal_values(key_list[13], (L, C, 4 * C), (2e-7), 1.1920928955078125e-06, ((1, 4),), jnp.float32),
        "first_bias": normal_values(key_list[14], (L, C, H), (2e-7), 1.1920928955078125e-06, ((1, 4),), jnp.float32),
        "first_output": normal_values(key_list[15], (L, C, C), (2e-7), 1.1920928955078125e-06, ((1, 4),), jnp.float32),
        "first_expand": normal_values(key_list[16], (L, C, 2 * F), (2e-7), 1.1920928955078125e-06, ((1, 4),), jnp.float32),
        "first_shrink": normal_values(key_list[17], (L, F, C), (2e-7), 1.1920928955078125e-06, ((1, 4),), jnp.float32),
        "first_vectors": normal_values(key_list[18], (4 * L + 1, C), (0.0001 * C ** -0.5), 5.340576171875e-05, ((1, 4),), jnp.float32),
        "second_tri": jnp.clip(jnp.exp(math.log(1.059999984786902e-14) - 1.3676022 * jax.random.uniform(key_list[19], (L, C, 5 * C), jnp.float32) ** shard_levels(key_list[19], (L, C, 5 * C), ((1, 4),), -0.2, 0.2)), 2.7000001050854396e-15, 1.059999984786902e-14),
        "second_tri_out": jnp.clip(jnp.exp(math.log(1.059999984786902e-14) - 1.3676022 * jax.random.uniform(key_list[20], (L, C, C), jnp.float32) ** shard_levels(key_list[20], (L, C, C), ((1, 4),), -0.2, 0.2)), 2.7000001050854396e-15, 1.059999984786902e-14),
        "second_attention": jnp.clip(jnp.exp(math.log(1.059999984786902e-14) - 1.3676022 * jax.random.uniform(key_list[21], (L, C, 4 * C), jnp.float32) ** shard_levels(key_list[21], (L, C, 4 * C), ((1, 4),), -0.2, 0.2)), 2.7000001050854396e-15, 1.059999984786902e-14),
        "second_bias": jnp.clip(jnp.exp(math.log(1.059999984786902e-14) - 1.3676022 * jax.random.uniform(key_list[22], (L, C, H), jnp.float32) ** shard_levels(key_list[22], (L, C, H), ((1, 4),), -0.2, 0.2)), 2.7000001050854396e-15, 1.059999984786902e-14),
        "second_output": jnp.clip(jnp.exp(math.log(1.059999984786902e-14) - 1.3676022 * jax.random.uniform(key_list[23], (L, C, C), jnp.float32) ** shard_levels(key_list[23], (L, C, C), ((1, 4),), -0.2, 0.2)), 2.7000001050854396e-15, 1.059999984786902e-14),
        "second_expand": jnp.clip(jnp.exp(math.log(1.059999984786902e-14) - 1.3676022 * jax.random.uniform(key_list[24], (L, C, 2 * F), jnp.float32) ** shard_levels(key_list[24], (L, C, 2 * F), ((1, 4),), -0.2, 0.2)), 2.7000001050854396e-15, 1.059999984786902e-14),
        "second_shrink": jnp.clip(jnp.exp(math.log(1.059999984786902e-14) - 1.3676022 * jax.random.uniform(key_list[25], (L, F, C), jnp.float32) ** shard_levels(key_list[25], (L, F, C), ((1, 4),), -0.2, 0.2)), 2.7000001050854396e-15, 1.059999984786902e-14),
        "second_vectors": jnp.clip(jnp.exp(math.log(3.124999911618964e-11) - 1.3862944 * jax.random.uniform(key_list[26], (4 * L + 1, C), jnp.float32) ** shard_levels(key_list[26], (4 * L + 1, C), ((1, 4),), -0.2, 0.2)), 7.81249977904741e-12, 3.124999911618964e-11),
    }


@jax.custom_vjp
def low(v):
    return lax.optimization_barrier(v.astype(jnp.bfloat16)).astype(jnp.float32)

@jax.custom_vjp
def low_back(v):
    return v

def low_keep(v):
    return (low(v), None)

def low_pass(kept, grad):
    return (grad,)

def back_keep(v):
    return (v, None)

def back_low(kept, grad):
    return (low(grad),)
low.defvjp(low_keep, low_pass)
low_back.defvjp(back_keep, back_low)
norm_epsilon = 1e-05
clip_limit = 0.001
learn_rate = 0.1
vector_rate = 0.8
beta_first = 0.9
beta_second = 0.999
adam_epsilon = 1e-08
weight_decay = 0.01
highest = lax.Precision.HIGHEST

def normalize(value, gain):
    mean = lax.optimization_barrier(jnp.mean(value, axis=-1, keepdims=True))
    centred = value - mean
    return centred * lax.rsqrt(lax.optimization_barrier(jnp.mean(centred * centred, axis=-1, keepdims=True)) + norm_epsilon) * gain

def project(value, weight):
    return jnp.einsum('...c,cd->...d', value, weight, precision=highest)

def incoming(stream, tri_w, tri_out_w, gain_tri, gain_centre):
    normed = low_back(low(normalize(stream, gain_tri)))
    projected = project(normed, tri_w)
    pieces = [low_back(projected[..., index * C:(index + 1) * C]) for index in range(5)]
    left = low_back(low(jax.nn.sigmoid(pieces[1]) * pieces[0]))
    right = low_back(low(jax.nn.sigmoid(pieces[3]) * pieces[2]))
    product = low_back(jnp.einsum('kic,kjc->ijc', left, right, precision=highest))
    centre = low_back(low(normalize(product, gain_centre)))
    linear = low_back(project(centre, tri_out_w))
    return low_back(low(jax.nn.sigmoid(pieces[4]) * linear))

def column_attend(bias_low, query, keys, values):
    scores = jnp.einsum('ihd,khd->hki', query, keys, precision=highest) * DH ** (-0.5) + bias_low
    scores = low_back(scores)
    probs = jax.nn.softmax(scores, axis=1)
    return low_back(jnp.einsum('hki,khd->ihd', low(probs), values, precision=highest))

def transition_rows(block, gain, expand_w, shrink_w):
    normed = low(normalize(block, gain))
    expanded = low_back(project(normed, expand_w))
    activated = low_back(low(jax.nn.silu(expanded[..., :F]) * expanded[..., F:]))
    return low_back(project(activated, shrink_w))

def layer(stream, tri_w, tri_out_w, project_w, pairbias_w, output_w, expand_w, shrink_w, gain_tri, gain_centre, gain_attend, gain_expand):
    stream = stream + jax.checkpoint(incoming)(stream, tri_w, tri_out_w, gain_tri, gain_centre)
    normed = low_back(low(normalize(stream, gain_attend)))
    projected = project(normed, project_w)
    query = low_back(low(projected[..., :C])).reshape(N, N, H, DH)
    keys = low_back(low(projected[..., C:2 * C])).reshape(N, N, H, DH)
    values = low_back(low(projected[..., 2 * C:3 * C])).reshape(N, N, H, DH)
    gate_logit = low_back(projected[..., 3 * C:])
    bias = low_back(low(project(normed, pairbias_w)))
    bias_low = jnp.transpose(bias, (2, 0, 1))
    attend = jax.checkpoint(column_attend)
    columns = lax.map(lambda item: attend(bias_low, item[0], item[1], item[2]), (jnp.moveaxis(query, 1, 0), jnp.moveaxis(keys, 1, 0), jnp.moveaxis(values, 1, 0)))
    attended = jnp.moveaxis(columns, 0, 1).reshape(N, N, C)
    gated = low(jax.nn.sigmoid(gate_logit) * attended)
    middle = stream + low_back(low(project(gated, output_w)))
    transit = jax.checkpoint(transition_rows)
    blocks = lax.map(lambda block: transit(block, gain_expand, expand_w, shrink_w), middle.reshape(N // 64, 64, N, C))
    return middle + blocks.reshape(N, N, C)

def crop_loss(weights, pair, target, weighting):
    tri_w, tri_out_w, project_w, pairbias_w, output_w, expand_w, shrink_w, vector_low = [low(entry) for entry in weights]
    stream = pair
    for index in range(L):
        stream = jax.checkpoint(layer)(stream, tri_w[index], tri_out_w[index], project_w[index], pairbias_w[index], output_w[index], expand_w[index], shrink_w[index], vector_low[4 * index], vector_low[4 * index + 1], vector_low[4 * index + 2], vector_low[4 * index + 3])
    readout = jnp.einsum('abc,c->ab', stream, vector_low[4 * L], precision=highest)
    error = readout - target
    return jnp.sum(weighting * error * error)

def reference(pair_act, targets, pair_mask, tri_proj, tri_out, attention_proj, bias_proj, output_proj, expand_proj, shrink_proj, vectors, first_tri, first_tri_out, first_attention, first_bias, first_output, first_expand, first_shrink, first_vectors, second_tri, second_tri_out, second_attention, second_bias, second_output, second_expand, second_shrink, second_vectors):
    masters = (tri_proj, tri_out, attention_proj, bias_proj, output_proj, expand_proj, shrink_proj, vectors)
    firsts = (first_tri, first_tri_out, first_attention, first_bias, first_output, first_expand, first_shrink, first_vectors)
    seconds = (second_tri, second_tri_out, second_attention, second_bias, second_output, second_expand, second_shrink, second_vectors)
    rates = (learn_rate,) * 7 + (vector_rate,)
    weighting = pair_mask.astype(jnp.float32)
    count = jnp.sum(weighting)

    def crop_step(carry, item):
        total, grads = carry
        pair, target, crop_weighting = item
        loss, pull = jax.vjp(lambda *weights: crop_loss(weights, pair.astype(jnp.float32), target, crop_weighting), *masters)
        got = pull(jnp.float32(1.0) / count)
        return ((total + loss, tuple((left + right for left, right in zip(grads, got)))), None)
    start = (jnp.zeros((), jnp.float32), tuple((jnp.zeros_like(entry) for entry in masters)))
    (loss_sum, grads), _ = lax.scan(crop_step, start, (pair_act, targets, weighting))
    grad_norm = jnp.sqrt(sum((jnp.sum(entry * entry) for entry in grads)))
    factor = jnp.minimum(1.0, clip_limit / (grad_norm + 1e-06))
    new_masters, new_firsts, new_seconds = ([], [], [])
    for master, grad, first, second, rate in zip(masters, grads, firsts, seconds, rates):
        clipped = grad * factor
        moment = beta_first * first + (1 - beta_first) * clipped
        square = beta_second * second + (1 - beta_second) * clipped * clipped
        stride = moment / (1 - beta_first ** STEP) / (jnp.sqrt(square / (1 - beta_second ** STEP)) + adam_epsilon)
        new_masters.append(master - rate * (stride + weight_decay * master))
        new_firsts.append(moment)
        new_seconds.append(square)
    return (loss_sum, count, grad_norm, new_masters[0], new_masters[1], new_masters[2], new_masters[3], new_masters[4], new_masters[5], new_masters[6], new_masters[7], new_firsts[0], new_firsts[1], new_firsts[2], new_firsts[3], new_firsts[4], new_firsts[5], new_firsts[6], new_firsts[7], new_seconds[0], new_seconds[1], new_seconds[2], new_seconds[3], new_seconds[4], new_seconds[5], new_seconds[6], new_seconds[7])
```

```python
import functools

import jax
import jax.numpy as jnp
from jax import lax
from jax.experimental import pallas as pl
from jax.experimental.pallas import tpu as pltpu
from jax.sharding import PartitionSpec as P

STEP = 10

norm_epsilon = 1e-05
clip_limit = 0.001
learn_rate = 0.1
vector_rate = 0.8
beta_first = 0.9
beta_second = 0.999
adam_epsilon = 1e-08
weight_decay = 0.01

BF = jnp.bfloat16
F32 = jnp.float32
LOG2E = 1.4426950408889634
EPS = norm_epsilon


def normalize(stream, gain):
    mean = jnp.mean(stream, axis=-1, keepdims=True)
    centred = stream - mean
    scale = lax.rsqrt(jnp.mean(centred * centred, axis=-1, keepdims=True) + norm_epsilon)
    normed = centred * scale
    return (normed * gain, normed, scale)


def normalize_back(upstream, gain, normed, scale):
    inner = upstream * gain
    below = scale * (
        inner
        - jnp.mean(inner, axis=-1, keepdims=True)
        - normed * jnp.mean(inner * normed, axis=-1, keepdims=True)
    )
    return (below, jnp.sum(upstream * normed, axis=(0, 1, 2)))


def matmul(value, weight):
    return jnp.einsum("...c,cd->...d", value, weight, preferred_element_type=jnp.float32)


def matmul_back(value, weight):
    return jnp.einsum("...d,cd->...c", value, weight, preferred_element_type=jnp.float32)


def weight_grad(left, right):
    flat_left = left.reshape(-1, left.shape[-1])
    flat_right = right.reshape(-1, right.shape[-1])
    return lax.dot_general(
        flat_left, flat_right, (((0,), (0,)), ((), ())), preferred_element_type=jnp.float32
    )


def rounded(value):
    return value.astype(jnp.bfloat16).astype(jnp.float32)


def nn(a, b):
    return lax.dot_general(a, b, (((1,), (0,)), ((), ())), preferred_element_type=F32)

def nt(a, b):
    return lax.dot_general(a, b, (((1,), (1,)), ((), ())), preferred_element_type=F32)

def sigm(v):
    return 0.5 * jnp.tanh(0.5 * v) + 0.5

def norm(v):
    mean = jnp.mean(v, axis=-1, keepdims=True)
    cen = v - mean
    scale = lax.rsqrt(jnp.mean(cen * cen, axis=-1, keepdims=True) + EPS)
    return cen * scale, scale

def norm_back(up, gain, n, scale):
    inner = up * gain
    return scale * (inner - jnp.mean(inner, axis=-1, keepdims=True) - n * jnp.mean(inner * n, axis=-1, keepdims=True))

def chunks(total, width):
    return [(s, min(width, total - s)) for s in range(0, total, width)]

def column_kernel(heads, after_ref, tgt_ref, msk_ref, bias_ref, w_ref, wt_ref, wo_ref, we_ref, vec_ref, z_ref,
                gx_ref, gmid_ref, gb_ref, gkvw_ref, gqgw_ref, gow_ref, gew_ref, svec_ref, small_ref,
                bias2, e_s, gs_s, acc, qbd, gobd, vaug, qn, gon, ores, cu, hv):
    j = pl.program_id(0)
    last = pl.num_programs(0) - 1
    n, c = after_ref.shape[1], after_ref.shape[2]
    dh = c // heads
    wide = heads * n
    scale = dh ** -0.5

    @pl.when(j == 0)
    def _():
        for h in range(heads):
            bias2[:, h * n:(h + 1) * n] = bias_ref[:, h * n:(h + 1) * n].astype(F32).T * LOG2E
        acc[...] = jnp.zeros_like(acc)
        qbd[...] = jnp.zeros_like(qbd)
        gobd[...] = jnp.zeros_like(gobd)
        lane = lax.broadcasted_iota(jnp.int32, (n, c), 1)
        vaug[:, c:] = jnp.where(lane < 3, 1.0, 0.0).astype(BF)
        for ref in (gkvw_ref, gqgw_ref, gow_ref, gew_ref, svec_ref, small_ref):
            ref[...] = jnp.zeros_like(ref)

    lane = lax.broadcasted_iota(jnp.int32, (n, c), 1)
    g3 = vec_ref[2:3, :]
    g4 = vec_ref[3:4, :]
    wr = vec_ref[4:5, :]
    after = after_ref[0]
    n3, _ = norm(after)
    x = (n3 * g3).astype(BF)
    nat = nn(x, w_ref[:, :3 * c])
    k_nat = nat[:, c:2 * c].astype(BF)
    vaug[:, :c] = nat[:, 2 * c:].astype(BF)
    q_nat = (nat[:, :c] * (scale * LOG2E)).astype(BF)
    for h in range(heads):
        qn[h * n:(h + 1) * n, :] = jnp.where((lane >= h * dh) & (lane < (h + 1) * dh), q_nat, jnp.zeros_like(q_nat))
    tr = nt(wt_ref[...], x)
    q_t = (tr[:c] * (scale * LOG2E)).astype(BF)
    k_t = tr[c:2 * c].astype(BF)
    v_t = jnp.concatenate([tr[2 * c:3 * c], jnp.ones((16, n), F32)], axis=0).astype(BF)
    gate_t = sigm(tr[3 * c:])
    for h in range(heads):
        qbd[h * dh:(h + 1) * dh, h * n:(h + 1) * n] = q_t[h * dh:(h + 1) * dh]

    for s0, w0 in chunks(wide, 256):
        sl = slice(s0, s0 + w0)
        sc = nn(k_nat, qbd[:, sl]) + bias2[:, sl]
        top = jnp.max(sc, axis=0, keepdims=True)
        ex = jnp.exp2(sc - top).astype(BF)
        e_s[:, sl] = ex
        ores[:, sl] = nn(v_t, ex)
    o_parts, r_parts = [], []
    for h in range(heads):
        r = 1.0 / ores[c:c + 1, h * n:(h + 1) * n]
        r_parts.append(r)
        o_parts.append(ores[h * dh:(h + 1) * dh, h * n:(h + 1) * n] * r)
    o_t = jnp.concatenate(o_parts, axis=0)
    y_t = (gate_t * o_t).astype(BF)
    out = nn(y_t.astype(F32).T.astype(BF), wo_ref[...]).astype(BF)
    mid = after + out.astype(F32)

    n4, sc4 = norm(mid)
    t = (n4 * g4).astype(BF)
    f = we_ref.shape[1] // 2
    racc = mid * wr
    for q in range(f // 128):
        u = nn(t, we_ref[:, q * 256:(q + 1) * 256])
        a, b = u[:, :128], u[:, 128:]
        zc = z_ref[:, q * 128:(q + 1) * 128]
        sig = sigm(a)
        silu = a * sig
        h_low = (silu * b).astype(BF)
        hv[:, q * 128:(q + 1) * 128] = h_low
        racc += h_low.astype(F32) * zc
        cu[:, q * 256:q * 256 + 128] = (zc * b * (sig + silu - silu * sig)).astype(BF)
        cu[:, q * 256 + 128:(q + 1) * 256] = (zc * silu).astype(BF)
    readout = jnp.sum(racc, axis=-1, keepdims=True)
    pick = lax.broadcasted_iota(jnp.int32, tgt_ref.shape, 1) == j
    tgt = jnp.sum(jnp.where(pick, tgt_ref[...], 0.0), axis=1, keepdims=True)
    msk = jnp.sum(jnp.where(pick, msk_ref[...], 0.0), axis=1, keepdims=True)
    err = readout - tgt
    wer = msk * err
    gr = 2.0 * wer
    small_ref[0:1, :] += jnp.sum(gr * mid, axis=0, keepdims=True)
    small_ref[2:3, :] += jnp.sum(jnp.where(lane == 0, wer * err, 0.0), axis=0, keepdims=True)
    svec_ref[...] += jnp.sum(gr * hv[...].astype(F32), axis=0, keepdims=True)
    gew_ref[...] += nn((gr * t.astype(F32)).T.astype(BF), cu[...])
    gt = gr * nt(cu[...], we_ref[...])
    small_ref[1:2, :] += jnp.sum(gt * n4, axis=0, keepdims=True)
    gmid = gr * wr + norm_back(gt, g4, n4, sc4)
    gmid_ref[0] = gmid

    gout = gmid.astype(BF)
    gow_ref[...] += nn(y_t, gout)
    gy_t = nt(wo_ref[...], gout)
    ggl_t = gy_t * o_t * gate_t * (1.0 - gate_t)
    go_t = (gy_t * gate_t).astype(BF).astype(F32)
    row = lax.broadcasted_iota(jnp.int32, (16, n), 0)
    gos = []
    for h in range(heads):
        part = (go_t[h * dh:(h + 1) * dh] * r_parts[h]).astype(BF)
        gobd[h * dh:(h + 1) * dh, h * n:(h + 1) * n] = part
        part = part.astype(F32)
        gos.append(part)
        d = -jnp.sum(part * o_parts[h], axis=0, keepdims=True)
        hi = d.astype(BF).astype(F32)
        mi = (d - hi).astype(BF).astype(F32)
        lo = d - hi - mi
        gobd[c:, h * n:(h + 1) * n] = jnp.where(row == 0, hi, jnp.where(row == 1, mi, jnp.where(row == 2, lo, 0.0))).astype(BF)
    go_n = jnp.concatenate(gos, axis=0).T.astype(BF)
    for h in range(heads):
        gon[h * n:(h + 1) * n, :] = jnp.where((lane >= h * dh) & (lane < (h + 1) * dh), go_n, jnp.zeros_like(go_n))

    vk = vaug[:, :c + 16]
    for s0, w0 in chunks(wide, 256):
        sl = slice(s0, s0 + w0)
        g = e_s[:, sl].astype(F32) * nn(vk, gobd[:, sl])
        acc[:, sl] += g
        gl = g.astype(BF)
        gs_s[:, sl] = gl
        ores[:c, sl] = nn(k_t, gl)
    gq_t = jnp.concatenate([ores[h * dh:(h + 1) * dh, h * n:(h + 1) * n] for h in range(heads)], axis=0) * scale
    gqg_t = jnp.concatenate([gq_t, ggl_t], axis=0).astype(BF)
    gk = nn(gs_s[...], qn[...]) * (1.0 / LOG2E)
    gv = nn(e_s[...], gon[...])
    gkv = jnp.concatenate([gk, gv], axis=1).astype(BF)
    gqgw_ref[...] += nn(gqg_t, x)
    gkvw_ref[...] += nn(x.astype(F32).T.astype(BF), gkv)
    w_qg = jnp.concatenate([w_ref[:, :c], w_ref[:, 3 * c:]], axis=1)
    gx_ref[0] = nt(gkv, w_ref[:, c:3 * c]) + nn(w_qg, gqg_t).T

    @pl.when(j == last)
    def _():
        for h in range(heads):
            gb_ref[:, h * n:(h + 1) * n] = acc[:, h * n:(h + 1) * n].T.astype(gb_ref.dtype)


def column_pass(after, tgt, msk, bias, w, wt, wo, we, vec, z):
    cols, n, c = after.shape
    heads = bias.shape[1] // n
    f = we.shape[1] // 2
    wide = heads * n
    full = lambda shape: pl.BlockSpec(shape, lambda j: (0,) * len(shape))
    col = pl.BlockSpec((1, n, c), lambda j: (j, 0, 0))
    outs = [
        jax.ShapeDtypeStruct((cols, n, c), F32),
        jax.ShapeDtypeStruct((cols, n, c), F32),
        jax.ShapeDtypeStruct((n, wide), BF),
        jax.ShapeDtypeStruct((c, 2 * c), F32),
        jax.ShapeDtypeStruct((2 * c, c), F32),
        jax.ShapeDtypeStruct((c, c), F32),
        jax.ShapeDtypeStruct((c, 2 * f), F32),
        jax.ShapeDtypeStruct((1, f), F32),
        jax.ShapeDtypeStruct((8, c), F32),
    ]
    return pl.pallas_call(
        functools.partial(column_kernel, heads),
        grid=(cols,),
        in_specs=[col] + [full(v.shape) for v in (tgt, msk, bias, w, wt, wo, we, vec, z)],
        out_specs=[col, col] + [full(o.shape) for o in outs[2:]],
        out_shape=outs,
        scratch_shapes=[
            pltpu.VMEM((n, wide), F32),
            pltpu.VMEM((n, wide), BF),
            pltpu.VMEM((n, wide), BF),
            pltpu.VMEM((n, wide), F32),
            pltpu.VMEM((c, wide), BF),
            pltpu.VMEM((c + 16, wide), BF),
            pltpu.VMEM((n, 2 * c), BF),
            pltpu.VMEM((wide, c), BF),
            pltpu.VMEM((wide, c), BF),
            pltpu.VMEM((c + 16, wide), F32),
            pltpu.VMEM((n, 2 * f), BF),
            pltpu.VMEM((n, f), BF),
        ],
        compiler_params=pltpu.CompilerParams(vmem_limit_bytes=56 << 20),
        name="columns",
    )(after, tgt, msk, bias, w, wt, wo, we, vec, z)


def incoming_parts(stream, tri_w, gain_tri):
    normed_in, normed, scale = normalize(stream, gain_tri)
    normed_low = normed_in.astype(jnp.bfloat16)
    projected = matmul(normed_low, tri_w)
    width = tri_w.shape[0]
    pieces = [projected[..., index * width : (index + 1) * width] for index in range(5)]
    left = (jax.nn.sigmoid(pieces[1]) * pieces[0]).astype(jnp.bfloat16)
    right = (jax.nn.sigmoid(pieces[3]) * pieces[2]).astype(jnp.bfloat16)
    return (normed_low, normed, scale, pieces, left, right)


def incoming_forward(stream, tri_w, tri_out_w, gain_tri, gain_centre):
    _, _, _, pieces, left, right = incoming_parts(stream, tri_w, gain_tri)
    part = jnp.einsum(
        "bkic,bkjc->bijc",
        lax.all_gather(left, "pair", axis=2, tiled=True),
        right,
        preferred_element_type=jnp.float32,
    )
    centre_in, _, _ = normalize(part, gain_centre)
    linear = matmul(centre_in.astype(jnp.bfloat16), tri_out_w)
    branch = (jax.nn.sigmoid(pieces[4]) * linear).astype(jnp.bfloat16)
    return (stream + branch.astype(jnp.float32), part)


def incoming_back(upstream, stream, product, tri_w, tri_out_w, gain_tri, gain_centre):
    normed_low, normed, scale, pieces, left, right = incoming_parts(stream, tri_w, gain_tri)
    centre_in, centre_normed, centre_scale = normalize(product, gain_centre)
    centre_low = centre_in.astype(jnp.bfloat16)
    linear = matmul(centre_low, tri_out_w)
    gate = jax.nn.sigmoid(pieces[4])
    grad_branch = rounded(upstream)
    grad_linear = (grad_branch * gate).astype(jnp.bfloat16)
    grad_gate = grad_branch * linear * gate * (1.0 - gate)
    grad_tri_out = weight_grad(centre_low, grad_linear)
    grad_centre = rounded(matmul_back(grad_linear, tri_out_w))
    grad_product, grad_gain_centre = normalize_back(
        grad_centre, gain_centre, centre_normed, centre_scale
    )
    grad_low = grad_product.astype(jnp.bfloat16)
    row_view = lax.all_to_all(grad_low, "pair", split_axis=1, concat_axis=2, tiled=True)
    left_piece = lax.all_gather(left, "pair", axis=2, tiled=True)
    right_piece = lax.all_gather(right, "pair", axis=2, tiled=True)
    grad_right = jnp.einsum(
        "bkic,bijc->bkjc", left_piece, grad_low, preferred_element_type=jnp.float32
    )
    grad_left = jnp.einsum(
        "bkjc,bijc->bkic", right_piece, row_view, preferred_element_type=jnp.float32
    )
    grad_left = rounded(grad_left)
    grad_right = rounded(grad_right)
    sig_left = jax.nn.sigmoid(pieces[1])
    sig_right = jax.nn.sigmoid(pieces[3])
    grad_projected = jnp.concatenate(
        [
            grad_left * sig_left,
            grad_left * pieces[0] * sig_left * (1.0 - sig_left),
            grad_right * sig_right,
            grad_right * pieces[2] * sig_right * (1.0 - sig_right),
            grad_gate,
        ],
        axis=-1,
    ).astype(jnp.bfloat16)
    grad_tri = weight_grad(normed_low, grad_projected)
    grad_normed = rounded(matmul_back(grad_projected, tri_w))
    below, grad_gain_tri = normalize_back(grad_normed, gain_tri, normed, scale)
    return (upstream + below, grad_tri, grad_tri_out, grad_gain_tri, grad_gain_centre)


def gather_weights(tri, tri_out, attn, bias, outp, expand, shrink, vectors):
    rows = tri.shape[1]
    pieces = [tri[0], tri_out[0], attn[0], outp[0], expand[0], shrink[0].reshape(rows, -1), bias[0], vectors.T]
    widths = [p.shape[1] for p in pieces]
    packed = lax.all_gather(jnp.concatenate([p.astype(BF) for p in pieces], axis=1), "item", axis=0, tiled=True)
    got, at = [], 0
    for w in widths:
        got.append(packed[:, at : at + w])
        at += w
    tri, tri_out, attn, outp, expand, shr, bias, vec = got
    return tri, tri_out, attn, bias, outp, expand, shr.reshape(-1, shrink.shape[2]), vec.T


def on_device(
    pair_act,
    targets,
    pair_mask,
    tri_proj,
    tri_out,
    attention_proj,
    bias_proj,
    output_proj,
    expand_proj,
    shrink_proj,
    vectors,
    first_tri,
    first_tri_out,
    first_attention,
    first_bias,
    first_output,
    first_expand,
    first_shrink,
    first_vectors,
    second_tri,
    second_tri_out,
    second_attention,
    second_bias,
    second_output,
    second_expand,
    second_shrink,
    second_vectors,
):
    layers = attention_proj.shape[0]
    assert layers == 1
    weight = gather_weights(
        tri_proj, tri_out, attention_proj, bias_proj, output_proj, expand_proj, shrink_proj, vectors
    )
    tri_w, tri_out_w, project_w, pairbias_w, output_w, expand_w, shrink_w, vector_low = weight
    vec = vector_low.astype(F32)
    weighting_rows = pair_mask.astype(F32)
    stream = lax.all_to_all(pair_act, "pair", split_axis=2, concat_axis=1, tiled=True).astype(F32)
    both = lax.all_to_all(
        jnp.concatenate([targets, weighting_rows]), "pair", split_axis=2, concat_axis=1, tiled=True
    )
    after, product = incoming_forward(stream, tri_w, tri_out_w, vec[0], vec[1])
    after_c = jnp.swapaxes(after[0], 0, 1)
    inputs_col = normalize(after_c, vec[2])[0].astype(BF)
    cols, tokens, width = after_c.shape
    bias_part = jnp.swapaxes(matmul(inputs_col, pairbias_w).astype(BF), 1, 2)
    bias_full = lax.all_gather(bias_part.reshape(cols, -1), "pair", axis=0, tiled=True)
    hidden = expand_w.shape[1] // 2
    expand_mix = (
        expand_w.reshape(width, 2, hidden // 128, 128).swapaxes(1, 2).reshape(width, 2 * hidden)
    )
    z = jnp.sum(shrink_w.astype(F32) * vec[4], axis=1)[None]
    vec8 = jnp.concatenate([vec, jnp.zeros((3, width), F32)])
    gx, upstream, gb, gkv_w, gqg_w, gow, gew, svec, small = column_pass(
        after_c, both[0], both[1], bias_full, project_w, project_w.T, output_w, expand_mix, vec8, z
    )
    bias_cols = lax.psum_scatter(gb.astype(F32), "pair", scatter_dimension=0, tiled=True)
    bias_low = jnp.swapaxes(bias_cols.reshape(cols, -1, tokens), 1, 2).astype(BF)
    grad_pairbias = weight_grad(inputs_col, bias_low)
    grad_inputs = rounded(gx + matmul_back(bias_low, pairbias_w))
    _, normed, scale = normalize(after_c, vec[2])
    below, grad_gain_attend = normalize_back(grad_inputs[None], vec[2], normed[None], scale[None])
    upstream = jnp.swapaxes(upstream + below[0], 0, 1)[None]
    upstream, grad_tri, grad_tri_out, grad_gain_tri, grad_gain_centre = incoming_back(
        upstream, stream, product, tri_w, tri_out_w, vec[0], vec[1]
    )
    summed = lax.psum(
        (
            grad_tri,
            grad_tri_out,
            gkv_w,
            gqg_w,
            grad_pairbias,
            gow,
            gew,
            svec,
            small,
            jnp.stack([grad_gain_tri, grad_gain_centre, grad_gain_attend]),
            jnp.sum(weighting_rows),
        ),
        ("item", "pair"),
    )
    g_tri, g_tri_out, g_kv, g_qg, g_bias, g_out, g_exp, s_sum, sm, gains, count = summed
    g_project = jnp.concatenate([g_qg[:width].T, g_kv, g_qg[width:].T], axis=1)
    g_expand = (
        g_exp.reshape(width, hidden // 128, 2, 128).swapaxes(1, 2).reshape(width, 2 * hidden)
    )
    g_shrink = s_sum[0][:, None] * vec[4][None, :]
    g_read = sm[0] + jnp.sum(s_sum[0][:, None] * shrink_w.astype(F32), axis=0)
    g_vec = jnp.concatenate([gains, sm[1:2], g_read[None]])
    grads = [
        g / count for g in (g_tri, g_tri_out, g_project, g_bias, g_out, g_expand, g_shrink, g_vec)
    ]
    loss_sum = jnp.sum(sm[2])
    grad_norm = jnp.sqrt(sum(jnp.sum(g * g) for g in grads))
    factor = jnp.minimum(1.0, clip_limit / (grad_norm + 1e-06))
    place = lax.axis_index("item")
    shards = []
    for master, grad in zip((tri_proj, tri_out, attention_proj, bias_proj, output_proj, expand_proj, shrink_proj), grads):
        rows = master.shape[1]
        shards.append(lax.dynamic_slice_in_dim(grad, place * rows, rows, 0)[None])
    shards.append(lax.dynamic_slice_in_dim(grads[7], place * vectors.shape[1], vectors.shape[1], 1))
    masters = (
        tri_proj,
        tri_out,
        attention_proj,
        bias_proj,
        output_proj,
        expand_proj,
        shrink_proj,
        vectors,
    )
    firsts = (
        first_tri,
        first_tri_out,
        first_attention,
        first_bias,
        first_output,
        first_expand,
        first_shrink,
        first_vectors,
    )
    seconds = (
        second_tri,
        second_tri_out,
        second_attention,
        second_bias,
        second_output,
        second_expand,
        second_shrink,
        second_vectors,
    )
    rates = (learn_rate,) * 7 + (vector_rate,)
    new_masters, new_firsts, new_seconds = ([], [], [])
    for master, grad, first, second, rate in zip(masters, shards, firsts, seconds, rates):
        clipped = grad * factor
        moment = beta_first * first + (1 - beta_first) * clipped
        square = beta_second * second + (1 - beta_second) * clipped * clipped
        stride = (
            moment
            / (1 - beta_first**STEP)
            / (jnp.sqrt(square / (1 - beta_second**STEP)) + adam_epsilon)
        )
        new_masters.append(master - rate * (stride + weight_decay * master))
        new_firsts.append(moment)
        new_seconds.append(square)
    return (
        (loss_sum, count, grad_norm) + tuple(new_masters) + tuple(new_firsts) + tuple(new_seconds)
    )


def solution(mesh):
    in_specs = (
        P("item", "pair", None, None),
        P("item", "pair", None),
        P("item", "pair", None),
        P(None, "item", None),
        P(None, "item", None),
        P(None, "item", None),
        P(None, "item", None),
        P(None, "item", None),
        P(None, "item", None),
        P(None, "item", None),
        P(None, "item"),
        P(None, "item", None),
        P(None, "item", None),
        P(None, "item", None),
        P(None, "item", None),
        P(None, "item", None),
        P(None, "item", None),
        P(None, "item", None),
        P(None, "item"),
        P(None, "item", None),
        P(None, "item", None),
        P(None, "item", None),
        P(None, "item", None),
        P(None, "item", None),
        P(None, "item", None),
        P(None, "item", None),
        P(None, "item"),
    )
    out_specs = (
        P(),
        P(),
        P(),
        P(None, "item", None),
        P(None, "item", None),
        P(None, "item", None),
        P(None, "item", None),
        P(None, "item", None),
        P(None, "item", None),
        P(None, "item", None),
        P(None, "item"),
        P(None, "item", None),
        P(None, "item", None),
        P(None, "item", None),
        P(None, "item", None),
        P(None, "item", None),
        P(None, "item", None),
        P(None, "item", None),
        P(None, "item"),
        P(None, "item", None),
        P(None, "item", None),
        P(None, "item", None),
        P(None, "item", None),
        P(None, "item", None),
        P(None, "item", None),
        P(None, "item", None),
        P(None, "item"),
    )
    return jax.shard_map(
        on_device, mesh=mesh, in_specs=in_specs, out_specs=out_specs, check_vma=False
    )
```

```python
import functools

import jax
import jax.numpy as jnp
from jax import lax
from jax.experimental import pallas as pl
from jax.experimental.pallas import tpu as pltpu
from jax.sharding import PartitionSpec as P

STEP = 10

norm_epsilon = 1e-05
clip_limit = 0.001
learn_rate = 0.1
vector_rate = 0.8
beta_first = 0.9
beta_second = 0.999
adam_epsilon = 1e-08
weight_decay = 0.01

BF = jnp.bfloat16
F32 = jnp.float32
LOG2E = 1.4426950408889634
EPS = norm_epsilon


def nn(a, b):
    return lax.dot_general(a, b, (((1,), (0,)), ((), ())), preferred_element_type=F32)

def nt(a, b):
    return lax.dot_general(a, b, (((1,), (1,)), ((), ())), preferred_element_type=F32)

def sigm(v):
    return 0.5 * jnp.tanh(0.5 * v) + 0.5

def norm(v):
    mean = jnp.mean(v, axis=-1, keepdims=True)
    cen = v - mean
    scale = lax.rsqrt(jnp.mean(cen * cen, axis=-1, keepdims=True) + EPS)
    return cen * scale, scale

def norm_back(up, gain, n, scale):
    inner = up * gain
    return scale * (inner - jnp.mean(inner, axis=-1, keepdims=True) - n * jnp.mean(inner * n, axis=-1, keepdims=True))

def chunks(total, width):
    return [(s, min(width, total - s)) for s in range(0, total, width)]

def column_kernel(heads, after_ref, tgt_ref, msk_ref, bias_ref, w_ref, wt_ref, wo_ref, we_ref, vec_ref, z_ref,
                gx_ref, gmid_ref, gb_ref, gkvw_ref, gqgw_ref, gow_ref, gew_ref, svec_ref, small_ref,
                bias2, e_s, gs_s, acc, qbd, gobd, vaug, qn, gon, ores, cu, hv):
    j = pl.program_id(0)
    last = pl.num_programs(0) - 1
    n, c = after_ref.shape[1], after_ref.shape[2]
    dh = c // heads
    wide = heads * n
    scale = dh ** -0.5

    @pl.when(j == 0)
    def _():
        for h in range(heads):
            bias2[:, h * n:(h + 1) * n] = bias_ref[:, h * n:(h + 1) * n].astype(F32).T * LOG2E
        acc[...] = jnp.zeros_like(acc)
        qbd[...] = jnp.zeros_like(qbd)
        gobd[...] = jnp.zeros_like(gobd)
        lane = lax.broadcasted_iota(jnp.int32, (n, c), 1)
        vaug[:, c:] = jnp.where(lane < 3, 1.0, 0.0).astype(BF)
        for ref in (gkvw_ref, gqgw_ref, gow_ref, gew_ref, svec_ref, small_ref):
            ref[...] = jnp.zeros_like(ref)

    lane = lax.broadcasted_iota(jnp.int32, (n, c), 1)
    g3 = vec_ref[2:3, :]
    g4 = vec_ref[3:4, :]
    wr = vec_ref[4:5, :]
    after = after_ref[0]
    n3, _ = norm(after)
    x = (n3 * g3).astype(BF)
    nat = nn(x, w_ref[:, :3 * c])
    k_nat = nat[:, c:2 * c].astype(BF)
    vaug[:, :c] = nat[:, 2 * c:].astype(BF)
    q_nat = (nat[:, :c] * (scale * LOG2E)).astype(BF)
    for h in range(heads):
        qn[h * n:(h + 1) * n, :] = jnp.where((lane >= h * dh) & (lane < (h + 1) * dh), q_nat, jnp.zeros_like(q_nat))
    tr = nt(wt_ref[...], x)
    q_t = (tr[:c] * (scale * LOG2E)).astype(BF)
    k_t = tr[c:2 * c].astype(BF)
    v_t = jnp.concatenate([tr[2 * c:3 * c], jnp.ones((16, n), F32)], axis=0).astype(BF)
    gate_t = sigm(tr[3 * c:])
    for h in range(heads):
        qbd[h * dh:(h + 1) * dh, h * n:(h + 1) * n] = q_t[h * dh:(h + 1) * dh]

    for s0, w0 in chunks(wide, 256):
        sl = slice(s0, s0 + w0)
        sc = nn(k_nat, qbd[:, sl]) + bias2[:, sl]
        top = jnp.max(sc, axis=0, keepdims=True)
        ex = jnp.exp2(sc - top).astype(BF)
        e_s[:, sl] = ex
        ores[:, sl] = nn(v_t, ex)
    o_parts, r_parts = [], []
    for h in range(heads):
        r = 1.0 / ores[c:c + 1, h * n:(h + 1) * n]
        r_parts.append(r)
        o_parts.append(ores[h * dh:(h + 1) * dh, h * n:(h + 1) * n] * r)
    o_t = jnp.concatenate(o_parts, axis=0)
    y_t = (gate_t * o_t).astype(BF)
    out = nn(y_t.astype(F32).T.astype(BF), wo_ref[...]).astype(BF)
    mid = after + out.astype(F32)

    n4, sc4 = norm(mid)
    t = (n4 * g4).astype(BF)
    f = we_ref.shape[1] // 2
    racc = mid * wr
    for q in range(f // 128):
        u = nn(t, we_ref[:, q * 256:(q + 1) * 256])
        a, b = u[:, :128], u[:, 128:]
        zc = z_ref[:, q * 128:(q + 1) * 128]
        sig = sigm(a)
        silu = a * sig
        h_low = (silu * b).astype(BF)
        hv[:, q * 128:(q + 1) * 128] = h_low
        racc += h_low.astype(F32) * zc
        cu[:, q * 256:q * 256 + 128] = (zc * b * (sig + silu - silu * sig)).astype(BF)
        cu[:, q * 256 + 128:(q + 1) * 256] = (zc * silu).astype(BF)
    readout = jnp.sum(racc, axis=-1, keepdims=True)
    pick = lax.broadcasted_iota(jnp.int32, tgt_ref.shape, 1) == j
    tgt = jnp.sum(jnp.where(pick, tgt_ref[...], 0.0), axis=1, keepdims=True)
    msk = jnp.sum(jnp.where(pick, msk_ref[...], 0.0), axis=1, keepdims=True)
    err = readout - tgt
    wer = msk * err
    gr = 2.0 * wer
    small_ref[0:1, :] += jnp.sum(gr * mid, axis=0, keepdims=True)
    small_ref[2:3, :] += jnp.sum(jnp.where(lane == 0, wer * err, 0.0), axis=0, keepdims=True)
    svec_ref[...] += jnp.sum(gr * hv[...].astype(F32), axis=0, keepdims=True)
    gew_ref[...] += nn((gr * t.astype(F32)).T.astype(BF), cu[...])
    gt = gr * nt(cu[...], we_ref[...])
    small_ref[1:2, :] += jnp.sum(gt * n4, axis=0, keepdims=True)
    gmid = gr * wr + norm_back(gt, g4, n4, sc4)
    gmid_ref[0] = gmid

    gout = gmid.astype(BF)
    gow_ref[...] += nn(y_t, gout)
    gy_t = nt(wo_ref[...], gout)
    ggl_t = gy_t * o_t * gate_t * (1.0 - gate_t)
    go_t = (gy_t * gate_t).astype(BF).astype(F32)
    row = lax.broadcasted_iota(jnp.int32, (16, n), 0)
    gos = []
    for h in range(heads):
        part = (go_t[h * dh:(h + 1) * dh] * r_parts[h]).astype(BF)
        gobd[h * dh:(h + 1) * dh, h * n:(h + 1) * n] = part
        part = part.astype(F32)
        gos.append(part)
        d = -jnp.sum(part * o_parts[h], axis=0, keepdims=True)
        hi = d.astype(BF).astype(F32)
        mi = (d - hi).astype(BF).astype(F32)
        lo = d - hi - mi
        gobd[c:, h * n:(h + 1) * n] = jnp.where(row == 0, hi, jnp.where(row == 1, mi, jnp.where(row == 2, lo, 0.0))).astype(BF)
    go_n = jnp.concatenate(gos, axis=0).T.astype(BF)
    for h in range(heads):
        gon[h * n:(h + 1) * n, :] = jnp.where((lane >= h * dh) & (lane < (h + 1) * dh), go_n, jnp.zeros_like(go_n))

    vk = vaug[:, :c + 16]
    for s0, w0 in chunks(wide, 256):
        sl = slice(s0, s0 + w0)
        g = e_s[:, sl].astype(F32) * nn(vk, gobd[:, sl])
        acc[:, sl] += g
        gl = g.astype(BF)
        gs_s[:, sl] = gl
        ores[:c, sl] = nn(k_t, gl)
    gq_t = jnp.concatenate([ores[h * dh:(h + 1) * dh, h * n:(h + 1) * n] for h in range(heads)], axis=0) * scale
    gqg_t = jnp.concatenate([gq_t, ggl_t], axis=0).astype(BF)
    gk = nn(gs_s[...], qn[...]) * (1.0 / LOG2E)
    gv = nn(e_s[...], gon[...])
    gkv = jnp.concatenate([gk, gv], axis=1).astype(BF)
    gqgw_ref[...] += nn(gqg_t, x)
    gkvw_ref[...] += nn(x.astype(F32).T.astype(BF), gkv)
    w_qg = jnp.concatenate([w_ref[:, :c], w_ref[:, 3 * c:]], axis=1)
    gx_ref[0] = nt(gkv, w_ref[:, c:3 * c]) + nn(w_qg, gqg_t).T

    @pl.when(j == last)
    def _():
        for h in range(heads):
            gb_ref[:, h * n:(h + 1) * n] = acc[:, h * n:(h + 1) * n].T.astype(gb_ref.dtype)


def column_pass(after, tgt, msk, bias, w, wt, wo, we, vec, z):
    cols, n, c = after.shape
    heads = bias.shape[1] // n
    f = we.shape[1] // 2
    wide = heads * n
    full = lambda shape: pl.BlockSpec(shape, lambda j: (0,) * len(shape))
    col = pl.BlockSpec((1, n, c), lambda j: (j, 0, 0))
    outs = [
        jax.ShapeDtypeStruct((cols, n, c), F32),
        jax.ShapeDtypeStruct((cols, n, c), F32),
        jax.ShapeDtypeStruct((n, wide), BF),
        jax.ShapeDtypeStruct((c, 2 * c), F32),
        jax.ShapeDtypeStruct((2 * c, c), F32),
        jax.ShapeDtypeStruct((c, c), F32),
        jax.ShapeDtypeStruct((c, 2 * f), F32),
        jax.ShapeDtypeStruct((1, f), F32),
        jax.ShapeDtypeStruct((8, c), F32),
    ]
    return pl.pallas_call(
        functools.partial(column_kernel, heads),
        grid=(cols,),
        in_specs=[col] + [full(v.shape) for v in (tgt, msk, bias, w, wt, wo, we, vec, z)],
        out_specs=[col, col] + [full(o.shape) for o in outs[2:]],
        out_shape=outs,
        scratch_shapes=[
            pltpu.VMEM((n, wide), F32),
            pltpu.VMEM((n, wide), BF),
            pltpu.VMEM((n, wide), BF),
            pltpu.VMEM((n, wide), F32),
            pltpu.VMEM((c, wide), BF),
            pltpu.VMEM((c + 16, wide), BF),
            pltpu.VMEM((n, 2 * c), BF),
            pltpu.VMEM((wide, c), BF),
            pltpu.VMEM((wide, c), BF),
            pltpu.VMEM((c + 16, wide), F32),
            pltpu.VMEM((n, 2 * f), BF),
            pltpu.VMEM((n, f), BF),
        ],
        compiler_params=pltpu.CompilerParams(vmem_limit_bytes=56 << 20),
        name="columns",
    )(after, tgt, msk, bias, w, wt, wo, we, vec, z)


GROUP = 16


def spread(scr, start, count, stride, value):
    for t in range(scr.shape[0]):
        scr[t, pl.ds(start, count, stride=stride), :] = value[:, t * 128 : (t + 1) * 128]


def joined(scr, rows=slice(None)):
    return jnp.concatenate([scr[t, rows] for t in range(scr.shape[0])], axis=1)


def padded(count):
    return -(-count // 128) * 128


def operand_kernel(cols, off_ref, x_ref, wl_ref, wr_ref, *refs):
    left_ref, right_ref, n_ref, nc_ref, xc_ref, lscr, rscr, nscr, xscr, cscr = refs[-10:]
    rows, n, c = x_ref.shape
    half = wl_ref.shape[0] // 2
    wide = nc_ref.shape[1]
    own = off_ref[0]
    other = off_ref[1]

    def step(k, carry):
        x = x_ref[k].astype(F32)
        nrm, _ = norm(x)
        low = nrm.astype(BF)
        n_ref[k] = low
        nscr[...] = nrm
        xscr[...] = x
        p = nt(wl_ref[...], low)
        spread(lscr, k, half, rows, p[:half] * sigm(p[half:]))
        near = [nscr[pl.ds(own, cols), :], nscr[pl.ds(other, cols), :]]
        if wide > 2 * cols:
            near.append(jnp.zeros((wide - 2 * cols, c), F32))
        near = jnp.concatenate(near, axis=0).astype(BF)
        nc_ref[k] = near
        p = nt(wr_ref[...], near)
        spread(rscr, k, half, rows, p[:half] * sigm(p[half:]))
        cscr[pl.ds(k, cols, stride=rows), :] = xscr[pl.ds(own, cols), :]
        return carry

    lax.fori_loop(0, rows, step, 0)
    left_ref[...] = joined(lscr).astype(BF).reshape(left_ref.shape)
    right_ref[...] = joined(rscr).astype(BF).reshape(right_ref.shape)
    xc_ref[...] = cscr[...].astype(BF).reshape(xc_ref.shape)


def operands(offs, x, wl, wr, cols, place, bufs):
    n, c = x.shape[1], x.shape[2]
    half = wl.shape[0] // 2
    wide = padded(2 * cols)
    g = GROUP
    shapes = [
        ((half, n, n), (half, g, n), lambda b: (0, place(b), 0)),
        ((half, n, wide), (half, g, wide), lambda b: (0, place(b), 0)),
        ((n, n, c), (g, n, c), lambda b: (place(b), 0, 0)),
        ((n, wide, c), (g, wide, c), lambda b: (place(b), 0, 0)),
        ((cols, n, c), (cols, g, c), lambda b: (0, place(b), 0)),
    ]
    full = lambda v: pl.BlockSpec(v.shape, lambda b: (0,) * v.ndim)
    ins = [offs, x, wl, wr]
    specs = [
        pl.BlockSpec(memory_space=pltpu.SMEM),
        pl.BlockSpec((g, n, c), lambda b: (b, 0, 0)),
        full(wl),
        full(wr),
    ]
    alias = {}
    if bufs is not None:
        alias = {4 + i: i for i in range(5)}
        ins += list(bufs)
        specs += [pl.BlockSpec(memory_space=pl.ANY)] * 5
    return pl.pallas_call(
        functools.partial(operand_kernel, cols),
        grid=(x.shape[0] // g,),
        in_specs=specs,
        out_specs=[pl.BlockSpec(b, m) for _, b, m in shapes],
        out_shape=[jax.ShapeDtypeStruct(s, BF) for s, _, _ in shapes],
        scratch_shapes=[
            pltpu.VMEM((n // 128, half * g, 128), F32),
            pltpu.VMEM((wide // 128, half * g, 128), F32),
            pltpu.VMEM((n, c), F32),
            pltpu.VMEM((n, c), F32),
            pltpu.VMEM((cols * g, c), F32),
        ],
        input_output_aliases=alias,
        compiler_params=pltpu.CompilerParams(vmem_limit_bytes=56 << 20),
        name="operands",
    )(*ins)


def product_kernel(left_ref, right_ref, mine_ref, theirs_ref, scr):
    g = left_ref.shape[0]
    cols = mine_ref.shape[0]
    for e in range(g):
        part = lax.dot_general(right_ref[e], left_ref[e], (((0,), (0,)), ((), ())), preferred_element_type=F32)
        spread(scr, e, 2 * cols, g, part[: 2 * cols])
    mine_ref[...] = joined(scr, slice(0, cols * g)).astype(mine_ref.dtype).reshape(mine_ref.shape)
    theirs_ref[...] = joined(scr, slice(cols * g, None)).astype(theirs_ref.dtype).reshape(theirs_ref.shape)


def products(left, right, cols):
    half, n, _ = left.shape
    wide = right.shape[2]
    g = GROUP
    out = jax.ShapeDtypeStruct((cols, half, n), BF)
    return pl.pallas_call(
        product_kernel,
        grid=(half // g,),
        in_specs=[pl.BlockSpec((g, n, n), lambda b: (b, 0, 0)), pl.BlockSpec((g, n, wide), lambda b: (b, 0, 0))],
        out_specs=[pl.BlockSpec((cols, g, n), lambda b: (0, b, 0))] * 2,
        out_shape=[out, out],
        scratch_shapes=[pltpu.VMEM((n // 128, 2 * cols * g, 128), F32)],
        compiler_params=pltpu.CompilerParams(vmem_limit_bytes=56 << 20),
        name="products",
    )(left, right)


def after_kernel(heads, xc_ref, mine_ref, theirs_ref, w4_ref, wout_ref, wb_ref, vec_ref, after_ref, bias_ref):
    n, c = xc_ref.shape[1:]
    x = xc_ref[0].astype(F32)
    n0, _ = norm(x)
    gate = sigm(nn(n0.astype(BF), w4_ref[...]))
    prod = jnp.concatenate([mine_ref[0].astype(F32), theirs_ref[0].astype(F32)], axis=0).T
    nc, _ = norm(prod)
    lin = nn((nc * vec_ref[1:2, :]).astype(BF), wout_ref[...])
    after = x + (gate * lin).astype(BF).astype(F32)
    after_ref[0] = after
    n3, _ = norm(after)
    bias = nt(wb_ref[...], (n3 * vec_ref[2:3, :]).astype(BF))
    for h in range(heads):
        bias_ref[0, :, h * n:(h + 1) * n] = bias[h:h + 1]


def afters(xc, mine, theirs, w4, wout, wb, vec, heads):
    cols, n, c = xc.shape
    half = mine.shape[1]
    full = lambda v: pl.BlockSpec(v.shape, lambda b: (0,) * v.ndim)
    col = lambda a, b: pl.BlockSpec((1, a, b), lambda j: (j, 0, 0))
    return pl.pallas_call(
        functools.partial(after_kernel, heads),
        grid=(cols,),
        in_specs=[col(n, c), col(half, n), col(half, n), full(w4), full(wout), full(wb), full(vec)],
        out_specs=[col(n, c), col(1, heads * n)],
        out_shape=[jax.ShapeDtypeStruct((cols, n, c), F32), jax.ShapeDtypeStruct((cols, 1, heads * n), F32)],
        compiler_params=pltpu.CompilerParams(vmem_limit_bytes=40 << 20),
        name="afters",
    )(xc, mine, theirs, w4, wout, wb, vec)


def back_kernel(after_ref, gx_ref, gmid_ref, gb_ref, xc_ref, mine_ref, theirs_ref, w4_ref, wout_ref, wb_ref, vec_ref,
                gmine_ref, gtheirs_ref, gwb_ref, gwout_ref, gw4_ref, small_ref):
    j = pl.program_id(0)

    @pl.when(j == 0)
    def _():
        for ref in (gwb_ref, gwout_ref, gw4_ref, small_ref):
            ref[...] = jnp.zeros_like(ref)

    n, c = xc_ref.shape[1:]
    half = mine_ref.shape[1]
    heads = gb_ref.shape[2]
    g1 = vec_ref[1:2, :]
    g2 = vec_ref[2:3, :]
    n3, s3 = norm(after_ref[0])
    x3 = (n3 * g2).astype(BF)
    gb = gb_ref[0, 0].astype(F32)
    for d in range(1, gb_ref.shape[0]):
        gb = gb + gb_ref[d, 0].astype(F32)
    gb = jnp.concatenate([gb, jnp.zeros((wb_ref.shape[0] - heads, n), F32)], axis=0)
    gwb_ref[...] += nn(gb.astype(BF), x3)
    gx = (gx_ref[0] + nn(gb.T.astype(BF), wb_ref[...])).astype(BF).astype(F32)
    small_ref[0:1, :] += jnp.sum(gx * n3, axis=0, keepdims=True)
    gafter = (gmid_ref[0] + norm_back(gx, g2, n3, s3)).astype(BF).astype(F32)

    n0, _ = norm(xc_ref[0].astype(F32))
    n0 = n0.astype(BF)
    gate = sigm(nn(n0, w4_ref[...]))
    prod = jnp.concatenate([mine_ref[0].astype(F32), theirs_ref[0].astype(F32)], axis=0).T
    nc, sc = norm(prod)
    centre = (nc * g1).astype(BF)
    lin = nn(centre, wout_ref[...])
    glin = (gafter * gate).astype(BF)
    gp4 = (gafter * lin * gate * (1.0 - gate)).astype(BF)
    gwout_ref[...] += nn(centre.astype(F32).T.astype(BF), glin)
    gw4_ref[...] += nn(n0.astype(F32).T.astype(BF), gp4)
    gc = nt(glin, wout_ref[...]).astype(BF).astype(F32)
    small_ref[1:2, :] += jnp.sum(gc * nc, axis=0, keepdims=True)
    gprod = norm_back(gc, g1, nc, sc).T
    gmine_ref[0] = gprod[:half].astype(BF)
    gtheirs_ref[0] = gprod[half:].astype(BF)


def back_pass(after, gx, gmid, gb, xc, mine, theirs, w4, wout, wb, vec):
    cols, n, c = xc.shape
    half = mine.shape[1]
    heads = gb.shape[2]
    full = lambda shape: pl.BlockSpec(shape, lambda b: (0,) * len(shape))
    col = lambda a, b: pl.BlockSpec((1, a, b), lambda j: (j, 0, 0))
    accs = [wb.shape, (c, c), (c, c), (8, c)]
    return pl.pallas_call(
        back_kernel,
        grid=(cols,),
        in_specs=[col(n, c)] * 3 + [pl.BlockSpec((gb.shape[0], 1, heads, n), lambda j: (0, j, 0, 0)), col(n, c), col(half, n), col(half, n)]
        + [full(v.shape) for v in (w4, wout, wb, vec)],
        out_specs=[col(half, n)] * 2 + [full(s) for s in accs],
        out_shape=[jax.ShapeDtypeStruct((cols, half, n), BF)] * 2 + [jax.ShapeDtypeStruct(s, F32) for s in accs],
        compiler_params=pltpu.CompilerParams(vmem_limit_bytes=40 << 20),
        name="back",
    )(after, gx, gmid, gb, xc, mine, theirs, w4, wout, wb, vec)


def operand_grads_kernel(left_ref, right_ref, gm_ref, gt_ref, gl_ref, gr_ref, scr, lscr, rscr):
    g, n, _ = left_ref.shape
    cols = gm_ref.shape[0]
    wide = right_ref.shape[2]
    gm = gm_ref[...].astype(F32).reshape(cols * g, n)
    gt = gt_ref[...].astype(F32).reshape(cols * g, n)
    for t in range(n // 128):
        scr[t, : cols * g] = gm[:, t * 128 : (t + 1) * 128]
        scr[t, cols * g :] = gt[:, t * 128 : (t + 1) * 128]
    for e in range(g):
        gp = jnp.concatenate([scr[t, pl.ds(e, 2 * cols, stride=g), :] for t in range(n // 128)], axis=1)
        if wide > 2 * cols:
            gp = jnp.concatenate([gp, jnp.zeros((wide - 2 * cols, n), F32)], axis=0)
        gp = gp.astype(BF)
        spread(rscr, e, n, g, nt(left_ref[e], gp))
        spread(lscr, e, n, g, nn(right_ref[e], gp))
    gl_ref[...] = joined(lscr).astype(BF).reshape(gl_ref.shape)
    gr_ref[...] = joined(rscr).astype(BF).reshape(gr_ref.shape)


def operand_grads(left, right, gmine, gtheirs):
    half, n, _ = left.shape
    wide = right.shape[2]
    cols = gmine.shape[0]
    g = GROUP
    return pl.pallas_call(
        operand_grads_kernel,
        grid=(half // g,),
        in_specs=[pl.BlockSpec((g, n, n), lambda b: (b, 0, 0)), pl.BlockSpec((g, n, wide), lambda b: (b, 0, 0))]
        + [pl.BlockSpec((cols, g, n), lambda b: (0, b, 0))] * 2,
        out_specs=[pl.BlockSpec((n, g, n), lambda b: (0, b, 0)), pl.BlockSpec((n, g, wide), lambda b: (0, b, 0))],
        out_shape=[jax.ShapeDtypeStruct((n, half, n), BF), jax.ShapeDtypeStruct((n, half, wide), BF)],
        scratch_shapes=[
            pltpu.VMEM((n // 128, 2 * cols * g, 128), F32),
            pltpu.VMEM((n // 128, n * g, 128), F32),
            pltpu.VMEM((wide // 128, n * g, 128), F32),
        ],
        compiler_params=pltpu.CompilerParams(vmem_limit_bytes=60 << 20),
        name="operand_grads",
    )(left, right, gmine, gtheirs)


def tri_grads_kernel(n_ref, nc_ref, gl_ref, gr_ref, wl_ref, wr_ref, al_ref, ar_ref):
    @pl.when(pl.program_id(0) == 0)
    def _():
        al_ref[...] = jnp.zeros_like(al_ref)
        ar_ref[...] = jnp.zeros_like(ar_ref)

    rows = n_ref.shape[0]
    half = gl_ref.shape[1]

    def one(low, grad, w):
        p = nt(w, low)
        s = sigm(p[half:])
        first = grad.astype(F32) * s
        gp = jnp.concatenate([first, first * p[:half] * (1.0 - s)], axis=0).astype(BF)
        return nn(gp, low)

    left = al_ref[...]
    right = ar_ref[...]
    for k in range(rows):
        left += one(n_ref[k], gl_ref[k], wl_ref[...])
        right += one(nc_ref[k], gr_ref[k], wr_ref[...])
    al_ref[...] = left
    ar_ref[...] = right


def tri_grads(nrm, near, gl, gr, wl, wr):
    n, _, c = nrm.shape
    half = gl.shape[1]
    wide = near.shape[1]
    rows = 8
    full = lambda v: pl.BlockSpec(v.shape, lambda b: (0,) * v.ndim)
    row = lambda a, b: pl.BlockSpec((rows, a, b), lambda k: (k, 0, 0))
    out = jax.ShapeDtypeStruct((2 * half, c), F32)
    return pl.pallas_call(
        tri_grads_kernel,
        grid=(n // rows,),
        in_specs=[row(n, c), row(wide, c), row(half, n), row(half, wide), full(wl), full(wr)],
        out_specs=[pl.BlockSpec(out.shape, lambda k: (0, 0))] * 2,
        out_shape=[out] * 2,
        compiler_params=pltpu.CompilerParams(vmem_limit_bytes=40 << 20),
        name="tri_grads",
    )(nrm, near, gl, gr, wl, wr)


def gather_weights(tri, tri_out, attn, bias, outp, expand, shrink, vectors):
    rows = tri.shape[1]
    pieces = [tri[0], tri_out[0], attn[0], outp[0], expand[0], shrink[0].reshape(rows, -1), bias[0], vectors.T]
    widths = [p.shape[1] for p in pieces]
    packed = lax.all_gather(jnp.concatenate([p.astype(BF) for p in pieces], axis=1), "item", axis=0, tiled=True)
    got, at = [], 0
    for w in widths:
        got.append(packed[:, at : at + w])
        at += w
    tri, tri_out, attn, outp, expand, shr, bias, vec = got
    return tri, tri_out, attn, bias, outp, expand, shr.reshape(-1, shrink.shape[2]), vec.T


def gather_rows(pair_act, pieces):
    rows = pair_act.shape[1] // pieces
    return [
        lax.all_gather(pair_act[0, m * rows : (m + 1) * rows], "pair", axis=0, tiled=True)
        for m in range(pieces)
    ]


def swap_cores(value):
    size = lax.axis_size("pair")
    return lax.ppermute(value, "pair", [(d, d ^ 1) for d in range(size)])


def exchange(value, axis, bit):
    size = lax.axis_size(axis)
    return lax.ppermute(value, axis, [(d, d ^ bit) for d in range(size)])


def sum_axis(value, axis):
    bit = 1
    while bit < lax.axis_size(axis):
        value = value + exchange(value, axis, bit)
        bit *= 2
    return value


def sum_all(value):
    return sum_axis(sum_axis(value, "item"), "pair")


def sum_shards(parts):
    size = lax.axis_size("item")
    here = lax.axis_index("item")
    bit = size // 2
    while bit:
        upper = (here // bit) % 2
        kept, sent = [], []
        for part in parts:
            rows = part.shape[0] // 2
            kept.append(lax.dynamic_slice_in_dim(part, upper * rows, rows, 0))
            sent.append(lax.dynamic_slice_in_dim(part, (1 - upper) * rows, rows, 0))
        parts = [k + exchange(s.astype(BF), "item", bit).astype(F32) for k, s in zip(kept, sent)]
        bit //= 2
    return [sum_axis(part, "pair") for part in parts]


def on_device(
    pair_act,
    targets,
    pair_mask,
    tri_proj,
    tri_out,
    attention_proj,
    bias_proj,
    output_proj,
    expand_proj,
    shrink_proj,
    vectors,
    first_tri,
    first_tri_out,
    first_attention,
    first_bias,
    first_output,
    first_expand,
    first_shrink,
    first_vectors,
    second_tri,
    second_tri_out,
    second_attention,
    second_bias,
    second_output,
    second_expand,
    second_shrink,
    second_vectors,
):
    layers = attention_proj.shape[0]
    assert layers == 1
    cols, tokens, width = pair_act.shape[1:]
    half = width // 2
    heads = bias_proj.shape[2]
    here = lax.axis_index("pair")
    core = here % 2
    pieces = 3 if cols % (3 * GROUP) == 0 else 1
    gathered = gather_rows(pair_act, pieces)
    weight = gather_weights(
        tri_proj, tri_out, attention_proj, bias_proj, output_proj, expand_proj, shrink_proj, vectors
    )
    tri_w, tri_out_w, project_w, pairbias_w, output_w, expand_w, shrink_w, vector_low = weight
    vec = vector_low.astype(F32)
    weighting_rows = pair_mask.astype(F32)
    both = lax.all_to_all(
        jnp.concatenate([targets, weighting_rows]), "pair", split_axis=2, concat_axis=1, tiled=True
    )

    scaled = (tri_w.astype(F32) * vec[0][:, None]).astype(BF).T
    halves = [
        lax.dynamic_slice_in_dim(scaled, width * s + half * core, half, 0) for s in range(4)
    ]
    w_left = jnp.concatenate(halves[:2])
    w_right = jnp.concatenate(halves[2:])
    w_gate = scaled[4 * width :].T
    wout = jnp.roll(tri_out_w, -half * core, axis=0)
    gain_c = jnp.roll(vec[1], -half * core)
    vec8 = jnp.concatenate([vec[:1], gain_c[None], vec[2:], jnp.zeros((3, width), F32)])
    wb = jnp.concatenate([pairbias_w.T, jnp.zeros((16 - heads, width), BF)])

    offs = jnp.stack([here * cols, (here + 1 - 2 * core) * cols]).astype(jnp.int32)
    span = cols // pieces // GROUP
    bufs = None
    for m in range(pieces):
        if pieces == 1:
            place = lambda b: b
        else:
            place = lambda b, m=m: (b // span) * (span * pieces) + m * span + b % span
        bufs = operands(offs, gathered[m], w_left, w_right, cols, place, bufs)
    left, right, nrm, near, xc = bufs
    mine, send = products(left, right, cols)
    theirs = swap_cores(send)
    after_c, bias_part = afters(xc, mine, theirs, w_gate, wout, wb, vec8, heads)
    bias_full = lax.all_gather(bias_part[:, 0].astype(BF), "pair", axis=0, tiled=True)
    hidden = expand_w.shape[1] // 2
    expand_mix = (
        expand_w.reshape(width, 2, hidden // 128, 128).swapaxes(1, 2).reshape(width, 2 * hidden)
    )
    z = jnp.sum(shrink_w.astype(F32) * vec[4], axis=1)[None]
    gx, gmid, gb, gkv_w, gqg_w, gow, gew, svec, small = column_pass(
        after_c, both[0], both[1], bias_full, project_w, project_w.T, output_w, expand_mix, vec8, z
    )
    bias_cols = lax.all_to_all(gb, "pair", split_axis=0, concat_axis=0, tiled=True)
    early = sum_shards(
        [
            jnp.concatenate(
                [gqg_w[:width].T, gkv_w, gqg_w[width:].T, gow, gew, svec.reshape(width, -1)], axis=1
            )
        ]
    )
    scalars = sum_all(jnp.stack([jnp.sum(small[2]), jnp.sum(weighting_rows)]))
    gmine, gsend, gwb, gwout, gw4, small2 = back_pass(
        after_c, gx, gmid, bias_cols.reshape(-1, cols, heads, tokens), xc, mine, theirs,
        w_gate, wout, wb, vec8,
    )
    gtheirs = swap_cores(gsend)
    gl, gr = operand_grads(left, right, gmine, gtheirs)
    al, ar = tri_grads(nrm, near, gl, gr, w_left, w_right)

    def halfway(part):
        zero = jnp.zeros_like(part)
        return [jnp.where(core == 0, part, zero), jnp.where(core == 1, part, zero)]

    a_tri = jnp.concatenate(
        halfway(al[:half]) + halfway(al[half:]) + halfway(ar[:half]) + halfway(ar[half:]) + [gw4.T]
    ).T
    g_read = small[0] + jnp.sum(svec[0][:, None] * shrink_w.astype(F32), axis=0)
    g_vec = jnp.stack(
        [
            jnp.sum(a_tri * tri_w.astype(F32), axis=1),
            jnp.roll(small2[1], half * core),
            small2[0],
            small[1],
            g_read,
        ]
    )
    late = sum_shards(
        [
            jnp.concatenate(
                [a_tri * vec[0][:, None], jnp.roll(gwout, half * core, axis=0), gwb[:heads].T, g_vec.T],
                axis=1,
            )
        ]
    )
    loss_sum, count = scalars[0], scalars[1]
    at = [width * s for s in range(11)]
    tall = early[0]
    shards = [
        late[0][:, : at[5]],
        late[0][:, at[5] : at[6]],
        tall[:, : at[4]],
        late[0][:, at[6] : at[6] + heads],
        tall[:, at[4] : at[5]],
        tall[:, at[5] : at[5] + 2 * hidden].reshape(-1, hidden // 128, 2, 128).swapaxes(1, 2).reshape(-1, 2 * hidden),
        tall[:, at[5] + 2 * hidden :].reshape(-1, 1) * vec[4][None, :],
        late[0][:, at[6] + heads :].T,
    ]
    shards = [s / count for s in shards]
    squares = sum_axis(sum(jnp.sum(s * s) for s in shards), "item")
    grad_norm = jnp.sqrt(squares)
    factor = jnp.minimum(1.0, clip_limit / (grad_norm + 1e-06))
    shards = [s[None] for s in shards[:7]] + shards[7:]
    masters = (
        tri_proj,
        tri_out,
        attention_proj,
        bias_proj,
        output_proj,
        expand_proj,
        shrink_proj,
        vectors,
    )
    firsts = (
        first_tri,
        first_tri_out,
        first_attention,
        first_bias,
        first_output,
        first_expand,
        first_shrink,
        first_vectors,
    )
    seconds = (
        second_tri,
        second_tri_out,
        second_attention,
        second_bias,
        second_output,
        second_expand,
        second_shrink,
        second_vectors,
    )
    rates = (learn_rate,) * 7 + (vector_rate,)
    new_masters, new_firsts, new_seconds = ([], [], [])
    for master, grad, first, second, rate in zip(masters, shards, firsts, seconds, rates):
        clipped = grad * factor
        moment = beta_first * first + (1 - beta_first) * clipped
        square = beta_second * second + (1 - beta_second) * clipped * clipped
        stride = (
            moment
            / (1 - beta_first**STEP)
            / (jnp.sqrt(square / (1 - beta_second**STEP)) + adam_epsilon)
        )
        new_masters.append(master - rate * (stride + weight_decay * master))
        new_firsts.append(moment)
        new_seconds.append(square)
    return (
        (loss_sum, count, grad_norm) + tuple(new_masters) + tuple(new_firsts) + tuple(new_seconds)
    )


def solution(mesh):
    in_specs = (
        P("item", "pair", None, None),
        P("item", "pair", None),
        P("item", "pair", None),
        P(None, "item", None),
        P(None, "item", None),
        P(None, "item", None),
        P(None, "item", None),
        P(None, "item", None),
        P(None, "item", None),
        P(None, "item", None),
        P(None, "item"),
        P(None, "item", None),
        P(None, "item", None),
        P(None, "item", None),
        P(None, "item", None),
        P(None, "item", None),
        P(None, "item", None),
        P(None, "item", None),
        P(None, "item"),
        P(None, "item", None),
        P(None, "item", None),
        P(None, "item", None),
        P(None, "item", None),
        P(None, "item", None),
        P(None, "item", None),
        P(None, "item", None),
        P(None, "item"),
    )
    out_specs = (
        P(),
        P(),
        P(),
        P(None, "item", None),
        P(None, "item", None),
        P(None, "item", None),
        P(None, "item", None),
        P(None, "item", None),
        P(None, "item", None),
        P(None, "item", None),
        P(None, "item"),
        P(None, "item", None),
        P(None, "item", None),
        P(None, "item", None),
        P(None, "item", None),
        P(None, "item", None),
        P(None, "item", None),
        P(None, "item", None),
        P(None, "item"),
        P(None, "item", None),
        P(None, "item", None),
        P(None, "item", None),
        P(None, "item", None),
        P(None, "item", None),
        P(None, "item", None),
        P(None, "item", None),
        P(None, "item"),
    )
    return jax.shard_map(
        on_device, mesh=mesh, in_specs=in_specs, out_specs=out_specs, check_vma=False
    )
```

```python
import functools

import jax
import jax.numpy as jnp
from jax import lax
from jax.experimental import pallas as pl
from jax.experimental.pallas import tpu as pltpu
from jax.sharding import PartitionSpec as P

STEP = 10

norm_epsilon = 1e-05
clip_limit = 0.001
learn_rate = 0.1
vector_rate = 0.8
beta_first = 0.9
beta_second = 0.999
adam_epsilon = 1e-08
weight_decay = 0.01

BF = jnp.bfloat16
F32 = jnp.float32
LOG2E = 1.4426950408889634
EPS = norm_epsilon


def cost(flops, moved, exps=0):
    return pl.CostEstimate(flops=int(flops), bytes_accessed=int(moved), transcendentals=int(exps))


def nn(a, b):
    return lax.dot_general(a, b, (((1,), (0,)), ((), ())), preferred_element_type=F32)

def nt(a, b):
    return lax.dot_general(a, b, (((1,), (1,)), ((), ())), preferred_element_type=F32)

def sigm(v):
    return 0.5 * jnp.tanh(0.5 * v) + 0.5

def norm(v):
    mean = jnp.mean(v, axis=-1, keepdims=True)
    cen = v - mean
    scale = lax.rsqrt(jnp.mean(cen * cen, axis=-1, keepdims=True) + EPS)
    return cen * scale, scale

def norm_back(up, gain, n, scale):
    inner = up * gain
    return scale * (inner - jnp.mean(inner, axis=-1, keepdims=True) - n * jnp.mean(inner * n, axis=-1, keepdims=True))

def chunks(total, width):
    return [(s, min(width, total - s)) for s in range(0, total, width)]

def column_kernel(heads, after_ref, tgt_ref, msk_ref, bias_ref, w_ref, wt_ref, wo_ref, we_ref, vec_ref, z_ref,
                gx_ref, gmid_ref, gb_ref, gkvw_ref, gqgw_ref, gow_ref, gew_ref, svec_ref, small_ref,
                bias2, e_s, gs_s, acc, qbd, gobd, vaug, qn, gon, ores, cu, hv):
    step = pl.program_id(0)
    last = pl.num_programs(0) - 1
    cb, n, c = after_ref.shape
    dh = c // heads
    wide = heads * n
    scale = dh ** -0.5
    every = range(cb)
    pairs = [(b, h) for b in every for h in range(heads)]
    lanes = lambda b, h: slice(b * wide + h * n, b * wide + (h + 1) * n)
    rows = lambda b: slice(b * n, (b + 1) * n)
    chans = lambda h: slice(h * dh, (h + 1) * dh)

    @pl.when(step == 0)
    def _():
        for h in range(heads):
            bias2[:, h * n:(h + 1) * n] = bias_ref[:, h * n:(h + 1) * n].astype(F32).T * LOG2E
        acc[...] = jnp.zeros_like(acc)
        qbd[...] = jnp.zeros_like(qbd)
        gobd[...] = jnp.zeros_like(gobd)
        first = lax.broadcasted_iota(jnp.int32, (cb * n, c), 1)
        vaug[:, c:] = jnp.where(first < 3, 1.0, 0.0).astype(BF)
        for ref in (gkvw_ref, gqgw_ref, gow_ref, gew_ref, svec_ref, small_ref):
            ref[...] = jnp.zeros_like(ref)

    lane = lax.broadcasted_iota(jnp.int32, (n, c), 1)
    g3 = vec_ref[2:3, :]
    g4 = vec_ref[3:4, :]
    wr = vec_ref[4:5, :]
    after = after_ref[...].reshape(cb * n, c)
    n3, _ = norm(after)
    x = (n3 * g3).astype(BF)
    nat = nn(x, w_ref[:, :3 * c])
    k_nat = nat[:, c:2 * c].astype(BF)
    vaug[:, :c] = nat[:, 2 * c:].astype(BF)
    q_nat = (nat[:, :c] * (scale * LOG2E)).astype(BF)
    tr = nt(wt_ref[...], x)
    q_t = (tr[:c] * (scale * LOG2E)).astype(BF)
    k_t = tr[c:2 * c].astype(BF)
    v_t = jnp.concatenate([tr[2 * c:3 * c], jnp.ones((16, cb * n), F32)], axis=0).astype(BF)
    gate_t = sigm(tr[3 * c:])
    for b, h in pairs:
        qbd[chans(h), lanes(b, h)] = q_t[chans(h), rows(b)]
        qn[lanes(b, h), :] = jnp.where((lane >= h * dh) & (lane < (h + 1) * dh), q_nat[rows(b)], jnp.zeros((n, c), BF))

    for s0, w0 in chunks(wide, wide):
        for b in every:
            sl = slice(b * wide + s0, b * wide + s0 + w0)
            sc = nn(k_nat[rows(b)], qbd[:, sl]) + bias2[:, s0:s0 + w0]
            top = jnp.max(sc, axis=0, keepdims=True)
            ex = jnp.exp2(sc - top).astype(BF)
            e_s[:, sl] = ex
            ores[:, sl] = nn(v_t[:, rows(b)], ex)
    r_of = {p: 1.0 / ores[c:c + 1, lanes(*p)] for p in pairs}
    o_of = {p: ores[chans(p[1]), lanes(*p)] * r_of[p] for p in pairs}
    o_t = jnp.concatenate([jnp.concatenate([o_of[b, h] for h in range(heads)], axis=0) for b in every], axis=1)
    y_t = (gate_t * o_t).astype(BF)
    out = nn(y_t.astype(F32).T.astype(BF), wo_ref[...]).astype(BF)
    mid = after + out.astype(F32)

    n4, sc4 = norm(mid)
    t = (n4 * g4).astype(BF)
    f = we_ref.shape[1] // 2
    racc = mid * wr
    for q in range(f // 128):
        u = nn(t, we_ref[:, q * 256:(q + 1) * 256])
        a, b = u[:, :128], u[:, 128:]
        zc = z_ref[:, q * 128:(q + 1) * 128]
        sig = sigm(a)
        silu = a * sig
        h_low = (silu * b).astype(BF)
        hv[:, q * 128:(q + 1) * 128] = h_low
        racc += h_low.astype(F32) * zc
        cu[:, q * 256:q * 256 + 128] = (zc * b * (sig + silu - silu * sig)).astype(BF)
        cu[:, q * 256 + 128:(q + 1) * 256] = (zc * silu).astype(BF)
    readout = jnp.sum(racc, axis=-1, keepdims=True)
    spot = lax.broadcasted_iota(jnp.int32, tgt_ref.shape, 1)
    pick = lambda ref: jnp.concatenate(
        [jnp.sum(jnp.where(spot == step * cb + b, ref[...], 0.0), axis=1, keepdims=True) for b in every], axis=0)
    err = readout - pick(tgt_ref)
    wer = pick(msk_ref) * err
    gr = 2.0 * wer
    small_ref[0:1, :] += jnp.sum(gr * mid, axis=0, keepdims=True)
    first = lax.broadcasted_iota(jnp.int32, (cb * n, c), 1)
    small_ref[2:3, :] += jnp.sum(jnp.where(first == 0, wer * err, 0.0), axis=0, keepdims=True)
    svec_ref[...] += jnp.sum(gr * hv[...].astype(F32), axis=0, keepdims=True)
    gew_ref[...] += nn((gr * t.astype(F32)).T.astype(BF), cu[...])
    gt = gr * nt(cu[...], we_ref[...])
    small_ref[1:2, :] += jnp.sum(gt * n4, axis=0, keepdims=True)
    gmid = gr * wr + norm_back(gt, g4, n4, sc4)
    gmid_ref[...] = gmid.reshape(gmid_ref.shape)

    gout = gmid.astype(BF)
    gow_ref[...] += nn(y_t, gout)
    gy_t = nt(wo_ref[...], gout)
    ggl_t = gy_t * o_t * gate_t * (1.0 - gate_t)
    go_t = (gy_t * gate_t).astype(BF).astype(F32)
    row = lax.broadcasted_iota(jnp.int32, (16, n), 0)
    gos = {}
    for b, h in pairs:
        part = (go_t[chans(h), rows(b)] * r_of[b, h]).astype(BF)
        gobd[chans(h), lanes(b, h)] = part
        part = part.astype(F32)
        gos[b, h] = part
        d = -jnp.sum(part * o_of[b, h], axis=0, keepdims=True)
        hi = d.astype(BF).astype(F32)
        mi = (d - hi).astype(BF).astype(F32)
        lo = d - hi - mi
        gobd[c:, lanes(b, h)] = jnp.where(row == 0, hi, jnp.where(row == 1, mi, jnp.where(row == 2, lo, 0.0))).astype(BF)
    go_n = jnp.concatenate([jnp.concatenate([gos[b, h] for h in range(heads)], axis=0) for b in every], axis=1).T.astype(BF)
    for b, h in pairs:
        gon[lanes(b, h), :] = jnp.where((lane >= h * dh) & (lane < (h + 1) * dh), go_n[rows(b)], jnp.zeros((n, c), BF))

    for s0, w0 in chunks(wide, wide):
        total = acc[:, s0:s0 + w0]
        for b in every:
            sl = slice(b * wide + s0, b * wide + s0 + w0)
            g = e_s[:, sl].astype(F32) * nn(vaug[rows(b), :c + 16], gobd[:, sl])
            total += g
            gl = g.astype(BF)
            gs_s[:, sl] = gl
            ores[:c, sl] = nn(k_t[:, rows(b)], gl)
        acc[:, s0:s0 + w0] = total
    gq_t = jnp.concatenate(
        [jnp.concatenate([ores[chans(h), lanes(b, h)] for h in range(heads)], axis=0) for b in every], axis=1) * scale
    gqg_t = jnp.concatenate([gq_t, ggl_t], axis=0).astype(BF)
    gk = [nn(gs_s[:, b * wide:(b + 1) * wide], qn[b * wide:(b + 1) * wide, :]) * (1.0 / LOG2E) for b in every]
    gv = [nn(e_s[:, b * wide:(b + 1) * wide], gon[b * wide:(b + 1) * wide, :]) for b in every]
    gkv = jnp.concatenate([jnp.concatenate([gk[b], gv[b]], axis=1) for b in every], axis=0).astype(BF)
    gqgw_ref[...] += nn(gqg_t, x)
    gkvw_ref[...] += nn(x.astype(F32).T.astype(BF), gkv)
    w_qg = jnp.concatenate([w_ref[:, :c], w_ref[:, 3 * c:]], axis=1)
    gx_ref[...] = (nt(gkv, w_ref[:, c:3 * c]) + nn(w_qg, gqg_t).T).reshape(gx_ref.shape)

    @pl.when(step == last)
    def _():
        for h in range(heads):
            gb_ref[:, h * n:(h + 1) * n] = acc[:, h * n:(h + 1) * n].T.astype(gb_ref.dtype)


def column_pass(after, tgt, msk, bias, w, wt, wo, we, vec, z):
    cols, n, c = after.shape
    heads = bias.shape[1] // n
    f = we.shape[1] // 2
    wide = heads * n
    cb = batch(cols, 3)
    full = lambda shape: pl.BlockSpec(shape, lambda j: (0,) * len(shape))
    col = pl.BlockSpec((cb, n, c), lambda j: (j, 0, 0))
    outs = [
        jax.ShapeDtypeStruct((cols, n, c), F32),
        jax.ShapeDtypeStruct((cols, n, c), F32),
        jax.ShapeDtypeStruct((n, wide), BF),
        jax.ShapeDtypeStruct((c, 2 * c), F32),
        jax.ShapeDtypeStruct((2 * c, c), F32),
        jax.ShapeDtypeStruct((c, c), F32),
        jax.ShapeDtypeStruct((c, 2 * f), F32),
        jax.ShapeDtypeStruct((1, f), F32),
        jax.ShapeDtypeStruct((8, c), F32),
    ]
    return pl.pallas_call(
        functools.partial(column_kernel, heads),
        grid=(cols // cb,),
        in_specs=[col] + [full(v.shape) for v in (tgt, msk, bias, w, wt, wo, we, vec, z)],
        out_specs=[col, col] + [full(o.shape) for o in outs[2:]],
        out_shape=outs,
        scratch_shapes=[
            pltpu.VMEM((n, wide), F32),
            pltpu.VMEM((n, cb * wide), BF),
            pltpu.VMEM((n, cb * wide), BF),
            pltpu.VMEM((n, wide), F32),
            pltpu.VMEM((c, cb * wide), BF),
            pltpu.VMEM((c + 16, cb * wide), BF),
            pltpu.VMEM((cb * n, 2 * c), BF),
            pltpu.VMEM((cb * wide, c), BF),
            pltpu.VMEM((cb * wide, c), BF),
            pltpu.VMEM((c + 16, cb * wide), F32),
            pltpu.VMEM((cb * n, 2 * f), BF),
            pltpu.VMEM((cb * n, f), BF),
        ],
        compiler_params=pltpu.CompilerParams(vmem_limit_bytes=56 << 20),
        cost_estimate=cost(12 * cols * heads * n * n * 128, 16 * cols * n * c, cols * heads * n * n),
        name="columns",
    )(after, tgt, msk, bias, w, wt, wo, we, vec, z)


GROUP = 16
AFTER_BATCH = 4
BACK_BATCH = 4


def spread(scr, start, count, stride, value):
    for t in range(scr.shape[0]):
        scr[t, pl.ds(start, count, stride=stride), :] = value[:, t * 128 : (t + 1) * 128]


def joined(scr, rows=slice(None)):
    return jnp.concatenate([scr[t, rows] for t in range(scr.shape[0])], axis=1)


def padded(count):
    return -(-count // 128) * 128


def operand_kernel(cols, off_ref, x_ref, wl_ref, wr_ref, *refs):
    left_ref, right_ref, n_ref, nc_ref, xc_ref, lscr, rscr, nscr, xscr, cscr = refs[-10:]
    rows, n, c = x_ref.shape
    half = wl_ref.shape[0] // 2
    wide = nc_ref.shape[1]
    own = off_ref[0]
    other = off_ref[1]
    for k in range(rows):
        x = x_ref[k].astype(F32)
        nrm, _ = norm(x)
        low = nrm.astype(BF)
        n_ref[k] = low
        nscr[k] = nrm
        xscr[k] = x
        p = nt(wl_ref[...], low)
        spread(lscr, k, half, rows, p[:half] * sigm(p[half:]))
    for k in range(rows):
        near = [nscr[k, pl.ds(own, cols), :], nscr[k, pl.ds(other, cols), :]]
        if wide > 2 * cols:
            near.append(jnp.zeros((wide - 2 * cols, c), F32))
        near = jnp.concatenate(near, axis=0).astype(BF)
        nc_ref[k] = near
        p = nt(wr_ref[...], near)
        spread(rscr, k, half, rows, p[:half] * sigm(p[half:]))
        cscr[pl.ds(k, cols, stride=rows), :] = xscr[k, pl.ds(own, cols), :]
    left_ref[...] = joined(lscr).astype(BF).reshape(left_ref.shape)
    right_ref[...] = joined(rscr).astype(BF).reshape(right_ref.shape)
    xc_ref[...] = cscr[...].astype(BF).reshape(xc_ref.shape)


def operands(offs, x, wl, wr, cols, place, bufs):
    n, c = x.shape[1], x.shape[2]
    half = wl.shape[0] // 2
    wide = padded(2 * cols)
    g = GROUP
    shapes = [
        ((half, n, n), (half, g, n), lambda b: (0, place(b), 0)),
        ((half, n, wide), (half, g, wide), lambda b: (0, place(b), 0)),
        ((n, n, c), (g, n, c), lambda b: (place(b), 0, 0)),
        ((n, wide, c), (g, wide, c), lambda b: (place(b), 0, 0)),
        ((cols, n, c), (cols, g, c), lambda b: (0, place(b), 0)),
    ]
    full = lambda v: pl.BlockSpec(v.shape, lambda b: (0,) * v.ndim)
    ins = [offs, x, wl, wr]
    specs = [
        pl.BlockSpec(memory_space=pltpu.SMEM),
        pl.BlockSpec((g, n, c), lambda b: (b, 0, 0)),
        full(wl),
        full(wr),
    ]
    alias = {}
    if bufs is not None:
        alias = {4 + i: i for i in range(5)}
        ins += list(bufs)
        specs += [pl.BlockSpec(memory_space=pl.ANY)] * 5
    return pl.pallas_call(
        functools.partial(operand_kernel, cols),
        grid=(x.shape[0] // g,),
        in_specs=specs,
        out_specs=[pl.BlockSpec(b, m) for _, b, m in shapes],
        out_shape=[jax.ShapeDtypeStruct(s, BF) for s, _, _ in shapes],
        scratch_shapes=[
            pltpu.VMEM((n // 128, half * g, 128), F32),
            pltpu.VMEM((wide // 128, half * g, 128), F32),
            pltpu.VMEM((g, n, c), F32),
            pltpu.VMEM((g, n, c), F32),
            pltpu.VMEM((cols * g, c), F32),
        ],
        input_output_aliases=alias,
        compiler_params=pltpu.CompilerParams(vmem_limit_bytes=56 << 20),
        cost_estimate=cost(4 * x.shape[0] * n * c * 2 * half, 6 * x.shape[0] * n * c, x.shape[0] * n * half),
        name="operands",
    )(*ins)


def product_kernel(left_ref, right_ref, mine_ref, theirs_ref, scr):
    g = left_ref.shape[0]
    cols = mine_ref.shape[0]
    for e in range(g):
        part = lax.dot_general(right_ref[e], left_ref[e], (((0,), (0,)), ((), ())), preferred_element_type=F32)
        spread(scr, e, 2 * cols, g, part[: 2 * cols])
    mine_ref[...] = joined(scr, slice(0, cols * g)).astype(mine_ref.dtype).reshape(mine_ref.shape)
    theirs_ref[...] = joined(scr, slice(cols * g, None)).astype(theirs_ref.dtype).reshape(theirs_ref.shape)


def products(left, right, cols):
    half, n, _ = left.shape
    wide = right.shape[2]
    g = GROUP
    out = jax.ShapeDtypeStruct((cols, half, n), BF)
    return pl.pallas_call(
        product_kernel,
        grid=(half // g,),
        in_specs=[pl.BlockSpec((g, n, n), lambda b: (b, 0, 0)), pl.BlockSpec((g, n, wide), lambda b: (b, 0, 0))],
        out_specs=[pl.BlockSpec((cols, g, n), lambda b: (0, b, 0))] * 2,
        out_shape=[out, out],
        scratch_shapes=[pltpu.VMEM((n // 128, 2 * cols * g, 128), F32)],
        compiler_params=pltpu.CompilerParams(vmem_limit_bytes=56 << 20),
        cost_estimate=cost(2 * half * n * n * wide, 4 * half * n * n),
        name="products",
    )(left, right)


def batch(count, most):
    return max(b for b in range(1, most + 1) if count % b == 0)


def product_rows(mine_ref, theirs_ref):
    return jnp.concatenate(
        [
            jnp.concatenate([mine_ref[b].astype(F32), theirs_ref[b].astype(F32)], axis=0).T
            for b in range(mine_ref.shape[0])
        ],
        axis=0,
    )


def after_kernel(heads, xc_ref, mine_ref, theirs_ref, w4_ref, wout_ref, wb_ref, vec_ref, after_ref, bias_ref):
    cb, n, c = xc_ref.shape
    x = xc_ref[...].astype(F32).reshape(cb * n, c)
    n0, _ = norm(x)
    gate = sigm(nn(n0.astype(BF), w4_ref[...]))
    nc, _ = norm(product_rows(mine_ref, theirs_ref))
    lin = nn((nc * vec_ref[1:2, :]).astype(BF), wout_ref[...])
    after = x + (gate * lin).astype(BF).astype(F32)
    after_ref[...] = after.reshape(after_ref.shape)
    n3, _ = norm(after)
    bias = nt(wb_ref[...], (n3 * vec_ref[2:3, :]).astype(BF))
    for b in range(cb):
        for h in range(heads):
            bias_ref[b, :, h * n:(h + 1) * n] = bias[h:h + 1, b * n:(b + 1) * n]


def afters(xc, mine, theirs, w4, wout, wb, vec, heads):
    cols, n, c = xc.shape
    half = mine.shape[1]
    cb = batch(cols, AFTER_BATCH)
    full = lambda v: pl.BlockSpec(v.shape, lambda b: (0,) * v.ndim)
    col = lambda a, b: pl.BlockSpec((cb, a, b), lambda j: (j, 0, 0))
    return pl.pallas_call(
        functools.partial(after_kernel, heads),
        grid=(cols // cb,),
        in_specs=[col(n, c), col(half, n), col(half, n), full(w4), full(wout), full(wb), full(vec)],
        out_specs=[col(n, c), col(1, heads * n)],
        out_shape=[jax.ShapeDtypeStruct((cols, n, c), F32), jax.ShapeDtypeStruct((cols, 1, heads * n), F32)],
        compiler_params=pltpu.CompilerParams(vmem_limit_bytes=56 << 20),
        cost_estimate=cost(8 * cols * n * c * c, 10 * cols * n * c, cols * n * c),
        name="afters",
    )(xc, mine, theirs, w4, wout, wb, vec)


def back_kernel(after_ref, gx_ref, gmid_ref, gb_ref, xc_ref, mine_ref, theirs_ref, w4_ref, wout_ref, wb_ref, vec_ref,
                gmine_ref, gtheirs_ref, gwb_ref, gwout_ref, gw4_ref, small_ref):
    @pl.when(pl.program_id(0) == 0)
    def _():
        for ref in (gwb_ref, gwout_ref, gw4_ref, small_ref):
            ref[...] = jnp.zeros_like(ref)

    cb, n, c = xc_ref.shape
    half = mine_ref.shape[1]
    heads = gb_ref.shape[2]
    flat = lambda ref: ref[...].reshape(cb * n, c)
    g1 = vec_ref[1:2, :]
    g2 = vec_ref[2:3, :]
    n3, s3 = norm(flat(after_ref))
    x3 = (n3 * g2).astype(BF)
    parts = []
    for b in range(cb):
        gb = gb_ref[0, b].astype(F32)
        for d in range(1, gb_ref.shape[0]):
            gb = gb + gb_ref[d, b].astype(F32)
        parts.append(jnp.concatenate([gb, jnp.zeros((wb_ref.shape[0] - heads, n), F32)], axis=0))
    gb = jnp.concatenate(parts, axis=1)
    gwb_ref[...] += nn(gb.astype(BF), x3)
    gx = (flat(gx_ref) + nn(gb.T.astype(BF), wb_ref[...])).astype(BF).astype(F32)
    small_ref[0:1, :] += jnp.sum(gx * n3, axis=0, keepdims=True)
    gafter = (flat(gmid_ref) + norm_back(gx, g2, n3, s3)).astype(BF).astype(F32)

    n0, _ = norm(flat(xc_ref).astype(F32))
    n0 = n0.astype(BF)
    gate = sigm(nn(n0, w4_ref[...]))
    nc, sc = norm(product_rows(mine_ref, theirs_ref))
    centre = (nc * g1).astype(BF)
    lin = nn(centre, wout_ref[...])
    glin = (gafter * gate).astype(BF)
    gp4 = (gafter * lin * gate * (1.0 - gate)).astype(BF)
    gwout_ref[...] += nn(centre.astype(F32).T.astype(BF), glin)
    gw4_ref[...] += nn(n0.astype(F32).T.astype(BF), gp4)
    gc = nt(glin, wout_ref[...]).astype(BF).astype(F32)
    small_ref[1:2, :] += jnp.sum(gc * nc, axis=0, keepdims=True)
    gprod = norm_back(gc, g1, nc, sc)
    for b in range(cb):
        part = gprod[b * n:(b + 1) * n].T.astype(BF)
        gmine_ref[b] = part[:half]
        gtheirs_ref[b] = part[half:]


def back_pass(after, gx, gmid, gb, xc, mine, theirs, w4, wout, wb, vec):
    cols, n, c = xc.shape
    half = mine.shape[1]
    heads = gb.shape[2]
    cb = batch(cols, BACK_BATCH)
    full = lambda shape: pl.BlockSpec(shape, lambda b: (0,) * len(shape))
    col = lambda a, b: pl.BlockSpec((cb, a, b), lambda j: (j, 0, 0))
    accs = [wb.shape, (c, c), (c, c), (8, c)]
    return pl.pallas_call(
        back_kernel,
        grid=(cols // cb,),
        in_specs=[col(n, c)] * 3
        + [pl.BlockSpec((gb.shape[0], cb, heads, n), lambda j: (0, j, 0, 0)), col(n, c), col(half, n), col(half, n)]
        + [full(v.shape) for v in (w4, wout, wb, vec)],
        out_specs=[col(half, n)] * 2 + [full(s) for s in accs],
        out_shape=[jax.ShapeDtypeStruct((cols, half, n), BF)] * 2 + [jax.ShapeDtypeStruct(s, F32) for s in accs],
        compiler_params=pltpu.CompilerParams(vmem_limit_bytes=56 << 20),
        cost_estimate=cost(16 * cols * n * c * c, 24 * cols * n * c, cols * n * c),
        name="back",
    )(after, gx, gmid, gb, xc, mine, theirs, w4, wout, wb, vec)


def operand_grads_kernel(left_ref, right_ref, gm_ref, gt_ref, gl_ref, gr_ref, scr, lscr, rscr):
    g, n, _ = left_ref.shape
    cols = gm_ref.shape[0]
    wide = right_ref.shape[2]
    gm = gm_ref[...].astype(F32).reshape(cols * g, n)
    gt = gt_ref[...].astype(F32).reshape(cols * g, n)
    for t in range(n // 128):
        scr[t, : cols * g] = gm[:, t * 128 : (t + 1) * 128]
        scr[t, cols * g :] = gt[:, t * 128 : (t + 1) * 128]
    for e in range(g):
        gp = jnp.concatenate([scr[t, pl.ds(e, 2 * cols, stride=g), :] for t in range(n // 128)], axis=1)
        if wide > 2 * cols:
            gp = jnp.concatenate([gp, jnp.zeros((wide - 2 * cols, n), F32)], axis=0)
        gp = gp.astype(BF)
        spread(rscr, e, n, g, nt(left_ref[e], gp))
        spread(lscr, e, n, g, nn(right_ref[e], gp))
    gl_ref[...] = joined(lscr).astype(BF).reshape(gl_ref.shape)
    gr_ref[...] = joined(rscr).astype(BF).reshape(gr_ref.shape)


def operand_grads(left, right, gmine, gtheirs):
    half, n, _ = left.shape
    wide = right.shape[2]
    cols = gmine.shape[0]
    g = GROUP
    return pl.pallas_call(
        operand_grads_kernel,
        grid=(half // g,),
        in_specs=[pl.BlockSpec((g, n, n), lambda b: (b, 0, 0)), pl.BlockSpec((g, n, wide), lambda b: (b, 0, 0))]
        + [pl.BlockSpec((cols, g, n), lambda b: (0, b, 0))] * 2,
        out_specs=[pl.BlockSpec((n, g, n), lambda b: (0, b, 0)), pl.BlockSpec((n, g, wide), lambda b: (0, b, 0))],
        out_shape=[jax.ShapeDtypeStruct((n, half, n), BF), jax.ShapeDtypeStruct((n, half, wide), BF)],
        scratch_shapes=[
            pltpu.VMEM((n // 128, 2 * cols * g, 128), F32),
            pltpu.VMEM((n // 128, n * g, 128), F32),
            pltpu.VMEM((wide // 128, n * g, 128), F32),
        ],
        compiler_params=pltpu.CompilerParams(vmem_limit_bytes=60 << 20),
        cost_estimate=cost(4 * half * n * n * wide, 8 * half * n * n),
        name="operand_grads",
    )(left, right, gmine, gtheirs)


def tri_grads_kernel(n_ref, nc_ref, gl_ref, gr_ref, wl_ref, wr_ref, al_ref, ar_ref, lg, rg):
    @pl.when(pl.program_id(0) == 0)
    def _():
        al_ref[...] = jnp.zeros_like(al_ref)
        ar_ref[...] = jnp.zeros_like(ar_ref)
    rows, n, c = n_ref.shape
    wide = nc_ref.shape[1]
    half = gl_ref.shape[1]
    def one(low, grad, w):
        p = nt(w, low)
        s = sigm(p[half:])
        first = grad.astype(F32) * s
        return first.astype(BF), (first * p[:half] * (1.0 - s)).astype(BF)
    for k in range(rows):
        a, b = one(n_ref[k], gl_ref[k], wl_ref[...])
        lg[:half, k*n:(k+1)*n] = a
        lg[half:, k*n:(k+1)*n] = b
        a, b = one(nc_ref[k], gr_ref[k], wr_ref[...])
        rg[:half, k*wide:(k+1)*wide] = a
        rg[half:, k*wide:(k+1)*wide] = b
    al_ref[...] += nn(lg[...], n_ref[...].reshape(rows*n, c))
    ar_ref[...] += nn(rg[...], nc_ref[...].reshape(rows*wide, c))


def tri_grads(nrm, near, gl, gr, wl, wr):
    n, _, c = nrm.shape
    half = gl.shape[1]
    wide = near.shape[1]
    rows = 24
    full = lambda v: pl.BlockSpec(v.shape, lambda b: (0,) * v.ndim)
    row = lambda a, b: pl.BlockSpec((rows, a, b), lambda k: (k, 0, 0))
    out = jax.ShapeDtypeStruct((2 * half, c), F32)
    return pl.pallas_call(
        tri_grads_kernel,
        grid=(n // rows,),
        in_specs=[row(n, c), row(wide, c), row(half, n), row(half, wide), full(wl), full(wr)],
        out_specs=[pl.BlockSpec(out.shape, lambda k: (0, 0))] * 2,
        out_shape=[out] * 2,
        scratch_shapes=[pltpu.VMEM((2*half, rows*n), BF), pltpu.VMEM((2*half, rows*wide), BF)],
        compiler_params=pltpu.CompilerParams(vmem_limit_bytes=56 << 20),
        cost_estimate=cost(8 * n * n * c * c, 8 * n * n * c, n * n * half),
        name="tri_grads",
    )(nrm, near, gl, gr, wl, wr)


def gather_weights(tri, tri_out, attn, bias, outp, expand, shrink, vectors):
    rows = tri.shape[1]
    pieces = [tri[0], tri_out[0], attn[0], outp[0], expand[0], shrink[0].reshape(rows, -1), bias[0], vectors.T]
    widths = [p.shape[1] for p in pieces]
    packed = lax.all_gather(jnp.concatenate([p.astype(BF) for p in pieces], axis=1), "item", axis=0, tiled=True)
    got, at = [], 0
    for w in widths:
        got.append(packed[:, at : at + w])
        at += w
    tri, tri_out, attn, outp, expand, shr, bias, vec = got
    return tri, tri_out, attn, bias, outp, expand, shr.reshape(-1, shrink.shape[2]), vec.T


def gather_rows(pair_act, pieces):
    rows = pair_act.shape[1] // pieces
    return [
        lax.all_gather(pair_act[0, m * rows : (m + 1) * rows], "pair", axis=0, tiled=True)
        for m in range(pieces)
    ]


def swap_cores(value):
    size = lax.axis_size("pair")
    return lax.ppermute(value, "pair", [(d, d ^ 1) for d in range(size)])


def exchange(value, axis, bit):
    size = lax.axis_size(axis)
    return lax.ppermute(value, axis, [(d, d ^ bit) for d in range(size)])


def sum_axis(value, axis):
    bit = 1
    while bit < lax.axis_size(axis):
        value = value + exchange(value, axis, bit)
        bit *= 2
    return value


def sum_all(value):
    return sum_axis(sum_axis(value, "item"), "pair")


def sum_shards(parts):
    size = lax.axis_size("item")
    here = lax.axis_index("item")
    bit = size // 2
    while bit:
        upper = (here // bit) % 2
        kept, sent = [], []
        for part in parts:
            rows = part.shape[0] // 2
            kept.append(lax.dynamic_slice_in_dim(part, upper * rows, rows, 0))
            sent.append(lax.dynamic_slice_in_dim(part, (1 - upper) * rows, rows, 0))
        parts = [k + exchange(s.astype(BF), "item", bit).astype(F32) for k, s in zip(kept, sent)]
        bit //= 2
    return [sum_axis(part, "pair") for part in parts]


def on_device(
    pair_act,
    targets,
    pair_mask,
    tri_proj,
    tri_out,
    attention_proj,
    bias_proj,
    output_proj,
    expand_proj,
    shrink_proj,
    vectors,
    first_tri,
    first_tri_out,
    first_attention,
    first_bias,
    first_output,
    first_expand,
    first_shrink,
    first_vectors,
    second_tri,
    second_tri_out,
    second_attention,
    second_bias,
    second_output,
    second_expand,
    second_shrink,
    second_vectors,
):
    layers = attention_proj.shape[0]
    assert layers == 1
    cols, tokens, width = pair_act.shape[1:]
    half = width // 2
    heads = bias_proj.shape[2]
    here = lax.axis_index("pair")
    core = here % 2
    pieces = 3 if cols % (3 * GROUP) == 0 else 1
    gathered = gather_rows(pair_act, pieces)
    weight = gather_weights(
        tri_proj, tri_out, attention_proj, bias_proj, output_proj, expand_proj, shrink_proj, vectors
    )
    tri_w, tri_out_w, project_w, pairbias_w, output_w, expand_w, shrink_w, vector_low = weight
    vec = vector_low.astype(F32)
    weighting_rows = pair_mask.astype(F32)
    both = lax.all_to_all(
        jnp.concatenate([targets, weighting_rows]), "pair", split_axis=2, concat_axis=1, tiled=True
    )

    scaled = (tri_w.astype(F32) * vec[0][:, None]).astype(BF).T
    halves = [
        lax.dynamic_slice_in_dim(scaled, width * s + half * core, half, 0) for s in range(4)
    ]
    w_left = jnp.concatenate(halves[:2])
    w_right = jnp.concatenate(halves[2:])
    w_gate = scaled[4 * width :].T
    wout = jnp.roll(tri_out_w, -half * core, axis=0)
    gain_c = jnp.roll(vec[1], -half * core)
    vec8 = jnp.concatenate([vec[:1], gain_c[None], vec[2:], jnp.zeros((3, width), F32)])
    wb = jnp.concatenate([pairbias_w.T, jnp.zeros((16 - heads, width), BF)])

    offs = jnp.stack([here * cols, (here + 1 - 2 * core) * cols]).astype(jnp.int32)
    span = cols // pieces // GROUP
    bufs = None
    for m in range(pieces):
        if pieces == 1:
            place = lambda b: b
        else:
            place = lambda b, m=m: (b // span) * (span * pieces) + m * span + b % span
        bufs = operands(offs, gathered[m], w_left, w_right, cols, place, bufs)
    left, right, nrm, near, xc = bufs
    mine, send = products(left, right, cols)
    theirs = swap_cores(send)
    after_c, bias_part = afters(xc, mine, theirs, w_gate, wout, wb, vec8, heads)
    bias_full = lax.all_gather(bias_part[:, 0].astype(BF), "pair", axis=0, tiled=True)
    hidden = expand_w.shape[1] // 2
    expand_mix = (
        expand_w.reshape(width, 2, hidden // 128, 128).swapaxes(1, 2).reshape(width, 2 * hidden)
    )
    z = jnp.sum(shrink_w.astype(F32) * vec[4], axis=1)[None]
    gx, gmid, gb, gkv_w, gqg_w, gow, gew, svec, small = column_pass(
        after_c, both[0], both[1], bias_full, project_w, project_w.T, output_w, expand_mix, vec8, z
    )
    bias_cols = lax.all_to_all(gb, "pair", split_axis=0, concat_axis=0, tiled=True)
    scalars = sum_all(jnp.stack([jnp.sum(small[2]), jnp.sum(weighting_rows)]))
    gmine, gsend, gwb, gwout, gw4, small2 = back_pass(
        after_c, gx, gmid, bias_cols.reshape(-1, cols, heads, tokens), xc, mine, theirs,
        w_gate, wout, wb, vec8,
    )
    gtheirs = swap_cores(gsend)
    gl, gr = operand_grads(left, right, gmine, gtheirs)
    al, ar = tri_grads(nrm, near, gl, gr, w_left, w_right)

    def halfway(part):
        zero = jnp.zeros_like(part)
        return [jnp.where(core == 0, part, zero), jnp.where(core == 1, part, zero)]

    a_tri = jnp.concatenate(
        halfway(al[:half]) + halfway(al[half:]) + halfway(ar[:half]) + halfway(ar[half:]) + [gw4.T]
    ).T
    g_read = small[0] + jnp.sum(svec[0][:, None] * shrink_w.astype(F32), axis=0)
    g_vec = jnp.stack(
        [
            jnp.sum(a_tri * tri_w.astype(F32), axis=1),
            jnp.roll(small2[1], half * core),
            small2[0],
            small[1],
            g_read,
        ]
    )
    (total,) = sum_shards(
        [
            jnp.concatenate(
                [
                    gqg_w[:width].T,
                    gkv_w,
                    gqg_w[width:].T,
                    gow,
                    gew,
                    a_tri * vec[0][:, None],
                    jnp.roll(gwout, half * core, axis=0),
                    svec.reshape(width, -1),
                    gwb[:heads].T,
                    g_vec.T,
                ],
                axis=1,
            )
        ]
    )
    loss_sum, count = scalars[0], scalars[1]
    widths = (4 * width, width, 2 * hidden, 5 * width, width, svec.shape[1] // width, heads)
    cuts = []
    for w in widths:
        cuts.append(total[:, :w])
        total = total[:, w:]
    shards = [
        cuts[3],
        cuts[4],
        cuts[0],
        cuts[6],
        cuts[1],
        cuts[2].reshape(-1, hidden // 128, 2, 128).swapaxes(1, 2).reshape(-1, 2 * hidden),
        cuts[5].reshape(-1, 1) * vec[4][None, :],
        total.T,
    ]
    shards = [s / count for s in shards]
    squares = sum_axis(sum(jnp.sum(s * s) for s in shards), "item")
    grad_norm = jnp.sqrt(squares)
    factor = jnp.minimum(1.0, clip_limit / (grad_norm + 1e-06))
    shards = [s[None] for s in shards[:7]] + shards[7:]
    masters = (
        tri_proj,
        tri_out,
        attention_proj,
        bias_proj,
        output_proj,
        expand_proj,
        shrink_proj,
        vectors,
    )
    firsts = (
        first_tri,
        first_tri_out,
        first_attention,
        first_bias,
        first_output,
        first_expand,
        first_shrink,
        first_vectors,
    )
    seconds = (
        second_tri,
        second_tri_out,
        second_attention,
        second_bias,
        second_output,
        second_expand,
        second_shrink,
        second_vectors,
    )
    rates = (learn_rate,) * 7 + (vector_rate,)
    new_masters, new_firsts, new_seconds = ([], [], [])
    for master, grad, first, second, rate in zip(masters, shards, firsts, seconds, rates):
        clipped = grad * factor
        moment = beta_first * first + (1 - beta_first) * clipped
        square = beta_second * second + (1 - beta_second) * clipped * clipped
        stride = (
            moment
            / (1 - beta_first**STEP)
            / (jnp.sqrt(square / (1 - beta_second**STEP)) + adam_epsilon)
        )
        new_masters.append(master - rate * (stride + weight_decay * master))
        new_firsts.append(moment)
        new_seconds.append(square)
    return (
        (loss_sum, count, grad_norm) + tuple(new_masters) + tuple(new_firsts) + tuple(new_seconds)
    )


def solution(mesh):
    in_specs = (
        P("item", "pair", None, None),
        P("item", "pair", None),
        P("item", "pair", None),
        P(None, "item", None),
        P(None, "item", None),
        P(None, "item", None),
        P(None, "item", None),
        P(None, "item", None),
        P(None, "item", None),
        P(None, "item", None),
        P(None, "item"),
        P(None, "item", None),
        P(None, "item", None),
        P(None, "item", None),
        P(None, "item", None),
        P(None, "item", None),
        P(None, "item", None),
        P(None, "item", None),
        P(None, "item"),
        P(None, "item", None),
        P(None, "item", None),
        P(None, "item", None),
        P(None, "item", None),
        P(None, "item", None),
        P(None, "item", None),
        P(None, "item", None),
        P(None, "item"),
    )
    out_specs = (
        P(),
        P(),
        P(),
        P(None, "item", None),
        P(None, "item", None),
        P(None, "item", None),
        P(None, "item", None),
        P(None, "item", None),
        P(None, "item", None),
        P(None, "item", None),
        P(None, "item"),
        P(None, "item", None),
        P(None, "item", None),
        P(None, "item", None),
        P(None, "item", None),
        P(None, "item", None),
        P(None, "item", None),
        P(None, "item", None),
        P(None, "item"),
        P(None, "item", None),
        P(None, "item", None),
        P(None, "item", None),
        P(None, "item", None),
        P(None, "item", None),
        P(None, "item", None),
        P(None, "item", None),
        P(None, "item"),
    )
    return jax.shard_map(
        on_device, mesh=mesh, in_specs=in_specs, out_specs=out_specs, check_vma=False
    )
```

```python
import functools

import jax
import jax.numpy as jnp
from jax import lax
from jax.experimental import pallas as pl
from jax.experimental.pallas import tpu as pltpu
from jax.sharding import PartitionSpec as P

STEP = 10

norm_epsilon = 1e-05
clip_limit = 0.001
learn_rate = 0.1
vector_rate = 0.8
beta_first = 0.9
beta_second = 0.999
adam_epsilon = 1e-08
weight_decay = 0.01

BF = jnp.bfloat16
F32 = jnp.float32
LOG2E = 1.4426950408889634
EPS = norm_epsilon


def cost(flops, moved, exps=0):
    return pl.CostEstimate(flops=int(flops), bytes_accessed=int(moved), transcendentals=int(exps))


def nn(a, b):
    return lax.dot_general(a, b, (((1,), (0,)), ((), ())), preferred_element_type=F32)

def nt(a, b):
    return lax.dot_general(a, b, (((1,), (1,)), ((), ())), preferred_element_type=F32)

def sigm(v):
    return 0.5 * jnp.tanh(0.5 * v) + 0.5

def norm(v):
    mean = jnp.mean(v, axis=-1, keepdims=True)
    cen = v - mean
    scale = lax.rsqrt(jnp.mean(cen * cen, axis=-1, keepdims=True) + EPS)
    return cen * scale, scale

def norm_back(up, gain, n, scale):
    inner = up * gain
    return scale * (inner - jnp.mean(inner, axis=-1, keepdims=True) - n * jnp.mean(inner * n, axis=-1, keepdims=True))

def chunks(total, width):
    return [(s, min(width, total - s)) for s in range(0, total, width)]

def column_kernel(heads, after_ref, tgt_ref, msk_ref, bias_ref, w_ref, wt_ref, wo_ref, we_ref, vec_ref, z_ref,
                gx_ref, gmid_ref, gb_ref, gkvw_ref, gqgw_ref, gow_ref, gew_ref, svec_ref, small_ref,
                bias2, e_s, gs_s, acc, qbd, gobd, vaug, qn, gon, ores, cu, hv):
    step = pl.program_id(0)
    last = pl.num_programs(0) - 1
    cb, n, c = after_ref.shape
    dh = c // heads
    wide = heads * n
    scale = dh ** -0.5
    every = range(cb)
    pairs = [(b, h) for b in every for h in range(heads)]
    lanes = lambda b, h: slice(b * wide + h * n, b * wide + (h + 1) * n)
    rows = lambda b: slice(b * n, (b + 1) * n)
    chans = lambda h: slice(h * dh, (h + 1) * dh)

    @pl.when(step == 0)
    def _():
        for h in range(heads):
            bias2[:, h * n:(h + 1) * n] = bias_ref[:, h * n:(h + 1) * n].astype(F32).T * LOG2E
        acc[...] = jnp.zeros_like(acc)
        qbd[...] = jnp.zeros_like(qbd)
        gobd[...] = jnp.zeros_like(gobd)
        first = lax.broadcasted_iota(jnp.int32, (cb * n, c), 1)
        vaug[:, c:] = jnp.where(first < 3, 1.0, 0.0).astype(BF)
        for ref in (gkvw_ref, gqgw_ref, gow_ref, gew_ref, svec_ref, small_ref):
            ref[...] = jnp.zeros_like(ref)

    lane = lax.broadcasted_iota(jnp.int32, (n, c), 1)
    g3 = vec_ref[2:3, :]
    g4 = vec_ref[3:4, :]
    wr = vec_ref[4:5, :]
    after = after_ref[...].reshape(cb * n, c)
    n3, _ = norm(after)
    x = (n3 * g3).astype(BF)
    nat = nn(x, w_ref[:, :3 * c])
    k_nat = nat[:, c:2 * c].astype(BF)
    vaug[:, :c] = nat[:, 2 * c:].astype(BF)
    q_nat = (nat[:, :c] * (scale * LOG2E)).astype(BF)
    tr = nt(wt_ref[...], x)
    q_t = (tr[:c] * (scale * LOG2E)).astype(BF)
    k_t = tr[c:2 * c].astype(BF)
    v_t = jnp.concatenate([tr[2 * c:3 * c], jnp.ones((16, cb * n), F32)], axis=0).astype(BF)
    gate_t = sigm(tr[3 * c:])
    for b, h in pairs:
        qbd[chans(h), lanes(b, h)] = q_t[chans(h), rows(b)]
        qn[lanes(b, h), :] = jnp.where((lane >= h * dh) & (lane < (h + 1) * dh), q_nat[rows(b)], jnp.zeros((n, c), BF))

    for s0, w0 in chunks(wide, wide):
        for b in every:
            sl = slice(b * wide + s0, b * wide + s0 + w0)
            sc = nn(k_nat[rows(b)], qbd[:, sl]) + bias2[:, s0:s0 + w0]
            top = jnp.max(sc, axis=0, keepdims=True)
            ex = jnp.exp2(sc - top).astype(BF)
            e_s[:, sl] = ex
            ores[:, sl] = nn(v_t[:, rows(b)], ex)
    r_of = {p: 1.0 / ores[c:c + 1, lanes(*p)] for p in pairs}
    o_of = {p: ores[chans(p[1]), lanes(*p)] * r_of[p] for p in pairs}
    o_t = jnp.concatenate([jnp.concatenate([o_of[b, h] for h in range(heads)], axis=0) for b in every], axis=1)
    y_t = (gate_t * o_t).astype(BF)
    out = nn(y_t.astype(F32).T.astype(BF), wo_ref[...]).astype(BF)
    mid = after + out.astype(F32)

    n4, sc4 = norm(mid)
    t = (n4 * g4).astype(BF)
    f = we_ref.shape[1] // 2
    racc = mid * wr
    for q in range(f // 128):
        u = nn(t, we_ref[:, q * 256:(q + 1) * 256])
        a, b = u[:, :128], u[:, 128:]
        zc = z_ref[:, q * 128:(q + 1) * 128]
        sig = sigm(a)
        silu = a * sig
        h_low = (silu * b).astype(BF)
        hv[:, q * 128:(q + 1) * 128] = h_low
        racc += h_low.astype(F32) * zc
        cu[:, q * 256:q * 256 + 128] = (zc * b * (sig + silu - silu * sig)).astype(BF)
        cu[:, q * 256 + 128:(q + 1) * 256] = (zc * silu).astype(BF)
    readout = jnp.sum(racc, axis=-1, keepdims=True)
    spot = lax.broadcasted_iota(jnp.int32, tgt_ref.shape, 1)
    pick = lambda ref: jnp.concatenate(
        [jnp.sum(jnp.where(spot == step * cb + b, ref[...], 0.0), axis=1, keepdims=True) for b in every], axis=0)
    err = readout - pick(tgt_ref)
    wer = pick(msk_ref) * err
    gr = 2.0 * wer
    small_ref[0:1, :] += jnp.sum(gr * mid, axis=0, keepdims=True)
    first = lax.broadcasted_iota(jnp.int32, (cb * n, c), 1)
    small_ref[2:3, :] += jnp.sum(jnp.where(first == 0, wer * err, 0.0), axis=0, keepdims=True)
    svec_ref[...] += jnp.sum(gr * hv[...].astype(F32), axis=0, keepdims=True)
    gew_ref[...] += nn((gr * t.astype(F32)).T.astype(BF), cu[...])
    gt = gr * nt(cu[...], we_ref[...])
    small_ref[1:2, :] += jnp.sum(gt * n4, axis=0, keepdims=True)
    gmid = gr * wr + norm_back(gt, g4, n4, sc4)
    gmid_ref[...] = gmid.reshape(gmid_ref.shape)

    gout = gmid.astype(BF)
    gow_ref[...] += nn(y_t, gout)
    gy_t = nt(wo_ref[...], gout)
    ggl_t = gy_t * o_t * gate_t * (1.0 - gate_t)
    go_t = (gy_t * gate_t).astype(BF).astype(F32)
    row = lax.broadcasted_iota(jnp.int32, (16, n), 0)
    gos = {}
    for b, h in pairs:
        part = (go_t[chans(h), rows(b)] * r_of[b, h]).astype(BF)
        gobd[chans(h), lanes(b, h)] = part
        part = part.astype(F32)
        gos[b, h] = part
        d = -jnp.sum(part * o_of[b, h], axis=0, keepdims=True)
        hi = d.astype(BF).astype(F32)
        mi = (d - hi).astype(BF).astype(F32)
        lo = d - hi - mi
        gobd[c:, lanes(b, h)] = jnp.where(row == 0, hi, jnp.where(row == 1, mi, jnp.where(row == 2, lo, 0.0))).astype(BF)
    go_n = jnp.concatenate([jnp.concatenate([gos[b, h] for h in range(heads)], axis=0) for b in every], axis=1).T.astype(BF)
    for b, h in pairs:
        gon[lanes(b, h), :] = jnp.where((lane >= h * dh) & (lane < (h + 1) * dh), go_n[rows(b)], jnp.zeros((n, c), BF))

    for s0, w0 in chunks(wide, wide):
        total = acc[:, s0:s0 + w0]
        for b in every:
            sl = slice(b * wide + s0, b * wide + s0 + w0)
            g = e_s[:, sl].astype(F32) * nn(vaug[rows(b), :c + 16], gobd[:, sl])
            total += g
            gl = g.astype(BF)
            gs_s[:, sl] = gl
            ores[:c, sl] = nn(k_t[:, rows(b)], gl)
        acc[:, s0:s0 + w0] = total
    gq_t = jnp.concatenate(
        [jnp.concatenate([ores[chans(h), lanes(b, h)] for h in range(heads)], axis=0) for b in every], axis=1) * scale
    gqg_t = jnp.concatenate([gq_t, ggl_t], axis=0).astype(BF)
    gk = [nn(gs_s[:, b * wide:(b + 1) * wide], qn[b * wide:(b + 1) * wide, :]) * (1.0 / LOG2E) for b in every]
    gv = [nn(e_s[:, b * wide:(b + 1) * wide], gon[b * wide:(b + 1) * wide, :]) for b in every]
    gkv = jnp.concatenate([jnp.concatenate([gk[b], gv[b]], axis=1) for b in every], axis=0).astype(BF)
    gqgw_ref[...] += nn(gqg_t, x)
    gkvw_ref[...] += nn(x.astype(F32).T.astype(BF), gkv)
    w_qg = jnp.concatenate([w_ref[:, :c], w_ref[:, 3 * c:]], axis=1)
    gx_ref[...] = (nt(gkv, w_ref[:, c:3 * c]) + nn(w_qg, gqg_t).T).reshape(gx_ref.shape)

    @pl.when(step == last)
    def _():
        for h in range(heads):
            gb_ref[:, h * n:(h + 1) * n] = acc[:, h * n:(h + 1) * n].T.astype(gb_ref.dtype)


def column_pass(after, tgt, msk, bias, w, wt, wo, we, vec, z):
    cols, n, c = after.shape
    heads = bias.shape[1] // n
    f = we.shape[1] // 2
    wide = heads * n
    cb = batch(cols, 3)
    full = lambda shape: pl.BlockSpec(shape, lambda j: (0,) * len(shape))
    col = pl.BlockSpec((cb, n, c), lambda j: (j, 0, 0))
    outs = [
        jax.ShapeDtypeStruct((cols, n, c), F32),
        jax.ShapeDtypeStruct((cols, n, c), F32),
        jax.ShapeDtypeStruct((n, wide), BF),
        jax.ShapeDtypeStruct((c, 2 * c), F32),
        jax.ShapeDtypeStruct((2 * c, c), F32),
        jax.ShapeDtypeStruct((c, c), F32),
        jax.ShapeDtypeStruct((c, 2 * f), F32),
        jax.ShapeDtypeStruct((1, f), F32),
        jax.ShapeDtypeStruct((8, c), F32),
    ]
    return pl.pallas_call(
        functools.partial(column_kernel, heads),
        grid=(cols // cb,),
        in_specs=[col] + [full(v.shape) for v in (tgt, msk, bias, w, wt, wo, we, vec, z)],
        out_specs=[col, col] + [full(o.shape) for o in outs[2:]],
        out_shape=outs,
        scratch_shapes=[
            pltpu.VMEM((n, wide), F32),
            pltpu.VMEM((n, cb * wide), BF),
            pltpu.VMEM((n, cb * wide), BF),
            pltpu.VMEM((n, wide), F32),
            pltpu.VMEM((c, cb * wide), BF),
            pltpu.VMEM((c + 16, cb * wide), BF),
            pltpu.VMEM((cb * n, 2 * c), BF),
            pltpu.VMEM((cb * wide, c), BF),
            pltpu.VMEM((cb * wide, c), BF),
            pltpu.VMEM((c + 16, cb * wide), F32),
            pltpu.VMEM((cb * n, 2 * f), BF),
            pltpu.VMEM((cb * n, f), BF),
        ],
        compiler_params=pltpu.CompilerParams(vmem_limit_bytes=56 << 20),
        cost_estimate=cost(12 * cols * heads * n * n * 128, 16 * cols * n * c, cols * heads * n * n),
        name="columns",
    )(after, tgt, msk, bias, w, wt, wo, we, vec, z)


GROUP = 16
AFTER_BATCH = 4
BACK_BATCH = 4


def spread(scr, start, count, stride, value):
    for t in range(scr.shape[0]):
        scr[t, pl.ds(start, count, stride=stride), :] = value[:, t * 128 : (t + 1) * 128]


def joined(scr, rows=slice(None)):
    return jnp.concatenate([scr[t, rows] for t in range(scr.shape[0])], axis=1)


def padded(count):
    return -(-count // 128) * 128


def operand_kernel(cols, off_ref, x_ref, wl_ref, wr_ref, *refs):
    keep_l, keep_r, send_l, send_r, n_ref, nc_ref, xc_ref, xs_ref, lscr, rscr, nscr, xscr, cscr = refs[-13:]
    rows, n, c = x_ref.shape
    wide = nc_ref.shape[1]
    half = c // 2
    own = off_ref[0]
    other = off_ref[1]
    for k in range(rows):
        x = x_ref[k].astype(F32)
        nrm, _ = norm(x)
        low = nrm.astype(BF)
        n_ref[k] = low
        nscr[k] = nrm
        xscr[k] = x
        p = nt(wl_ref[...], low)
        spread(lscr, k, c, rows, p[:c] * sigm(p[c:]))
    blank = [jnp.zeros((wide - 2 * cols, c), F32)] if wide > 2 * cols else []
    for k in range(rows):
        mine, theirs = nscr[k, pl.ds(own, cols), :], nscr[k, pl.ds(other, cols), :]
        near = jnp.concatenate([mine, theirs] + blank, axis=0).astype(BF)
        nc_ref[k] = near
        turned = jnp.concatenate([theirs, mine] + blank, axis=0).astype(BF)
        p = nt(wr_ref[:c], near)
        spread(rscr, k, half, rows, p[:half] * sigm(p[half:]))
        p = nt(wr_ref[c:], turned)
        spread(rscr, half * rows + k, half, rows, p[:half] * sigm(p[half:]))
        cscr[pl.ds(k, cols, stride=rows), :] = xscr[k, pl.ds(own, cols), :]
        cscr[pl.ds(cols * rows + k, cols, stride=rows), :] = xscr[k, pl.ds(other, cols), :]
    for scr, keep, send in ((lscr, keep_l, send_l), (rscr, keep_r, send_r)):
        cut = half * rows
        keep[...] = joined(scr, slice(0, cut)).astype(BF).reshape(keep.shape)
        send[...] = joined(scr, slice(cut, None)).astype(BF).reshape(send.shape)
    xc_ref[...] = cscr[:cols * rows].astype(BF).reshape(xc_ref.shape)
    xs_ref[...] = cscr[cols * rows:].astype(BF).reshape(xs_ref.shape)


def operands(offs, x, wl, wr, cols, start, total, bufs):
    count, n, c = x.shape
    half = c // 2
    wide = padded(2 * cols)
    g = GROUP
    at = start // g
    shapes = [
        ((half, count, n), (half, g, n), lambda b, o: (0, b, 0)),
        ((half, count, wide), (half, g, wide), lambda b, o: (0, b, 0)),
        ((half, count, n), (half, g, n), lambda b, o: (0, b, 0)),
        ((half, count, wide), (half, g, wide), lambda b, o: (0, b, 0)),
        ((total, n, c), (g, n, c), lambda b, o: (at + b, 0, 0)),
        ((total, wide, c), (g, wide, c), lambda b, o: (at + b, 0, 0)),
        ((cols, total, c), (cols, g, c), lambda b, o: (0, o[2 + at + b], 0)),
        ((cols, total, c), (cols, g, c), lambda b, o: (0, o[2 + at + b], 0)),
    ]
    full = lambda v: pl.BlockSpec(v.shape, lambda b, o: (0,) * v.ndim)
    ins = [x, wl, wr]
    specs = [pl.BlockSpec((g, n, c), lambda b, o: (b, 0, 0)), full(wl), full(wr)]
    alias = {}
    if bufs is not None:
        alias = {4 + i: 4 + i for i in range(4)}
        ins += list(bufs)
        specs += [pl.BlockSpec(memory_space=pl.ANY)] * 4
    got = pl.pallas_call(
        functools.partial(operand_kernel, cols),
        grid_spec=pltpu.PrefetchScalarGridSpec(
            num_scalar_prefetch=1,
            grid=(count // g,),
            in_specs=specs,
            out_specs=[pl.BlockSpec(b, m) for _, b, m in shapes],
            scratch_shapes=[
                pltpu.VMEM((n // 128, c * g, 128), F32),
                pltpu.VMEM((wide // 128, c * g, 128), F32),
                pltpu.VMEM((g, n, c), F32),
                pltpu.VMEM((g, n, c), F32),
                pltpu.VMEM((2 * cols * g, c), F32),
            ],
        ),
        out_shape=[jax.ShapeDtypeStruct(s, BF) for s, _, _ in shapes],
        input_output_aliases=alias,
        compiler_params=pltpu.CompilerParams(vmem_limit_bytes=60 << 20),
        cost_estimate=cost(8 * count * n * c * c, 8 * count * n * c, count * n * c),
        name="operands",
    )(offs, *ins)
    return got[:2], got[2:4], got[4:]


def product_kernel(groups, *refs):
    lefts, rights = refs[:groups], refs[groups:2 * groups]
    mine_ref, theirs_ref, scr = refs[2 * groups:]
    g = lefts[0].shape[0]
    cols = mine_ref.shape[0]
    for e in range(g):
        part = lax.dot_general(
            jnp.concatenate([r[e] for r in rights], axis=0),
            jnp.concatenate([r[e] for r in lefts], axis=0),
            (((0,), (0,)), ((), ())),
            preferred_element_type=F32,
        )
        spread(scr, e, 2 * cols, g, part[: 2 * cols])
    mine_ref[...] = joined(scr, slice(0, cols * g)).astype(mine_ref.dtype).reshape(mine_ref.shape)
    theirs_ref[...] = joined(scr, slice(cols * g, None)).astype(theirs_ref.dtype).reshape(theirs_ref.shape)


def products(lefts, rights, cols):
    half, _, n = lefts[0].shape
    wide = rights[0].shape[2]
    g = GROUP
    out = jax.ShapeDtypeStruct((cols, half, n), BF)
    return pl.pallas_call(
        functools.partial(product_kernel, len(lefts)),
        grid=(half // g,),
        in_specs=[pl.BlockSpec((g,) + v.shape[1:], lambda b: (b, 0, 0)) for v in lefts + rights],
        out_specs=[pl.BlockSpec((cols, g, n), lambda b: (0, b, 0))] * 2,
        out_shape=[out, out],
        scratch_shapes=[pltpu.VMEM((n // 128, 2 * cols * g, 128), F32)],
        compiler_params=pltpu.CompilerParams(vmem_limit_bytes=56 << 20),
        cost_estimate=cost(2 * half * n * n * wide, 4 * half * n * n),
        name="products",
    )(*lefts, *rights)


def batch(count, most):
    return max(b for b in range(1, most + 1) if count % b == 0)


def product_rows(mine_ref, theirs_ref):
    return jnp.concatenate(
        [
            jnp.concatenate([mine_ref[b].astype(F32), theirs_ref[b].astype(F32)], axis=0).T
            for b in range(mine_ref.shape[0])
        ],
        axis=0,
    )


def after_kernel(heads, core_ref, xm_ref, xo_ref, mine_ref, theirs_ref, w4_ref, wout_ref, wb_ref, vec_ref,
                 after_ref, bias_ref, xc_ref):
    cb, n, c = xc_ref.shape
    first = core_ref[0] == 0
    span = core_ref.shape[0]
    parts = []
    for b in range(cb):
        near, far = xm_ref[b].astype(F32), xo_ref[b].astype(F32)
        low, high = jnp.where(first, near, far), jnp.where(first, far, near)
        for r in range(0, n // 2, span):
            parts += [low[r:r + span], high[r:r + span]]
    x = jnp.concatenate(parts, axis=0)
    xc_ref[...] = x.astype(BF).reshape(xc_ref.shape)
    n0, _ = norm(x)
    gate = sigm(nn(n0.astype(BF), w4_ref[...]))
    nc, _ = norm(product_rows(mine_ref, theirs_ref))
    lin = nn((nc * vec_ref[1:2, :]).astype(BF), wout_ref[...])
    after = x + (gate * lin).astype(BF).astype(F32)
    after_ref[...] = after.reshape(after_ref.shape)
    n3, _ = norm(after)
    bias = nt(wb_ref[...], (n3 * vec_ref[2:3, :]).astype(BF))
    for b in range(cb):
        for h in range(heads):
            bias_ref[b, :, h * n:(h + 1) * n] = bias[h:h + 1, b * n:(b + 1) * n]


def afters(core, xm, xo, mine, theirs, w4, wout, wb, vec, heads):
    cols, rows, c = xm.shape
    n = 2 * rows
    half = mine.shape[1]
    cb = batch(cols, AFTER_BATCH)
    full = lambda v: pl.BlockSpec(v.shape, lambda b: (0,) * v.ndim)
    col = lambda a, b: pl.BlockSpec((cb, a, b), lambda j: (j, 0, 0))
    return pl.pallas_call(
        functools.partial(after_kernel, heads),
        grid=(cols // cb,),
        in_specs=[pl.BlockSpec(memory_space=pltpu.SMEM), col(rows, c), col(rows, c), col(half, n), col(half, n)]
        + [full(v) for v in (w4, wout, wb, vec)],
        out_specs=[col(n, c), col(1, heads * n), col(n, c)],
        out_shape=[
            jax.ShapeDtypeStruct((cols, n, c), F32),
            jax.ShapeDtypeStruct((cols, 1, heads * n), F32),
            jax.ShapeDtypeStruct((cols, n, c), BF),
        ],
        compiler_params=pltpu.CompilerParams(vmem_limit_bytes=56 << 20),
        cost_estimate=cost(8 * cols * n * c * c, 10 * cols * n * c, cols * n * c),
        name="afters",
    )(core, xm, xo, mine, theirs, w4, wout, wb, vec)


def back_kernel(after_ref, gx_ref, gmid_ref, gb_ref, xc_ref, mine_ref, theirs_ref, w4_ref, wout_ref, wb_ref, vec_ref,
                gmine_ref, gtheirs_ref, gwb_ref, gwout_ref, gw4_ref, small_ref):
    @pl.when(pl.program_id(0) == 0)
    def _():
        for ref in (gwb_ref, gwout_ref, gw4_ref, small_ref):
            ref[...] = jnp.zeros_like(ref)

    cb, n, c = xc_ref.shape
    half = mine_ref.shape[1]
    heads = gb_ref.shape[2]
    flat = lambda ref: ref[...].reshape(cb * n, c)
    g1 = vec_ref[1:2, :]
    g2 = vec_ref[2:3, :]
    n3, s3 = norm(flat(after_ref))
    x3 = (n3 * g2).astype(BF)
    parts = []
    for b in range(cb):
        gb = gb_ref[0, b].astype(F32)
        for d in range(1, gb_ref.shape[0]):
            gb = gb + gb_ref[d, b].astype(F32)
        parts.append(jnp.concatenate([gb, jnp.zeros((wb_ref.shape[0] - heads, n), F32)], axis=0))
    gb = jnp.concatenate(parts, axis=1)
    gwb_ref[...] += nn(gb.astype(BF), x3)
    gx = (flat(gx_ref) + nn(gb.T.astype(BF), wb_ref[...])).astype(BF).astype(F32)
    small_ref[0:1, :] += jnp.sum(gx * n3, axis=0, keepdims=True)
    gafter = (flat(gmid_ref) + norm_back(gx, g2, n3, s3)).astype(BF).astype(F32)

    n0, _ = norm(flat(xc_ref).astype(F32))
    n0 = n0.astype(BF)
    gate = sigm(nn(n0, w4_ref[...]))
    nc, sc = norm(product_rows(mine_ref, theirs_ref))
    centre = (nc * g1).astype(BF)
    lin = nn(centre, wout_ref[...])
    glin = (gafter * gate).astype(BF)
    gp4 = (gafter * lin * gate * (1.0 - gate)).astype(BF)
    gwout_ref[...] += nn(centre.astype(F32).T.astype(BF), glin)
    gw4_ref[...] += nn(n0.astype(F32).T.astype(BF), gp4)
    gc = nt(glin, wout_ref[...]).astype(BF).astype(F32)
    small_ref[1:2, :] += jnp.sum(gc * nc, axis=0, keepdims=True)
    gprod = norm_back(gc, g1, nc, sc)
    for b in range(cb):
        part = gprod[b * n:(b + 1) * n].T.astype(BF)
        gmine_ref[b] = part[:half]
        gtheirs_ref[b] = part[half:]


def back_pass(after, gx, gmid, gb, xc, mine, theirs, w4, wout, wb, vec):
    cols, n, c = xc.shape
    half = mine.shape[1]
    heads = gb.shape[2]
    cb = batch(cols, BACK_BATCH)
    full = lambda shape: pl.BlockSpec(shape, lambda b: (0,) * len(shape))
    col = lambda a, b: pl.BlockSpec((cb, a, b), lambda j: (j, 0, 0))
    accs = [wb.shape, (c, c), (c, c), (8, c)]
    return pl.pallas_call(
        back_kernel,
        grid=(cols // cb,),
        in_specs=[col(n, c)] * 3
        + [pl.BlockSpec((gb.shape[0], cb, heads, n), lambda j: (0, j, 0, 0)), col(n, c), col(half, n), col(half, n)]
        + [full(v.shape) for v in (w4, wout, wb, vec)],
        out_specs=[col(half, n)] * 2 + [full(s) for s in accs],
        out_shape=[jax.ShapeDtypeStruct((cols, half, n), BF)] * 2 + [jax.ShapeDtypeStruct(s, F32) for s in accs],
        compiler_params=pltpu.CompilerParams(vmem_limit_bytes=56 << 20),
        cost_estimate=cost(16 * cols * n * c * c, 24 * cols * n * c, cols * n * c),
        name="back",
    )(after, gx, gmid, gb, xc, mine, theirs, w4, wout, wb, vec)


def operand_grads_kernel(groups, *refs):
    sets = [refs[groups * s:groups * (s + 1)] for s in range(4)]
    gm_ref, gt_ref, gl_keep, gr_keep, gl_send, gr_send, scr, lscr, rscr = refs[4 * groups:]
    g, _, n = sets[0][0].shape
    wide = sets[2][0].shape[2]
    cols = gm_ref.shape[0]
    rows = gl_keep.shape[0]
    gm = gm_ref[...].astype(F32).reshape(cols * g, n)
    gt = gt_ref[...].astype(F32).reshape(cols * g, n)
    for t in range(n // 128):
        scr[t, : cols * g] = gm[:, t * 128 : (t + 1) * 128]
        scr[t, cols * g :] = gt[:, t * 128 : (t + 1) * 128]
    blank = [jnp.zeros((wide - 2 * cols, n), F32)] if wide > 2 * cols else []
    fetch = lambda at: jnp.concatenate([scr[t, pl.ds(at, cols, stride=g), :] for t in range(n // 128)], axis=1)
    for part, (gl_ref, gr_ref) in enumerate(((gl_keep, gr_keep), (gl_send, gr_send))):
        for e in range(g):
            pieces = [fetch(e), fetch(cols * g + e)]
            gp = jnp.concatenate(pieces + blank, axis=0).astype(BF)
            seen = gp if part == 0 else jnp.concatenate(pieces[::-1] + blank, axis=0).astype(BF)
            left = jnp.concatenate([r[e] for r in sets[part]], axis=0)
            right = jnp.concatenate([r[e] for r in sets[2 + part]], axis=0)
            spread(rscr, e, rows, g, nt(left, seen))
            spread(lscr, e, rows, g, nn(right, gp))
        gl_ref[...] = joined(lscr).astype(BF).reshape(gl_ref.shape)
        gr_ref[...] = joined(rscr).astype(BF).reshape(gr_ref.shape)


def operand_grads(keep_l, recv_l, keep_r, recv_r, gmine, gtheirs):
    half, _, n = keep_l[0].shape
    wide = keep_r[0].shape[2]
    rows = sum(v.shape[1] for v in keep_l)
    cols = gmine.shape[0]
    g = GROUP
    ins = keep_l + recv_l + keep_r + recv_r
    left = pl.BlockSpec((rows, g, n), lambda b: (0, b, 0))
    right = pl.BlockSpec((rows, g, wide), lambda b: (0, b, 0))
    return pl.pallas_call(
        functools.partial(operand_grads_kernel, len(keep_l)),
        grid=(half // g,),
        in_specs=[pl.BlockSpec((g,) + v.shape[1:], lambda b: (b, 0, 0)) for v in ins]
        + [pl.BlockSpec((cols, g, n), lambda b: (0, b, 0))] * 2,
        out_specs=[left, right] * 2,
        out_shape=[jax.ShapeDtypeStruct((rows, half, n), BF), jax.ShapeDtypeStruct((rows, half, wide), BF)] * 2,
        scratch_shapes=[
            pltpu.VMEM((n // 128, 2 * cols * g, 128), F32),
            pltpu.VMEM((n // 128, rows * g, 128), F32),
            pltpu.VMEM((wide // 128, rows * g, 128), F32),
        ],
        compiler_params=pltpu.CompilerParams(vmem_limit_bytes=60 << 20),
        cost_estimate=cost(4 * half * n * n * wide, 8 * half * n * n),
        name="operand_grads",
    )(*ins, gmine, gtheirs)


def tri_grads_kernel(n_ref, nc_ref, gl_ref, gr_ref, wl_ref, wr_ref, al_ref, ar_ref, lg, rg):
    @pl.when(pl.program_id(0) == 0)
    def _():
        al_ref[...] = jnp.zeros_like(al_ref)
        ar_ref[...] = jnp.zeros_like(ar_ref)
    rows, n, c = n_ref.shape
    wide = nc_ref.shape[1]
    half = gl_ref.shape[1]
    def one(low, grad, w):
        p = nt(w, low)
        s = sigm(p[half:])
        first = grad.astype(F32) * s
        return first.astype(BF), (first * p[:half] * (1.0 - s)).astype(BF)
    for k in range(rows):
        a, b = one(n_ref[k], gl_ref[k], wl_ref[...])
        lg[:half, k*n:(k+1)*n] = a
        lg[half:, k*n:(k+1)*n] = b
        a, b = one(nc_ref[k], gr_ref[k], wr_ref[...])
        rg[:half, k*wide:(k+1)*wide] = a
        rg[half:, k*wide:(k+1)*wide] = b
    al_ref[...] += nn(lg[...], n_ref[...].reshape(rows*n, c))
    ar_ref[...] += nn(rg[...], nc_ref[...].reshape(rows*wide, c))


def tri_grads(nrm, near, gl, gr, wl, wr):
    count, n, c = nrm.shape
    half = gl.shape[1]
    wide = near.shape[1]
    rows = batch(count, 24)
    full = lambda v: pl.BlockSpec(v.shape, lambda b: (0,) * v.ndim)
    row = lambda a, b: pl.BlockSpec((rows, a, b), lambda k: (k, 0, 0))
    out = jax.ShapeDtypeStruct((2 * half, c), F32)
    return pl.pallas_call(
        tri_grads_kernel,
        grid=(count // rows,),
        in_specs=[row(n, c), row(wide, c), row(half, n), row(half, wide), full(wl), full(wr)],
        out_specs=[pl.BlockSpec(out.shape, lambda k: (0, 0))] * 2,
        out_shape=[out] * 2,
        scratch_shapes=[pltpu.VMEM((2*half, rows*n), BF), pltpu.VMEM((2*half, rows*wide), BF)],
        compiler_params=pltpu.CompilerParams(vmem_limit_bytes=56 << 20),
        cost_estimate=cost(8 * count * n * c * c, 8 * count * n * c, count * n * half),
        name="tri_grads",
    )(nrm, near, gl, gr, wl, wr)


def gather_weights(tri, tri_out, attn, bias, outp, expand, shrink, vectors):
    rows = tri.shape[1]
    pieces = [tri[0], tri_out[0], attn[0], outp[0], expand[0], shrink[0].reshape(rows, -1), bias[0], vectors.T]
    widths = [p.shape[1] for p in pieces]
    packed = lax.all_gather(jnp.concatenate([p.astype(BF) for p in pieces], axis=1), "item", axis=0, tiled=True)
    got, at = [], 0
    for w in widths:
        got.append(packed[:, at : at + w])
        at += w
    tri, tri_out, attn, outp, expand, shr, bias, vec = got
    return tri, tri_out, attn, bias, outp, expand, shr.reshape(-1, shrink.shape[2]), vec.T


def gather_rows(rows):
    size = lax.axis_size("pair")
    here = lax.axis_index("pair")
    count = rows.shape[0]
    if size != 8 or count % 48:
        sets = [list(range(c, size, 2)) for c in range(2)]
        return [lax.all_gather(rows, "pair", axis=0, tiled=True, axis_index_groups=sets)], jnp.arange(
            size // 2 * count // GROUP
        )
    stages = 3
    step = count // stages
    per = step // GROUP
    x = [rows[s * step : (s + 1) * step] for s in range(stages)]
    spot = lambda device, s: [device // 2 * (stages * per) + s * per + u for u in range(per)]
    groups, places = [rows], [p for s in range(stages) for p in spot(here, s)]
    late = []
    for s in range(stages):
        side, above = exchange(x[s], "pair", 2), exchange(x[s], "pair", 4)
        if s + 1 < stages:
            x[s + 1], side, above = lax.optimization_barrier((x[s + 1], side, above))
        groups.append(jnp.concatenate([side, above] + late))
        places += spot(here ^ 2, s) + spot(here ^ 4, s) + (spot(here ^ 6, s - 1) if late else [])
        late = [exchange(side[: step // 2], "pair", 4), exchange(above[step // 2 :], "pair", 2)]
    groups.append(jnp.concatenate(late))
    places += spot(here ^ 6, stages - 1)
    return groups, jnp.stack(places)


def swap_cores(value):
    size = lax.axis_size("pair")
    return lax.ppermute(value, "pair", [(d, d ^ 1) for d in range(size)])


def exchange(value, axis, bit):
    size = lax.axis_size(axis)
    return lax.ppermute(value, axis, [(d, d ^ bit) for d in range(size)])


def sum_axis(value, axis):
    bit = 1
    while bit < lax.axis_size(axis):
        value = value + exchange(value, axis, bit)
        bit *= 2
    return value


def sum_all(value):
    return sum_axis(sum_axis(value, "item"), "pair")


def sum_shards(parts):
    size = lax.axis_size("item")
    here = lax.axis_index("item")
    bit = size // 2
    while bit:
        upper = (here // bit) % 2
        kept, sent = [], []
        for part in parts:
            rows = part.shape[0] // 2
            kept.append(lax.dynamic_slice_in_dim(part, upper * rows, rows, 0))
            sent.append(lax.dynamic_slice_in_dim(part, (1 - upper) * rows, rows, 0))
        parts = [k + exchange(s.astype(BF), "item", bit).astype(F32) for k, s in zip(kept, sent)]
        bit //= 2
    return [sum_axis(part, "pair") for part in parts]


def on_device(
    pair_act,
    targets,
    pair_mask,
    tri_proj,
    tri_out,
    attention_proj,
    bias_proj,
    output_proj,
    expand_proj,
    shrink_proj,
    vectors,
    first_tri,
    first_tri_out,
    first_attention,
    first_bias,
    first_output,
    first_expand,
    first_shrink,
    first_vectors,
    second_tri,
    second_tri_out,
    second_attention,
    second_bias,
    second_output,
    second_expand,
    second_shrink,
    second_vectors,
):
    layers = attention_proj.shape[0]
    assert layers == 1
    cols, tokens, width = pair_act.shape[1:]
    half = width // 2
    heads = bias_proj.shape[2]
    here = lax.axis_index("pair")
    core = here % 2
    groups, places = gather_rows(pair_act[0])
    weight = gather_weights(
        tri_proj, tri_out, attention_proj, bias_proj, output_proj, expand_proj, shrink_proj, vectors
    )
    tri_w, tri_out_w, project_w, pairbias_w, output_w, expand_w, shrink_w, vector_low = weight
    vec = vector_low.astype(F32)
    weighting_rows = pair_mask.astype(F32)
    both = lax.all_to_all(
        jnp.concatenate([targets, weighting_rows]), "pair", split_axis=2, concat_axis=1, tiled=True
    )

    scaled = (tri_w.astype(F32) * vec[0][:, None]).astype(BF).T
    tri_half = lambda s, c: lax.dynamic_slice_in_dim(scaled, width * s + half * c, half, 0)
    near_w = [tri_half(s, core) for s in range(4)]
    far_w = [tri_half(s, 1 - core) for s in range(4)]
    w_left = jnp.concatenate([near_w[0], far_w[0], near_w[1], far_w[1]])
    w_right = jnp.concatenate([near_w[2], near_w[3], far_w[2], far_w[3]])
    w_gate = scaled[4 * width :].T
    wout = jnp.roll(tri_out_w, -half * core, axis=0)
    gain_c = jnp.roll(vec[1], -half * core)
    vec8 = jnp.concatenate([vec[:1], gain_c[None], vec[2:], jnp.zeros((3, width), F32)])
    wb = jnp.concatenate([pairbias_w.T, jnp.zeros((16 - heads, width), BF)])

    offs = jnp.concatenate(
        [jnp.stack([here * cols, (here + 1 - 2 * core) * cols]), places]
    ).astype(jnp.int32)
    keep, recv, bufs, start = [], [], None, 0
    for rows in groups:
        mine, sent, bufs = operands(offs, rows, w_left, w_right, cols, start, tokens // 2, bufs)
        keep.append(mine)
        recv.append([swap_cores(v) for v in sent])
        start += rows.shape[0]
    nrm, near, xm, xs = bufs
    xo = swap_cores(xs)
    keep_l, keep_r = [v[0] for v in keep], [v[1] for v in keep]
    recv_l, recv_r = [v[0] for v in recv], [v[1] for v in recv]
    mine, send = products(keep_l + recv_l, keep_r + recv_r, cols)
    theirs = swap_cores(send)
    cores = jnp.full((cols,), core, jnp.int32)
    after_c, bias_part, xc = afters(cores, xm, xo, mine, theirs, w_gate, wout, wb, vec8, heads)
    bias_full = lax.all_gather(bias_part[:, 0].astype(BF), "pair", axis=0, tiled=True)
    hidden = expand_w.shape[1] // 2
    expand_mix = (
        expand_w.reshape(width, 2, hidden // 128, 128).swapaxes(1, 2).reshape(width, 2 * hidden)
    )
    z = jnp.sum(shrink_w.astype(F32) * vec[4], axis=1)[None]
    gx, gmid, gb, gkv_w, gqg_w, gow, gew, svec, small = column_pass(
        after_c, both[0], both[1], bias_full, project_w, project_w.T, output_w, expand_mix, vec8, z
    )
    bias_cols = lax.all_to_all(gb, "pair", split_axis=0, concat_axis=0, tiled=True)
    scalars = sum_all(jnp.stack([jnp.sum(small[2]), jnp.sum(weighting_rows)]))
    gmine, gsend, gwb, gwout, gw4, small2 = back_pass(
        after_c, gx, gmid, bias_cols.reshape(-1, cols, heads, tokens), xc, mine, theirs,
        w_gate, wout, wb, vec8,
    )
    gtheirs = swap_cores(gsend)
    gl, gr, gl_sent, gr_sent = operand_grads(keep_l, recv_l, keep_r, recv_r, gmine, gtheirs)
    gl_far, gr_far = swap_cores(gl_sent), swap_cores(gr_sent)
    w_l = [jnp.concatenate([w[0], w[1]]) for w in (near_w, far_w)]
    w_r = [jnp.concatenate([w[2], w[3]]) for w in (near_w, far_w)]
    near_a = tri_grads(nrm, near, gl, gr, w_l[0], w_r[0])
    far_a = tri_grads(nrm, near, gl_far, gr_far, w_l[1], w_r[1])
    a_tri = []
    for near_part, far_part in zip(near_a, far_a):
        for s in range(2):
            parts = [p[s * half : (s + 1) * half] for p in (near_part, far_part)]
            a_tri += [jnp.where(core == 0, parts[0], parts[1]), jnp.where(core == 0, parts[1], parts[0])]
    a_tri = jnp.concatenate(a_tri + [gw4.T]).T
    g_read = small[0] + jnp.sum(svec[0][:, None] * shrink_w.astype(F32), axis=0)
    g_vec = jnp.stack(
        [
            jnp.sum(a_tri * tri_w.astype(F32), axis=1),
            jnp.roll(small2[1], half * core),
            small2[0],
            small[1],
            g_read,
        ]
    )
    (total,) = sum_shards(
        [
            jnp.concatenate(
                [
                    gqg_w[:width].T,
                    gkv_w,
                    gqg_w[width:].T,
                    gow,
                    gew,
                    a_tri * vec[0][:, None],
                    jnp.roll(gwout, half * core, axis=0),
                    svec.reshape(width, -1),
                    gwb[:heads].T,
                    g_vec.T,
                ],
                axis=1,
            )
        ]
    )
    loss_sum, count = scalars[0], scalars[1]
    widths = (4 * width, width, 2 * hidden, 5 * width, width, svec.shape[1] // width, heads)
    cuts = []
    for w in widths:
        cuts.append(total[:, :w])
        total = total[:, w:]
    shards = [
        cuts[3],
        cuts[4],
        cuts[0],
        cuts[6],
        cuts[1],
        cuts[2].reshape(-1, hidden // 128, 2, 128).swapaxes(1, 2).reshape(-1, 2 * hidden),
        cuts[5].reshape(-1, 1) * vec[4][None, :],
        total.T,
    ]
    shards = [s / count for s in shards]
    squares = sum_axis(sum(jnp.sum(s * s) for s in shards), "item")
    grad_norm = jnp.sqrt(squares)
    factor = jnp.minimum(1.0, clip_limit / (grad_norm + 1e-06))
    shards = [s[None] for s in shards[:7]] + shards[7:]
    masters = (
        tri_proj,
        tri_out,
        attention_proj,
        bias_proj,
        output_proj,
        expand_proj,
        shrink_proj,
        vectors,
    )
    firsts = (
        first_tri,
        first_tri_out,
        first_attention,
        first_bias,
        first_output,
        first_expand,
        first_shrink,
        first_vectors,
    )
    seconds = (
        second_tri,
        second_tri_out,
        second_attention,
        second_bias,
        second_output,
        second_expand,
        second_shrink,
        second_vectors,
    )
    rates = (learn_rate,) * 7 + (vector_rate,)
    new_masters, new_firsts, new_seconds = ([], [], [])
    for master, grad, first, second, rate in zip(masters, shards, firsts, seconds, rates):
        clipped = grad * factor
        moment = beta_first * first + (1 - beta_first) * clipped
        square = beta_second * second + (1 - beta_second) * clipped * clipped
        stride = (
            moment
            / (1 - beta_first**STEP)
            / (jnp.sqrt(square / (1 - beta_second**STEP)) + adam_epsilon)
        )
        new_masters.append(master - rate * (stride + weight_decay * master))
        new_firsts.append(moment)
        new_seconds.append(square)
    return (
        (loss_sum, count, grad_norm) + tuple(new_masters) + tuple(new_firsts) + tuple(new_seconds)
    )


def solution(mesh):
    in_specs = (
        P("item", "pair", None, None),
        P("item", "pair", None),
        P("item", "pair", None),
        P(None, "item", None),
        P(None, "item", None),
        P(None, "item", None),
        P(None, "item", None),
        P(None, "item", None),
        P(None, "item", None),
        P(None, "item", None),
        P(None, "item"),
        P(None, "item", None),
        P(None, "item", None),
        P(None, "item", None),
        P(None, "item", None),
        P(None, "item", None),
        P(None, "item", None),
        P(None, "item", None),
        P(None, "item"),
        P(None, "item", None),
        P(None, "item", None),
        P(None, "item", None),
        P(None, "item", None),
        P(None, "item", None),
        P(None, "item", None),
        P(None, "item", None),
        P(None, "item"),
    )
    out_specs = (
        P(),
        P(),
        P(),
        P(None, "item", None),
        P(None, "item", None),
        P(None, "item", None),
        P(None, "item", None),
        P(None, "item", None),
        P(None, "item", None),
        P(None, "item", None),
        P(None, "item"),
        P(None, "item", None),
        P(None, "item", None),
        P(None, "item", None),
        P(None, "item", None),
        P(None, "item", None),
        P(None, "item", None),
        P(None, "item", None),
        P(None, "item"),
        P(None, "item", None),
        P(None, "item", None),
        P(None, "item", None),
        P(None, "item", None),
        P(None, "item", None),
        P(None, "item", None),
        P(None, "item", None),
        P(None, "item"),
    )
    return jax.shard_map(
        on_device, mesh=mesh, in_specs=in_specs, out_specs=out_specs, check_vma=False
    )
```

```python
import functools

import jax
import jax.numpy as jnp
from jax import lax
from jax.experimental import pallas as pl
from jax.experimental.pallas import tpu as pltpu
from jax.sharding import PartitionSpec as P

STEP = 10

norm_epsilon = 1e-05
clip_limit = 0.001
learn_rate = 0.1
vector_rate = 0.8
beta_first = 0.9
beta_second = 0.999
adam_epsilon = 1e-08
weight_decay = 0.01

BF = jnp.bfloat16
F32 = jnp.float32
LOG2E = 1.4426950408889634
EPS = norm_epsilon


def cost(flops, moved, exps=0):
    return pl.CostEstimate(flops=int(flops), bytes_accessed=int(moved), transcendentals=int(exps))


def nn(a, b):
    return lax.dot_general(a, b, (((1,), (0,)), ((), ())), preferred_element_type=F32)

def nt(a, b):
    return lax.dot_general(a, b, (((1,), (1,)), ((), ())), preferred_element_type=F32)

def sigm(v):
    return 0.5 * jnp.tanh(0.5 * v) + 0.5

def norm(v):
    mean = jnp.mean(v, axis=-1, keepdims=True)
    cen = v - mean
    scale = lax.rsqrt(jnp.mean(cen * cen, axis=-1, keepdims=True) + EPS)
    return cen * scale, scale

def norm_back(up, gain, n, scale):
    inner = up * gain
    return scale * (inner - jnp.mean(inner, axis=-1, keepdims=True) - n * jnp.mean(inner * n, axis=-1, keepdims=True))

def chunks(total, width):
    return [(s, min(width, total - s)) for s in range(0, total, width)]

def column_kernel(heads, after_ref, tgt_ref, msk_ref, bias_ref, w_ref, wt_ref, wo_ref, we_ref, vec_ref, z_ref,
                gx_ref, gmid_ref, gb_ref, gkvw_ref, gqgw_ref, gow_ref, gew_ref, svec_ref, small_ref,
                bias2, e_s, gs_s, acc, qbd, gobd, vaug, qn, gon, ores, cu, hv):
    step = pl.program_id(0)
    last = pl.num_programs(0) - 1
    cb, n, c = after_ref.shape
    dh = c // heads
    wide = heads * n
    scale = dh ** -0.5
    every = range(cb)
    pairs = [(b, h) for b in every for h in range(heads)]
    lanes = lambda b, h: slice(b * wide + h * n, b * wide + (h + 1) * n)
    rows = lambda b: slice(b * n, (b + 1) * n)
    chans = lambda h: slice(h * dh, (h + 1) * dh)

    @pl.when(step == 0)
    def _():
        for h in range(heads):
            bias2[:, h * n:(h + 1) * n] = bias_ref[:, h * n:(h + 1) * n].astype(F32).T * LOG2E
        acc[...] = jnp.zeros_like(acc)
        qbd[...] = jnp.zeros_like(qbd)
        gobd[...] = jnp.zeros_like(gobd)
        first = lax.broadcasted_iota(jnp.int32, (cb * n, c), 1)
        vaug[:, c:] = jnp.where(first < 3, 1.0, 0.0).astype(BF)
        for ref in (gkvw_ref, gqgw_ref, gow_ref, gew_ref, svec_ref, small_ref):
            ref[...] = jnp.zeros_like(ref)

    lane = lax.broadcasted_iota(jnp.int32, (n, c), 1)
    g3 = vec_ref[2:3, :]
    g4 = vec_ref[3:4, :]
    wr = vec_ref[4:5, :]
    after = after_ref[...].reshape(cb * n, c)
    n3, _ = norm(after)
    x = (n3 * g3).astype(BF)
    nat = nn(x, w_ref[:, :3 * c])
    k_nat = nat[:, c:2 * c].astype(BF)
    vaug[:, :c] = nat[:, 2 * c:].astype(BF)
    q_nat = (nat[:, :c] * (scale * LOG2E)).astype(BF)
    tr = nt(wt_ref[...], x)
    q_t = (tr[:c] * (scale * LOG2E)).astype(BF)
    k_t = tr[c:2 * c].astype(BF)
    v_t = jnp.concatenate([tr[2 * c:3 * c], jnp.ones((16, cb * n), F32)], axis=0).astype(BF)
    gate_t = sigm(tr[3 * c:])
    for b, h in pairs:
        qbd[chans(h), lanes(b, h)] = q_t[chans(h), rows(b)]
        qn[lanes(b, h), :] = jnp.where((lane >= h * dh) & (lane < (h + 1) * dh), q_nat[rows(b)], jnp.zeros((n, c), BF))

    for s0, w0 in chunks(wide, wide):
        for b in every:
            sl = slice(b * wide + s0, b * wide + s0 + w0)
            sc = nn(k_nat[rows(b)], qbd[:, sl]) + bias2[:, s0:s0 + w0]
            top = jnp.max(sc, axis=0, keepdims=True)
            ex = jnp.exp2(sc - top).astype(BF)
            e_s[:, sl] = ex
            ores[:, sl] = nn(v_t[:, rows(b)], ex)
    r_of = {p: 1.0 / ores[c:c + 1, lanes(*p)] for p in pairs}
    o_of = {p: ores[chans(p[1]), lanes(*p)] * r_of[p] for p in pairs}
    o_t = jnp.concatenate([jnp.concatenate([o_of[b, h] for h in range(heads)], axis=0) for b in every], axis=1)
    y_t = (gate_t * o_t).astype(BF)
    out = nn(y_t.astype(F32).T.astype(BF), wo_ref[...]).astype(BF)
    mid = after + out.astype(F32)

    n4, sc4 = norm(mid)
    t = (n4 * g4).astype(BF)
    f = we_ref.shape[1] // 2
    racc = mid * wr
    u = nn(t, we_ref[...])
    a, b = u[:, :f], u[:, f:]
    sig = sigm(a)
    silu = a * sig
    h_low = (silu * b).astype(BF)
    hv[...] = h_low
    part = h_low.astype(F32) * z_ref[...]
    for q in range(f // c):
        racc += part[:, q * c:(q + 1) * c]
    cu[:, :f] = (z_ref[...] * b * (sig + silu - silu * sig)).astype(BF)
    cu[:, f:] = (z_ref[...] * silu).astype(BF)
    readout = jnp.sum(racc, axis=-1, keepdims=True)
    spot = lax.broadcasted_iota(jnp.int32, tgt_ref.shape, 1)
    pick = lambda ref: jnp.concatenate(
        [jnp.sum(jnp.where(spot == step * cb + b, ref[...], 0.0), axis=1, keepdims=True) for b in every], axis=0)
    err = readout - pick(tgt_ref)
    wer = pick(msk_ref) * err
    gr = 2.0 * wer
    small_ref[0:1, :] += jnp.sum(gr * mid, axis=0, keepdims=True)
    first = lax.broadcasted_iota(jnp.int32, (cb * n, c), 1)
    small_ref[2:3, :] += jnp.sum(jnp.where(first == 0, wer * err, 0.0), axis=0, keepdims=True)
    svec_ref[...] += jnp.sum(gr * hv[...].astype(F32), axis=0, keepdims=True)
    gew_ref[...] += nn((gr * t.astype(F32)).T.astype(BF), cu[...])
    gt = gr * nt(cu[...], we_ref[...])
    small_ref[1:2, :] += jnp.sum(gt * n4, axis=0, keepdims=True)
    gmid = gr * wr + norm_back(gt, g4, n4, sc4)
    gmid_ref[...] = gmid.reshape(gmid_ref.shape)

    gout = gmid.astype(BF)
    gow_ref[...] += nn(y_t, gout)
    gy_t = nt(wo_ref[...], gout)
    ggl_t = gy_t * o_t * gate_t * (1.0 - gate_t)
    go_t = (gy_t * gate_t).astype(BF).astype(F32)
    row = lax.broadcasted_iota(jnp.int32, (16, n), 0)
    gos = {}
    for b, h in pairs:
        part = (go_t[chans(h), rows(b)] * r_of[b, h]).astype(BF)
        gobd[chans(h), lanes(b, h)] = part
        part = part.astype(F32)
        gos[b, h] = part
        d = -jnp.sum(part * o_of[b, h], axis=0, keepdims=True)
        hi = d.astype(BF).astype(F32)
        mi = (d - hi).astype(BF).astype(F32)
        lo = d - hi - mi
        gobd[c:, lanes(b, h)] = jnp.where(row == 0, hi, jnp.where(row == 1, mi, jnp.where(row == 2, lo, 0.0))).astype(BF)
    go_n = jnp.concatenate([jnp.concatenate([gos[b, h] for h in range(heads)], axis=0) for b in every], axis=1).T.astype(BF)
    for b, h in pairs:
        gon[lanes(b, h), :] = jnp.where((lane >= h * dh) & (lane < (h + 1) * dh), go_n[rows(b)], jnp.zeros((n, c), BF))

    for s0, w0 in chunks(wide, wide):
        total = acc[:, s0:s0 + w0]
        for b in every:
            sl = slice(b * wide + s0, b * wide + s0 + w0)
            g = e_s[:, sl].astype(F32) * nn(vaug[rows(b), :c + 16], gobd[:, sl])
            total += g
            gl = g.astype(BF)
            gs_s[:, sl] = gl
            ores[:c, sl] = nn(k_t[:, rows(b)], gl)
        acc[:, s0:s0 + w0] = total
    gq_t = jnp.concatenate(
        [jnp.concatenate([ores[chans(h), lanes(b, h)] for h in range(heads)], axis=0) for b in every], axis=1) * scale
    gqg_t = jnp.concatenate([gq_t, ggl_t], axis=0).astype(BF)
    gk = [nn(gs_s[:, b * wide:(b + 1) * wide], qn[b * wide:(b + 1) * wide, :]) * (1.0 / LOG2E) for b in every]
    gv = [nn(e_s[:, b * wide:(b + 1) * wide], gon[b * wide:(b + 1) * wide, :]) for b in every]
    gkv = jnp.concatenate([jnp.concatenate([gk[b], gv[b]], axis=1) for b in every], axis=0).astype(BF)
    gqgw_ref[...] += nn(gqg_t, x)
    gkvw_ref[...] += nn(x.astype(F32).T.astype(BF), gkv)
    w_qg = jnp.concatenate([w_ref[:, :c], w_ref[:, 3 * c:]], axis=1)
    gx_ref[...] = (nt(gkv, w_ref[:, c:3 * c]) + nn(w_qg, gqg_t).T).reshape(gx_ref.shape)

    @pl.when(step == last)
    def _():
        for h in range(heads):
            gb_ref[:, h * n:(h + 1) * n] = acc[:, h * n:(h + 1) * n].T.astype(gb_ref.dtype)


def column_pass(after, tgt, msk, bias, w, wt, wo, we, vec, z):
    cols, n, c = after.shape
    heads = bias.shape[1] // n
    f = we.shape[1] // 2
    wide = heads * n
    cb = batch(cols, 3)
    full = lambda shape: pl.BlockSpec(shape, lambda j: (0,) * len(shape))
    col = pl.BlockSpec((cb, n, c), lambda j: (j, 0, 0))
    outs = [
        jax.ShapeDtypeStruct((cols, n, c), F32),
        jax.ShapeDtypeStruct((cols, n, c), F32),
        jax.ShapeDtypeStruct((n, wide), BF),
        jax.ShapeDtypeStruct((c, 2 * c), F32),
        jax.ShapeDtypeStruct((2 * c, c), F32),
        jax.ShapeDtypeStruct((c, c), F32),
        jax.ShapeDtypeStruct((c, 2 * f), F32),
        jax.ShapeDtypeStruct((1, f), F32),
        jax.ShapeDtypeStruct((8, c), F32),
    ]
    return pl.pallas_call(
        functools.partial(column_kernel, heads),
        grid=(cols // cb,),
        in_specs=[col] + [full(v.shape) for v in (tgt, msk, bias, w, wt, wo, we, vec, z)],
        out_specs=[col, col] + [full(o.shape) for o in outs[2:]],
        out_shape=outs,
        scratch_shapes=[
            pltpu.VMEM((n, wide), F32),
            pltpu.VMEM((n, cb * wide), BF),
            pltpu.VMEM((n, cb * wide), BF),
            pltpu.VMEM((n, wide), F32),
            pltpu.VMEM((c, cb * wide), BF),
            pltpu.VMEM((c + 16, cb * wide), BF),
            pltpu.VMEM((cb * n, 2 * c), BF),
            pltpu.VMEM((cb * wide, c), BF),
            pltpu.VMEM((cb * wide, c), BF),
            pltpu.VMEM((c + 16, cb * wide), F32),
            pltpu.VMEM((cb * n, 2 * f), BF),
            pltpu.VMEM((cb * n, f), BF),
        ],
        compiler_params=pltpu.CompilerParams(vmem_limit_bytes=56 << 20),
        cost_estimate=cost(12 * cols * heads * n * n * 128, 16 * cols * n * c, cols * heads * n * n),
        name="columns",
    )(after, tgt, msk, bias, w, wt, wo, we, vec, z)


GROUP = 16
AFTER_BATCH = 4
BACK_BATCH = 4


def spread(scr, start, count, stride, value):
    for t in range(scr.shape[0]):
        scr[t, pl.ds(start, count, stride=stride), :] = value[:, t * 128 : (t + 1) * 128]


def joined(scr, rows=slice(None)):
    return jnp.concatenate([scr[t, rows] for t in range(scr.shape[0])], axis=1)


def padded(count):
    return -(-count // 128) * 128


def operand_kernel(cols, off_ref, x_ref, wl_ref, wr_ref, *refs):
    keep_ref, send_ref, n_ref, nc_ref, xc_ref, xs_ref, lscr, rscr, nscr, xscr, cscr = refs[-11:]
    rows, n, c = x_ref.shape
    wide = nc_ref.shape[1]
    half = c // 2
    own = off_ref[0]
    other = off_ref[1]
    for k in range(rows):
        x = x_ref[k].astype(F32)
        nrm, _ = norm(x)
        low = nrm.astype(BF)
        n_ref[k] = low
        nscr[k] = nrm
        xscr[k] = x
        p = nt(wl_ref[...], low)
        spread(lscr, k, c, rows, p[:c] * sigm(p[c:]))
    blank = [jnp.zeros((wide - 2 * cols, c), F32)] if wide > 2 * cols else []
    for k in range(rows):
        mine, theirs = nscr[k, pl.ds(own, cols), :], nscr[k, pl.ds(other, cols), :]
        near = jnp.concatenate([mine, theirs] + blank, axis=0).astype(BF)
        nc_ref[k] = near
        turned = jnp.concatenate([theirs, mine] + blank, axis=0).astype(BF)
        p = nt(wr_ref[:c], near)
        spread(rscr, k, half, rows, p[:half] * sigm(p[half:]))
        p = nt(wr_ref[c:], turned)
        spread(rscr, half * rows + k, half, rows, p[:half] * sigm(p[half:]))
        cscr[pl.ds(k, cols, stride=rows), :] = xscr[k, pl.ds(own, cols), :]
        cscr[pl.ds(cols * rows + k, cols, stride=rows), :] = xscr[k, pl.ds(other, cols), :]
    cut = half * rows
    for ref, span in ((keep_ref, slice(0, cut)), (send_ref, slice(cut, None))):
        both = jnp.concatenate([joined(lscr, span), joined(rscr, span)], axis=1)
        ref[...] = both.astype(BF).reshape(ref.shape)
    xc_ref[...] = cscr[:cols * rows].astype(BF).reshape(xc_ref.shape)
    xs_ref[...] = cscr[cols * rows:].astype(BF).reshape(xs_ref.shape)


def operands(offs, x, wl, wr, cols, start, total, bufs):
    count, n, c = x.shape
    half = c // 2
    wide = padded(2 * cols)
    g = GROUP
    at = start // g
    shapes = [
        ((half, count, n + wide), (half, g, n + wide), lambda b, o: (0, b, 0)),
        ((half, count, n + wide), (half, g, n + wide), lambda b, o: (0, b, 0)),
        ((total, n, c), (g, n, c), lambda b, o: (at + b, 0, 0)),
        ((total, wide, c), (g, wide, c), lambda b, o: (at + b, 0, 0)),
        ((cols, total, c), (cols, g, c), lambda b, o: (0, o[2 + b], 0)),
        ((cols, total, c), (cols, g, c), lambda b, o: (0, o[2 + b], 0)),
    ]
    full = lambda v: pl.BlockSpec(v.shape, lambda b, o: (0,) * v.ndim)
    ins = [x, wl, wr]
    specs = [pl.BlockSpec((g, n, c), lambda b, o: (b, 0, 0)), full(wl), full(wr)]
    alias = {}
    if bufs is not None:
        alias = {4 + i: 2 + i for i in range(4)}
        ins += list(bufs)
        specs += [pl.BlockSpec(memory_space=pl.ANY)] * 4
    got = pl.pallas_call(
        functools.partial(operand_kernel, cols),
        grid_spec=pltpu.PrefetchScalarGridSpec(
            num_scalar_prefetch=1,
            grid=(count // g,),
            in_specs=specs,
            out_specs=[pl.BlockSpec(b, m) for _, b, m in shapes],
            scratch_shapes=[
                pltpu.VMEM((n // 128, c * g, 128), F32),
                pltpu.VMEM((wide // 128, c * g, 128), F32),
                pltpu.VMEM((g, n, c), F32),
                pltpu.VMEM((g, n, c), F32),
                pltpu.VMEM((2 * cols * g, c), F32),
            ],
        ),
        out_shape=[jax.ShapeDtypeStruct(s, BF) for s, _, _ in shapes],
        input_output_aliases=alias,
        compiler_params=pltpu.CompilerParams(vmem_limit_bytes=60 << 20),
        cost_estimate=cost(3e9 * count, 8 * count * n * c),
        name="operands",
    )(offs, *ins)
    return got[0], got[1], got[2:]


def product_kernel(groups, *refs):
    mine_ref, theirs_ref, scr = refs[groups:]
    g = refs[0].shape[0]
    cols, _, n = mine_ref.shape
    for e in range(g):
        both = jnp.concatenate([r[e] for r in refs[:groups]], axis=0)
        part = lax.dot_general(
            both[:, n:], both[:, :n], (((0,), (0,)), ((), ())), preferred_element_type=F32
        )
        spread(scr, e, 2 * cols, g, part[: 2 * cols])
    mine_ref[...] = joined(scr, slice(0, cols * g)).astype(mine_ref.dtype).reshape(mine_ref.shape)
    theirs_ref[...] = joined(scr, slice(cols * g, None)).astype(theirs_ref.dtype).reshape(theirs_ref.shape)


def products(sets, cols, n):
    half, _, wide = sets[0].shape
    wide -= n
    g = GROUP
    out = jax.ShapeDtypeStruct((cols, half, n), BF)
    return pl.pallas_call(
        functools.partial(product_kernel, len(sets)),
        grid=(half // g,),
        in_specs=[pl.BlockSpec((g,) + v.shape[1:], lambda b: (b, 0, 0)) for v in sets],
        out_specs=[pl.BlockSpec((cols, g, n), lambda b: (0, b, 0))] * 2,
        out_shape=[out, out],
        scratch_shapes=[pltpu.VMEM((n // 128, 2 * cols * g, 128), F32)],
        compiler_params=pltpu.CompilerParams(vmem_limit_bytes=56 << 20),
        cost_estimate=cost(2 * half * n * n * wide, 4 * half * n * n),
        name="products",
    )(*sets)


def batch(count, most):
    return max(b for b in range(1, most + 1) if count % b == 0)


def product_rows(mine_ref, theirs_ref):
    return jnp.concatenate(
        [
            jnp.concatenate([mine_ref[b].astype(F32), theirs_ref[b].astype(F32)], axis=0).T
            for b in range(mine_ref.shape[0])
        ],
        axis=0,
    )


def after_kernel(heads, core_ref, xm_ref, xo_ref, mine_ref, theirs_ref, w4_ref, wout_ref, wb_ref, vec_ref,
                 after_ref, bias_ref, xc_ref, bscr):
    cb, n, c = xc_ref.shape
    first = core_ref[0] == 0
    span = core_ref.shape[0]
    parts = []
    for b in range(cb):
        near, far = xm_ref[b].astype(F32), xo_ref[b].astype(F32)
        low, high = jnp.where(first, near, far), jnp.where(first, far, near)
        for r in range(0, n // 2, span):
            parts += [low[r:r + span], high[r:r + span]]
    x = jnp.concatenate(parts, axis=0)
    xc_ref[...] = x.astype(BF).reshape(xc_ref.shape)
    n0, _ = norm(x)
    gate = sigm(nn(n0.astype(BF), w4_ref[...]))
    nc, _ = norm(product_rows(mine_ref, theirs_ref))
    lin = nn((nc * vec_ref[1:2, :]).astype(BF), wout_ref[...])
    after = x + (gate * lin).astype(BF).astype(F32)
    after_ref[...] = after.reshape(after_ref.shape)
    n3, _ = norm(after)
    bias = nt(wb_ref[...], (n3 * vec_ref[2:3, :]).astype(BF))
    for b in range(cb):
        for h in range(heads):
            at = pl.program_id(0) * cb + b
            bscr[pl.ds(at, 1), h * n:(h + 1) * n] = bias[h:h + 1, b * n:(b + 1) * n]

    @pl.when(pl.program_id(0) == pl.num_programs(0) - 1)
    def _():
        bias_ref[...] = bscr[...].astype(BF)


def afters(core, xm, xo, mine, theirs, w4, wout, wb, vec, heads):
    cols, rows, c = xm.shape
    n = 2 * rows
    half = mine.shape[1]
    cb = batch(cols, AFTER_BATCH)
    full = lambda v: pl.BlockSpec(v.shape, lambda b: (0,) * v.ndim)
    col = lambda a, b: pl.BlockSpec((cb, a, b), lambda j: (j, 0, 0))
    return pl.pallas_call(
        functools.partial(after_kernel, heads),
        grid=(cols // cb,),
        in_specs=[pl.BlockSpec(memory_space=pltpu.SMEM), col(rows, c), col(rows, c), col(half, n), col(half, n)]
        + [full(v) for v in (w4, wout, wb, vec)],
        out_specs=[col(n, c), pl.BlockSpec((cols, heads * n), lambda j: (0, 0)), col(n, c)],
        out_shape=[
            jax.ShapeDtypeStruct((cols, n, c), F32),
            jax.ShapeDtypeStruct((cols, heads * n), BF),
            jax.ShapeDtypeStruct((cols, n, c), BF),
        ],
        scratch_shapes=[pltpu.VMEM((cols, heads * n), F32)],
        compiler_params=pltpu.CompilerParams(vmem_limit_bytes=56 << 20),
        cost_estimate=cost(8 * cols * n * c * c, 10 * cols * n * c, cols * n * c),
        name="afters",
    )(core, xm, xo, mine, theirs, w4, wout, wb, vec)


def back_kernel(after_ref, gx_ref, gmid_ref, gb_ref, xc_ref, mine_ref, theirs_ref, w4_ref, wout_ref, wb_ref, vec_ref,
                gmine_ref, gtheirs_ref, gwb_ref, gwout_ref, gw4_ref, small_ref):
    @pl.when(pl.program_id(0) == 0)
    def _():
        for ref in (gwb_ref, gwout_ref, gw4_ref, small_ref):
            ref[...] = jnp.zeros_like(ref)

    cb, n, c = xc_ref.shape
    half = mine_ref.shape[1]
    heads = gb_ref.shape[2]
    flat = lambda ref: ref[...].reshape(cb * n, c)
    g1 = vec_ref[1:2, :]
    g2 = vec_ref[2:3, :]
    n3, s3 = norm(flat(after_ref))
    x3 = (n3 * g2).astype(BF)
    parts = []
    for b in range(cb):
        gb = gb_ref[0, b].astype(F32)
        for d in range(1, gb_ref.shape[0]):
            gb = gb + gb_ref[d, b].astype(F32)
        parts.append(jnp.concatenate([gb, jnp.zeros((wb_ref.shape[0] - heads, n), F32)], axis=0))
    gb = jnp.concatenate(parts, axis=1)
    gwb_ref[...] += nn(gb.astype(BF), x3)
    gx = (flat(gx_ref) + nn(gb.T.astype(BF), wb_ref[...])).astype(BF).astype(F32)
    small_ref[0:1, :] += jnp.sum(gx * n3, axis=0, keepdims=True)
    gafter = (flat(gmid_ref) + norm_back(gx, g2, n3, s3)).astype(BF).astype(F32)

    n0, _ = norm(flat(xc_ref).astype(F32))
    n0 = n0.astype(BF)
    gate = sigm(nn(n0, w4_ref[...]))
    nc, sc = norm(product_rows(mine_ref, theirs_ref))
    centre = (nc * g1).astype(BF)
    lin = nn(centre, wout_ref[...])
    glin = (gafter * gate).astype(BF)
    gp4 = (gafter * lin * gate * (1.0 - gate)).astype(BF)
    gwout_ref[...] += nn(centre.astype(F32).T.astype(BF), glin)
    gw4_ref[...] += nn(n0.astype(F32).T.astype(BF), gp4)
    gc = nt(glin, wout_ref[...]).astype(BF).astype(F32)
    small_ref[1:2, :] += jnp.sum(gc * nc, axis=0, keepdims=True)
    gprod = norm_back(gc, g1, nc, sc)
    for b in range(cb):
        part = gprod[b * n:(b + 1) * n].T.astype(BF)
        gmine_ref[b] = part[:half]
        gtheirs_ref[b] = part[half:]


def back_pass(after, gx, gmid, gb, xc, mine, theirs, w4, wout, wb, vec):
    cols, n, c = xc.shape
    half = mine.shape[1]
    heads = gb.shape[2]
    cb = batch(cols, BACK_BATCH)
    full = lambda shape: pl.BlockSpec(shape, lambda b: (0,) * len(shape))
    col = lambda a, b: pl.BlockSpec((cb, a, b), lambda j: (j, 0, 0))
    accs = [wb.shape, (c, c), (c, c), (8, c)]
    return pl.pallas_call(
        back_kernel,
        grid=(cols // cb,),
        in_specs=[col(n, c)] * 3
        + [pl.BlockSpec((gb.shape[0], cb, heads, n), lambda j: (0, j, 0, 0)), col(n, c), col(half, n), col(half, n)]
        + [full(v.shape) for v in (w4, wout, wb, vec)],
        out_specs=[col(half, n)] * 2 + [full(s) for s in accs],
        out_shape=[jax.ShapeDtypeStruct((cols, half, n), BF)] * 2 + [jax.ShapeDtypeStruct(s, F32) for s in accs],
        compiler_params=pltpu.CompilerParams(vmem_limit_bytes=56 << 20),
        cost_estimate=cost(16 * cols * n * c * c, 24 * cols * n * c, cols * n * c),
        name="back",
    )(after, gx, gmid, gb, xc, mine, theirs, w4, wout, wb, vec)


def operand_grads_kernel(groups, *refs):
    sets = [refs[:groups], refs[groups:2 * groups]]
    gm_ref, gt_ref, keep_ref, send_ref, scr, lscr, rscr = refs[2 * groups:]
    cols, g, n = gm_ref.shape
    rows = keep_ref.shape[0]
    wide = keep_ref.shape[2] - n
    gm = gm_ref[...].astype(F32).reshape(cols * g, n)
    gt = gt_ref[...].astype(F32).reshape(cols * g, n)
    for t in range(n // 128):
        scr[t, : cols * g] = gm[:, t * 128 : (t + 1) * 128]
        scr[t, cols * g :] = gt[:, t * 128 : (t + 1) * 128]
    blank = [jnp.zeros((wide - 2 * cols, n), F32)] if wide > 2 * cols else []
    fetch = lambda at: jnp.concatenate([scr[t, pl.ds(at, cols, stride=g), :] for t in range(n // 128)], axis=1)
    for part, out_ref in enumerate((keep_ref, send_ref)):
        for e in range(g):
            pieces = [fetch(e), fetch(cols * g + e)]
            gp = jnp.concatenate(pieces + blank, axis=0).astype(BF)
            seen = gp if part == 0 else jnp.concatenate(pieces[::-1] + blank, axis=0).astype(BF)
            both = jnp.concatenate([r[e] for r in sets[part]], axis=0)
            spread(rscr, e, rows, g, nt(both[:, :n], seen))
            spread(lscr, e, rows, g, nn(both[:, n:], gp))
        both = jnp.concatenate([joined(lscr), joined(rscr)], axis=1)
        out_ref[...] = both.astype(BF).reshape(out_ref.shape)


def operand_grads(keep, recv, gmine, gtheirs):
    half, _, lanes = keep[0].shape
    rows = sum(v.shape[1] for v in keep)
    cols, _, n = gmine.shape
    wide = lanes - n
    g = GROUP
    out = jax.ShapeDtypeStruct((rows, half, lanes), BF)
    return pl.pallas_call(
        functools.partial(operand_grads_kernel, len(keep)),
        grid=(half // g,),
        in_specs=[pl.BlockSpec((g,) + v.shape[1:], lambda b: (b, 0, 0)) for v in keep + recv]
        + [pl.BlockSpec((cols, g, n), lambda b: (0, b, 0))] * 2,
        out_specs=[pl.BlockSpec((rows, g, lanes), lambda b: (0, b, 0))] * 2,
        out_shape=[out, out],
        scratch_shapes=[
            pltpu.VMEM((n // 128, 2 * cols * g, 128), F32),
            pltpu.VMEM((n // 128, rows * g, 128), F32),
            pltpu.VMEM((wide // 128, rows * g, 128), F32),
        ],
        compiler_params=pltpu.CompilerParams(vmem_limit_bytes=60 << 20),
        cost_estimate=cost(4 * half * n * n * wide, 8 * half * n * n),
        name="operand_grads",
    )(*keep, *recv, gmine, gtheirs)


def tri_grads_kernel(n_ref, nc_ref, g_ref, wl_ref, wr_ref, al_ref, ar_ref, lg, rg):
    @pl.when(pl.program_id(0) == 0)
    def _():
        al_ref[...] = jnp.zeros_like(al_ref)
        ar_ref[...] = jnp.zeros_like(ar_ref)
    rows, n, c = n_ref.shape
    wide = nc_ref.shape[1]
    half = g_ref.shape[1]
    def one(low, grad, w):
        p = nt(w, low)
        s = sigm(p[half:])
        first = grad.astype(F32) * s
        return first.astype(BF), (first * p[:half] * (1.0 - s)).astype(BF)
    for k in range(rows):
        a, b = one(n_ref[k], g_ref[k, :, :n], wl_ref[...])
        lg[:half, k*n:(k+1)*n] = a
        lg[half:, k*n:(k+1)*n] = b
        a, b = one(nc_ref[k], g_ref[k, :, n:], wr_ref[...])
        rg[:half, k*wide:(k+1)*wide] = a
        rg[half:, k*wide:(k+1)*wide] = b
    al_ref[...] += nn(lg[...], n_ref[...].reshape(rows*n, c))
    ar_ref[...] += nn(rg[...], nc_ref[...].reshape(rows*wide, c))


def tri_grads(nrm, near, grad, wl, wr):
    count, n, c = nrm.shape
    half = grad.shape[1]
    wide = near.shape[1]
    rows = batch(count, 24)
    full = lambda v: pl.BlockSpec(v.shape, lambda b: (0,) * v.ndim)
    row = lambda a, b: pl.BlockSpec((rows, a, b), lambda k: (k, 0, 0))
    out = jax.ShapeDtypeStruct((2 * half, c), F32)
    return pl.pallas_call(
        tri_grads_kernel,
        grid=(count // rows,),
        in_specs=[row(n, c), row(wide, c), row(half, n + wide), full(wl), full(wr)],
        out_specs=[pl.BlockSpec(out.shape, lambda k: (0, 0))] * 2,
        out_shape=[out] * 2,
        scratch_shapes=[pltpu.VMEM((2*half, rows*n), BF), pltpu.VMEM((2*half, rows*wide), BF)],
        compiler_params=pltpu.CompilerParams(vmem_limit_bytes=56 << 20),
        cost_estimate=cost(8 * count * n * c * c, 8 * count * n * c, count * n * half),
        name="tri_grads",
    )(nrm, near, grad, wl, wr)


def adam_kernel(scale_ref, sum_ref, shrink_ref, bias_ref, vec_ref, *refs):
    masters, firsts, seconds = refs[:8], refs[8:16], refs[16:24]
    new_masters, new_firsts, new_seconds = refs[24:32], refs[32:40], refs[40:]
    at = [0]

    def take(ref):
        at[0] += ref.shape[-1]
        return sum_ref[:, at[0] - ref.shape[-1] : at[0]]

    grads = {slot: take(masters[slot]) for slot in (2, 4, 5, 1, 0)}
    grads.update({3: bias_ref[...], 6: shrink_ref[...], 7: vec_ref[...]})
    for slot in range(8):
        whole = (lambda ref: ref[...]) if slot == 7 else (lambda ref: ref[0])
        clipped = grads[slot] * scale_ref[0]
        master = whole(masters[slot])
        moment = beta_first * whole(firsts[slot]) + (1 - beta_first) * clipped
        square = beta_second * whole(seconds[slot]) + (1 - beta_second) * clipped * clipped
        stride = (
            moment
            / (1 - beta_first**STEP)
            / (jnp.sqrt(square / (1 - beta_second**STEP)) + adam_epsilon)
        )
        rate = vector_rate if slot == 7 else learn_rate
        fresh = (master - rate * (stride + weight_decay * master), moment, square)
        for refs_out, value in zip((new_masters, new_firsts, new_seconds), fresh):
            if slot == 7:
                refs_out[slot][...] = value
            else:
                refs_out[slot][0] = value


def adam(scale, total, shrink, bias, vec, masters, firsts, seconds):
    ins = [total, shrink, bias, vec, *masters, *firsts, *seconds]
    vmem = pl.BlockSpec(memory_space=pltpu.VMEM)
    return pl.pallas_call(
        adam_kernel,
        in_specs=[pl.BlockSpec(memory_space=pltpu.SMEM)] + [vmem] * len(ins),
        out_specs=[vmem] * 24,
        out_shape=[jax.ShapeDtypeStruct(v.shape, F32) for v in [*masters, *firsts, *seconds]],
        compiler_params=pltpu.CompilerParams(vmem_limit_bytes=40 << 20),
        name="adam",
    )(scale, *ins)


def gather_weights(tri, tri_out, attn, bias, outp, expand, shrink, vectors):
    rows = tri.shape[1]
    pieces = [tri[0], tri_out[0], attn[0], outp[0], expand[0], shrink[0].reshape(rows, -1), bias[0], vectors.T]
    widths = [p.shape[1] for p in pieces]
    packed = jnp.concatenate(all_item(jnp.concatenate([p.astype(BF) for p in pieces], axis=1)))
    got, at = [], 0
    for w in widths:
        got.append(packed[:, at : at + w])
        at += w
    tri, tri_out, attn, outp, expand, shr, bias, vec = got
    return tri, tri_out, attn, bias, outp, expand, shr.reshape(-1, shrink.shape[2]), vec.T


def project_rows(rows, project, size, first):
    here = lax.axis_index("pair")
    count = rows.shape[0]
    if size != 8 or count % 48:
        sets = [list(range(c, size, 2)) for c in range(2)]
        got = lax.all_gather(rows, "pair", axis=0, tiled=True, axis_index_groups=sets)
        return [project(got, list(range(got.shape[0] // GROUP)))], first
    stages = 3
    step = count // stages
    per = step // GROUP
    x = [rows[s * step : (s + 1) * step] for s in range(stages)] + [None]
    spot = lambda device, s: [device // 2 * (stages * per) + s * per + u for u in range(per)]
    send = lambda value: [exchange(value, "pair", 2), exchange(value, "pair", 4)]
    near, late = send(x[0]), []
    done = [project(rows, [p for s in range(stages) for p in spot(here, s)])]
    for s in range(stages):
        waits = [x[s + 1], near, late, done[-1][0]]
        if s == 1:
            waits.append(first)
        if s:
            waits.append(done[-2][1])
        held = lax.optimization_barrier(tuple(waits))
        following, near, arrived, done[-1][0] = held[:4]
        if s == 1:
            first = held[4]
        if s:
            done[-2][1] = held[-1]
        late = [exchange(near[0][: step // 2], "pair", 4), exchange(near[1][step // 2 :], "pair", 2)]
        places = spot(here ^ 2, s) + spot(here ^ 4, s) + (spot(here ^ 6, s - 1) if arrived else [])
        group = jnp.concatenate(near + arrived)
        if s + 1 < stages:
            near = send(following)
        done.append(project(group, places))
    late, done[-1][0], done[-2][1] = lax.optimization_barrier((late, done[-1][0], done[-2][1]))
    done.append(project(jnp.concatenate(late), spot(here ^ 6, stages - 1)))
    return done, first


def swap_cores(value):
    size = lax.axis_size("pair")
    return lax.ppermute(value, "pair", [(d, d ^ 1) for d in range(size)])


def exchange(value, axis, bit):
    size = lax.axis_size(axis)
    return lax.ppermute(value, axis, [(d, d ^ bit) for d in range(size)])


def sum_axis(value, axis):
    bit = 1
    while bit < lax.axis_size(axis):
        value = value + exchange(value, axis, bit)
        bit *= 2
    return value


def sum_item(part, beside=()):
    bit = lax.axis_size("item") // 2
    here = lax.axis_index("item")
    beside = list(beside)
    while bit:
        upper = (here // bit) % 2
        rows = part.shape[0] // 2
        kept = lax.dynamic_slice_in_dim(part, upper * rows, rows, 0)
        sent = lax.dynamic_slice_in_dim(part, (1 - upper) * rows, rows, 0)
        got = exchange(sent.astype(BF), "item", bit)
        if beside:
            work = beside.pop(0)
            got, work[0] = lax.optimization_barrier((got, work[0]))
        part = kept + got.astype(F32)
        bit //= 2
    return part


def all_item(value):
    size = lax.axis_size("item")
    here = lax.axis_index("item")
    got = jnp.stack([value] + [exchange(value, "item", bit) for bit in range(1, size)])
    return [lax.dynamic_index_in_dim(got, here ^ t, 0, keepdims=False) for t in range(size)]


def on_device(
    pair_act,
    targets,
    pair_mask,
    tri_proj,
    tri_out,
    attention_proj,
    bias_proj,
    output_proj,
    expand_proj,
    shrink_proj,
    vectors,
    first_tri,
    first_tri_out,
    first_attention,
    first_bias,
    first_output,
    first_expand,
    first_shrink,
    first_vectors,
    second_tri,
    second_tri_out,
    second_attention,
    second_bias,
    second_output,
    second_expand,
    second_shrink,
    second_vectors,
):
    layers = attention_proj.shape[0]
    assert layers == 1
    cols, tokens, width = pair_act.shape[1:]
    half = width // 2
    heads = bias_proj.shape[2]
    here = lax.axis_index("pair")
    core = here % 2
    weight = gather_weights(
        tri_proj, tri_out, attention_proj, bias_proj, output_proj, expand_proj, shrink_proj, vectors
    )
    tri_w, tri_out_w, project_w, pairbias_w, output_w, expand_w, shrink_w, vector_low = weight
    vec = vector_low.astype(F32)
    weighting_rows = pair_mask.astype(F32)
    both = lax.all_gather(
        jnp.concatenate([targets, weighting_rows]), "pair", axis=1, tiled=True
    )
    both = lax.dynamic_slice_in_dim(both, here * cols, cols, 2)

    scaled = (tri_w.astype(F32) * vec[0][:, None]).astype(BF).T
    tri_half = lambda s, c: lax.dynamic_slice_in_dim(scaled, width * s + half * c, half, 0)
    near_w = [tri_half(s, core) for s in range(4)]
    far_w = [tri_half(s, 1 - core) for s in range(4)]
    w_left = jnp.concatenate([near_w[0], far_w[0], near_w[1], far_w[1]])
    w_right = jnp.concatenate([near_w[2], near_w[3], far_w[2], far_w[3]])
    w_gate = scaled[4 * width :].T
    wout = jnp.roll(tri_out_w, -half * core, axis=0)
    gain_c = jnp.roll(vec[1], -half * core)
    vec8 = jnp.concatenate([vec[:1], gain_c[None], vec[2:], jnp.zeros((3, width), F32)])
    wb = jnp.concatenate([pairbias_w.T, jnp.zeros((16 - heads, width), BF)])

    state = {"bufs": None, "start": 0}

    def project(rows, places):
        offs = jnp.stack([here * cols, (here + 1 - 2 * core) * cols, *places]).astype(jnp.int32)
        mine, sent, state["bufs"] = operands(
            offs, rows, w_left, w_right, cols, state["start"], tokens // 2, state["bufs"]
        )
        state["start"] += rows.shape[0]
        return [mine, swap_cores(sent)]

    done, both = project_rows(pair_act[0], project, lax.axis_size("pair"), both)
    keep, recv = [v[0] for v in done], [v[1] for v in done]
    bufs = state["bufs"]
    nrm, near, xm, xs = bufs
    xo = swap_cores(xs)
    mine, send = products(keep + recv, cols, tokens)
    theirs = swap_cores(send)
    cores = jnp.full((cols,), core, jnp.int32)
    after_c, bias_part, xc = afters(cores, xm, xo, mine, theirs, w_gate, wout, wb, vec8, heads)
    bias_full = lax.all_gather(bias_part, "pair", axis=0, tiled=True)
    hidden = expand_w.shape[1] // 2
    z = jnp.sum(shrink_w.astype(F32) * vec[4], axis=1)[None]
    gx, gmid, gb, gkv_w, gqg_w, gow, gew, svec, small = column_pass(
        after_c, both[0], both[1], bias_full, project_w, project_w.T, output_w, expand_w, vec8, z
    )
    bias_cols = lax.all_to_all(gb, "pair", split_axis=0, concat_axis=0, tiled=True)
    gmine, gsend, gwb, gwout, gw4, small2 = back_pass(
        after_c, gx, gmid, bias_cols.reshape(-1, cols, heads, tokens), xc, mine, theirs,
        w_gate, wout, wb, vec8,
    )
    early = jnp.concatenate(
            [
                gqg_w[:width].T,
                gkv_w,
                gqg_w[width:].T,
                gow,
                gew,
                jnp.roll(gwout, half * core, axis=0),
                gw4 * vec[0][:, None],
                gwb[:heads].T,
                jnp.roll(small2[1], half * core)[:, None],
                small2[0][:, None],
                small[1][:, None],
                (small[0] + jnp.sum(svec[0][:, None] * shrink_w.astype(F32), axis=0))[:, None],
                svec.reshape(width, -1),
            ],
            axis=1,
        )
    gtheirs = swap_cores(gsend)
    grad_keep, grad_sent = operand_grads(keep, recv, gmine, gtheirs)
    grad_far = swap_cores(grad_sent)
    w_l = [jnp.concatenate([w[0], w[1]]) for w in (near_w, far_w)]
    w_r = [jnp.concatenate([w[2], w[3]]) for w in (near_w, far_w)]
    near_a = list(tri_grads(nrm, near, grad_keep, w_l[0], w_r[0]))
    far_a = list(tri_grads(nrm, near, grad_far, w_l[1], w_r[1]))
    early = sum_item(early, (near_a, far_a))
    a_tri = []
    for near_part, far_part in zip(near_a, far_a):
        for s in range(2):
            parts = [p[s * half : (s + 1) * half] for p in (near_part, far_part)]
            a_tri += [jnp.where(core == 0, parts[0], parts[1]), jnp.where(core == 0, parts[1], parts[0])]
    a_tri = jnp.concatenate(a_tri + [gw4.T]).T
    g_gain = jnp.sum(a_tri * tri_w.astype(F32), axis=1)[:, None]
    late = sum_item(jnp.concatenate([a_tri[:, : 4 * width] * vec[0][:, None], g_gain], axis=1))
    cut = 8 * width + 2 * hidden - width
    joint = sum_axis(
        jnp.concatenate(
            [
                early[:, : cut - width],
                late[:, : 4 * width],
                early[:, cut - width :],
                late[:, 4 * width :],
                jnp.pad(jnp.stack([jnp.sum(small[2]), jnp.sum(weighting_rows)]), (0, late.shape[0] - 2))[:, None],
            ],
            axis=1,
        ),
        "pair",
    )
    total = joint[:, : cut + 4 * width]
    rest = joint[:, cut + 4 * width :]
    g_bias, g_vec, g_svec = rest[:, :heads], rest[:, heads : heads + 4], rest[:, heads + 4 : -2]
    g_gain = rest[:, -2:-1]
    g_vec = jnp.concatenate([g_gain, g_vec], axis=1).T
    g_shrink = g_svec.reshape(-1, 1) * vec[4][None, :]
    squares = (
        jnp.sum(total * total)
        + jnp.sum(g_bias * g_bias)
        + jnp.sum(g_vec * g_vec)
        + jnp.sum(g_svec * g_svec) * jnp.sum(vec[4] * vec[4])
    )
    sums = sum(all_item(jnp.stack([squares, rest[0, -1], rest[1, -1]])))
    loss_sum, count = sums[1], sums[2]
    grad_norm = jnp.sqrt(sums[0]) / count
    factor = jnp.minimum(1.0, clip_limit / (grad_norm + 1e-06))
    masters = (
        tri_proj,
        tri_out,
        attention_proj,
        bias_proj,
        output_proj,
        expand_proj,
        shrink_proj,
        vectors,
    )
    firsts = (
        first_tri,
        first_tri_out,
        first_attention,
        first_bias,
        first_output,
        first_expand,
        first_shrink,
        first_vectors,
    )
    seconds = (
        second_tri,
        second_tri_out,
        second_attention,
        second_bias,
        second_output,
        second_expand,
        second_shrink,
        second_vectors,
    )
    outs = adam(
        (factor / count)[None], total, g_shrink, g_bias, g_vec, masters, firsts, seconds
    )
    return (loss_sum, count, grad_norm) + tuple(outs)


def solution(mesh):
    in_specs = (
        P("item", "pair", None, None),
        P("item", "pair", None),
        P("item", "pair", None),
        P(None, "item", None),
        P(None, "item", None),
        P(None, "item", None),
        P(None, "item", None),
        P(None, "item", None),
        P(None, "item", None),
        P(None, "item", None),
        P(None, "item"),
        P(None, "item", None),
        P(None, "item", None),
        P(None, "item", None),
        P(None, "item", None),
        P(None, "item", None),
        P(None, "item", None),
        P(None, "item", None),
        P(None, "item"),
        P(None, "item", None),
        P(None, "item", None),
        P(None, "item", None),
        P(None, "item", None),
        P(None, "item", None),
        P(None, "item", None),
        P(None, "item", None),
        P(None, "item"),
    )
    out_specs = (
        P(),
        P(),
        P(),
        P(None, "item", None),
        P(None, "item", None),
        P(None, "item", None),
        P(None, "item", None),
        P(None, "item", None),
        P(None, "item", None),
        P(None, "item", None),
        P(None, "item"),
        P(None, "item", None),
        P(None, "item", None),
        P(None, "item", None),
        P(None, "item", None),
        P(None, "item", None),
        P(None, "item", None),
        P(None, "item", None),
        P(None, "item"),
        P(None, "item", None),
        P(None, "item", None),
        P(None, "item", None),
        P(None, "item", None),
        P(None, "item", None),
        P(None, "item", None),
        P(None, "item", None),
        P(None, "item"),
    )
    return jax.shard_map(
        on_device, mesh=mesh, in_specs=in_specs, out_specs=out_specs, check_vma=False
    )
```

```python
import functools

import jax
import jax.numpy as jnp
from jax import lax
from jax.experimental import pallas as pl
from jax.experimental.pallas import tpu as pltpu
from jax.sharding import PartitionSpec as P

STEP = 10

norm_epsilon = 1e-05
clip_limit = 0.001
learn_rate = 0.1
vector_rate = 0.8
beta_first = 0.9
beta_second = 0.999
adam_epsilon = 1e-08
weight_decay = 0.01

BF = jnp.bfloat16
F32 = jnp.float32
LOG2E = 1.4426950408889634
EPS = norm_epsilon


def cost(flops, moved, exps=0):
    return pl.CostEstimate(flops=int(flops), bytes_accessed=int(moved), transcendentals=int(exps))


def nn(a, b):
    return lax.dot_general(a, b, (((1,), (0,)), ((), ())), preferred_element_type=F32)

def nt(a, b):
    return lax.dot_general(a, b, (((1,), (1,)), ((), ())), preferred_element_type=F32)

def sigm(v):
    return 0.5 * jnp.tanh(0.5 * v) + 0.5

def norm(v):
    mean = jnp.mean(v, axis=-1, keepdims=True)
    cen = v - mean
    scale = lax.rsqrt(jnp.mean(cen * cen, axis=-1, keepdims=True) + EPS)
    return cen * scale, scale

def norm_back(up, gain, n, scale):
    inner = up * gain
    return scale * (inner - jnp.mean(inner, axis=-1, keepdims=True) - n * jnp.mean(inner * n, axis=-1, keepdims=True))

def chunks(total, width):
    return [(s, min(width, total - s)) for s in range(0, total, width)]

def column_kernel(heads, after_ref, tgt_ref, msk_ref, bias_ref, w_ref, wt_ref, wo_ref, we_ref, vec_ref, z_ref,
                gx_ref, gmid_ref, gb_ref, gkvw_ref, gqgw_ref, gow_ref, gew_ref, svec_ref, small_ref,
                bias2, e_s, gs_s, acc, qbd, gobd, vaug, qn, gon, ores, cu, hv):
    step = pl.program_id(0)
    last = pl.num_programs(0) - 1
    cb, n, c = after_ref.shape
    dh = c // heads
    wide = heads * n
    scale = dh ** -0.5
    every = range(cb)
    pairs = [(b, h) for b in every for h in range(heads)]
    lanes = lambda b, h: slice(b * wide + h * n, b * wide + (h + 1) * n)
    rows = lambda b: slice(b * n, (b + 1) * n)
    chans = lambda h: slice(h * dh, (h + 1) * dh)

    @pl.when(step == 0)
    def _():
        for h in range(heads):
            bias2[:, h * n:(h + 1) * n] = bias_ref[:, h * n:(h + 1) * n].astype(F32).T * LOG2E
        acc[...] = jnp.zeros_like(acc)
        qbd[...] = jnp.zeros_like(qbd)
        gobd[...] = jnp.zeros_like(gobd)
        first = lax.broadcasted_iota(jnp.int32, (cb * n, c), 1)
        vaug[:, c:] = jnp.where(first < 3, 1.0, 0.0).astype(BF)
        for ref in (gkvw_ref, gqgw_ref, gow_ref, gew_ref, svec_ref, small_ref):
            ref[...] = jnp.zeros_like(ref)

    lane = lax.broadcasted_iota(jnp.int32, (n, c), 1)
    g3 = vec_ref[2:3, :]
    g4 = vec_ref[3:4, :]
    wr = vec_ref[4:5, :]
    after = after_ref[...].reshape(cb * n, c)
    n3, _ = norm(after)
    x = (n3 * g3).astype(BF)
    nat = nn(x, w_ref[:, :3 * c])
    k_nat = nat[:, c:2 * c].astype(BF)
    vaug[:, :c] = nat[:, 2 * c:].astype(BF)
    q_nat = (nat[:, :c] * (scale * LOG2E)).astype(BF)
    tr = nt(wt_ref[...], x)
    q_t = (tr[:c] * (scale * LOG2E)).astype(BF)
    k_t = tr[c:2 * c].astype(BF)
    v_t = jnp.concatenate([tr[2 * c:3 * c], jnp.ones((16, cb * n), F32)], axis=0).astype(BF)
    gate_t = sigm(tr[3 * c:])
    for b, h in pairs:
        qbd[chans(h), lanes(b, h)] = q_t[chans(h), rows(b)]
        qn[lanes(b, h), :] = jnp.where((lane >= h * dh) & (lane < (h + 1) * dh), q_nat[rows(b)], jnp.zeros((n, c), BF))

    for s0, w0 in chunks(wide, wide):
        for b in every:
            sl = slice(b * wide + s0, b * wide + s0 + w0)
            sc = nn(k_nat[rows(b)], qbd[:, sl]) + bias2[:, s0:s0 + w0]
            top = jnp.max(sc, axis=0, keepdims=True)
            ex = jnp.exp2(sc - top).astype(BF)
            e_s[:, sl] = ex
            ores[:, sl] = nn(v_t[:, rows(b)], ex)
    r_of = {p: 1.0 / ores[c:c + 1, lanes(*p)] for p in pairs}
    o_of = {p: ores[chans(p[1]), lanes(*p)] * r_of[p] for p in pairs}
    o_t = jnp.concatenate([jnp.concatenate([o_of[b, h] for h in range(heads)], axis=0) for b in every], axis=1)
    y_t = (gate_t * o_t).astype(BF)
    out = nn(y_t.astype(F32).T.astype(BF), wo_ref[...]).astype(BF)
    mid = after + out.astype(F32)

    n4, sc4 = norm(mid)
    t = (n4 * g4).astype(BF)
    f = we_ref.shape[1] // 2
    racc = mid * wr
    u = nn(t, we_ref[...])
    a, b = u[:, :f], u[:, f:]
    sig = sigm(a)
    silu = a * sig
    h_low = (silu * b).astype(BF)
    hv[...] = h_low
    part = h_low.astype(F32) * z_ref[...]
    for q in range(f // c):
        racc += part[:, q * c:(q + 1) * c]
    cu[:, :f] = (z_ref[...] * b * (sig + silu - silu * sig)).astype(BF)
    cu[:, f:] = (z_ref[...] * silu).astype(BF)
    readout = jnp.sum(racc, axis=-1, keepdims=True)
    spot = lax.broadcasted_iota(jnp.int32, tgt_ref.shape, 1)
    pick = lambda ref: jnp.concatenate(
        [jnp.sum(jnp.where(spot == step * cb + b, ref[...], 0.0), axis=1, keepdims=True) for b in every], axis=0)
    err = readout - pick(tgt_ref)
    wer = pick(msk_ref) * err
    gr = 2.0 * wer
    small_ref[0:1, :] += jnp.sum(gr * mid, axis=0, keepdims=True)
    first = lax.broadcasted_iota(jnp.int32, (cb * n, c), 1)
    small_ref[2:3, :] += jnp.sum(jnp.where(first == 0, wer * err, 0.0), axis=0, keepdims=True)
    svec_ref[...] += jnp.sum(gr * hv[...].astype(F32), axis=0, keepdims=True)
    gew_ref[...] += nn((gr * t.astype(F32)).T.astype(BF), cu[...])
    gt = gr * nt(cu[...], we_ref[...])
    small_ref[1:2, :] += jnp.sum(gt * n4, axis=0, keepdims=True)
    gmid = gr * wr + norm_back(gt, g4, n4, sc4)
    gmid_ref[...] = gmid.reshape(gmid_ref.shape)

    gout = gmid.astype(BF)
    gow_ref[...] += nn(y_t, gout)
    gy_t = nt(wo_ref[...], gout)
    ggl_t = gy_t * o_t * gate_t * (1.0 - gate_t)
    go_t = (gy_t * gate_t).astype(BF).astype(F32)
    row = lax.broadcasted_iota(jnp.int32, (16, n), 0)
    gos = {}
    for b, h in pairs:
        part = (go_t[chans(h), rows(b)] * r_of[b, h]).astype(BF)
        gobd[chans(h), lanes(b, h)] = part
        part = part.astype(F32)
        gos[b, h] = part
        d = -jnp.sum(part * o_of[b, h], axis=0, keepdims=True)
        hi = d.astype(BF).astype(F32)
        mi = (d - hi).astype(BF).astype(F32)
        lo = d - hi - mi
        gobd[c:, lanes(b, h)] = jnp.where(row == 0, hi, jnp.where(row == 1, mi, jnp.where(row == 2, lo, 0.0))).astype(BF)
    go_n = jnp.concatenate([jnp.concatenate([gos[b, h] for h in range(heads)], axis=0) for b in every], axis=1).T.astype(BF)
    for b, h in pairs:
        gon[lanes(b, h), :] = jnp.where((lane >= h * dh) & (lane < (h + 1) * dh), go_n[rows(b)], jnp.zeros((n, c), BF))

    for s0, w0 in chunks(wide, wide):
        total = acc[:, s0:s0 + w0]
        for b in every:
            sl = slice(b * wide + s0, b * wide + s0 + w0)
            g = e_s[:, sl].astype(F32) * nn(vaug[rows(b), :c + 16], gobd[:, sl])
            total += g
            gl = g.astype(BF)
            gs_s[:, sl] = gl
            ores[:c, sl] = nn(k_t[:, rows(b)], gl)
        acc[:, s0:s0 + w0] = total
    gq_t = jnp.concatenate(
        [jnp.concatenate([ores[chans(h), lanes(b, h)] for h in range(heads)], axis=0) for b in every], axis=1) * scale
    gqg_t = jnp.concatenate([gq_t, ggl_t], axis=0).astype(BF)
    gk = [nn(gs_s[:, b * wide:(b + 1) * wide], qn[b * wide:(b + 1) * wide, :]) * (1.0 / LOG2E) for b in every]
    gv = [nn(e_s[:, b * wide:(b + 1) * wide], gon[b * wide:(b + 1) * wide, :]) for b in every]
    gkv = jnp.concatenate([jnp.concatenate([gk[b], gv[b]], axis=1) for b in every], axis=0).astype(BF)
    gqgw_ref[...] += nn(gqg_t, x)
    gkvw_ref[...] += nn(x.astype(F32).T.astype(BF), gkv)
    w_qg = jnp.concatenate([w_ref[:, :c], w_ref[:, 3 * c:]], axis=1)
    gx_ref[...] = (nt(gkv, w_ref[:, c:3 * c]) + nn(w_qg, gqg_t).T).reshape(gx_ref.shape)

    @pl.when(step == last)
    def _():
        for h in range(heads):
            gb_ref[:, h * n:(h + 1) * n] = acc[:, h * n:(h + 1) * n].T.astype(gb_ref.dtype)


def column_pass(after, tgt, msk, bias, w, wt, wo, we, vec, z):
    cols, n, c = after.shape
    heads = bias.shape[1] // n
    f = we.shape[1] // 2
    wide = heads * n
    cb = batch(cols, 3)
    full = lambda shape: pl.BlockSpec(shape, lambda j: (0,) * len(shape))
    col = pl.BlockSpec((cb, n, c), lambda j: (j, 0, 0))
    outs = [
        jax.ShapeDtypeStruct((cols, n, c), F32),
        jax.ShapeDtypeStruct((cols, n, c), F32),
        jax.ShapeDtypeStruct((n, wide), BF),
        jax.ShapeDtypeStruct((c, 2 * c), F32),
        jax.ShapeDtypeStruct((2 * c, c), F32),
        jax.ShapeDtypeStruct((c, c), F32),
        jax.ShapeDtypeStruct((c, 2 * f), F32),
        jax.ShapeDtypeStruct((1, f), F32),
        jax.ShapeDtypeStruct((8, c), F32),
    ]
    return pl.pallas_call(
        functools.partial(column_kernel, heads),
        grid=(cols // cb,),
        in_specs=[col] + [full(v.shape) for v in (tgt, msk, bias, w, wt, wo, we, vec, z)],
        out_specs=[col, col] + [full(o.shape) for o in outs[2:]],
        out_shape=outs,
        scratch_shapes=[
            pltpu.VMEM((n, wide), F32),
            pltpu.VMEM((n, cb * wide), BF),
            pltpu.VMEM((n, cb * wide), BF),
            pltpu.VMEM((n, wide), F32),
            pltpu.VMEM((c, cb * wide), BF),
            pltpu.VMEM((c + 16, cb * wide), BF),
            pltpu.VMEM((cb * n, 2 * c), BF),
            pltpu.VMEM((cb * wide, c), BF),
            pltpu.VMEM((cb * wide, c), BF),
            pltpu.VMEM((c + 16, cb * wide), F32),
            pltpu.VMEM((cb * n, 2 * f), BF),
            pltpu.VMEM((cb * n, f), BF),
        ],
        compiler_params=pltpu.CompilerParams(vmem_limit_bytes=56 << 20),
        cost_estimate=cost(12 * cols * heads * n * n * 128, 16 * cols * n * c, cols * heads * n * n),
        name="columns",
    )(after, tgt, msk, bias, w, wt, wo, we, vec, z)


GROUP = 16
AFTER_BATCH = 6
BACK_BATCH = 6


def spread(scr, start, count, stride, value):
    for t in range(scr.shape[0]):
        scr[t, pl.ds(start, count, stride=stride), :] = value[:, t * 128 : (t + 1) * 128]


def joined(scr, rows=slice(None)):
    return jnp.concatenate([scr[t, rows] for t in range(scr.shape[0])], axis=1)


def padded(count):
    return -(-count // 128) * 128


def operand_kernel(cols, sizes, off_ref, *refs):
    x_refs, (wl_ref, wr_ref) = refs[: len(sizes)], refs[len(sizes) : len(sizes) + 2]
    keep_ref, send_ref, n_ref, nc_ref, xc_ref, xs_ref, lscr, rscr, nscr, xscr, cscr, block = refs[-12:]
    rows, n, c = n_ref.shape
    if len(sizes) == 1:
        x_ref = x_refs[0]
    else:
        x_ref = block
        at = 0
        for size, ref in zip(sizes, x_refs):

            @pl.when(pl.program_id(0) == at // rows)
            def _(ref=ref, first=at % rows, size=size):
                block[first : first + size] = ref[...]

            at += size
    wide = nc_ref.shape[1]
    half = c // 2
    own = off_ref[0]
    other = off_ref[1]
    for k in range(rows):
        x = x_ref[k].astype(F32)
        nrm, _ = norm(x)
        low = nrm.astype(BF)
        n_ref[k] = low
        nscr[k] = nrm
        xscr[k] = x
        p = nt(wl_ref[...], low)
        spread(lscr, k, c, rows, p[:c] * sigm(p[c:]))
    blank = [jnp.zeros((wide - 2 * cols, c), F32)] if wide > 2 * cols else []
    for k in range(rows):
        mine, theirs = nscr[k, pl.ds(own, cols), :], nscr[k, pl.ds(other, cols), :]
        near = jnp.concatenate([mine, theirs] + blank, axis=0).astype(BF)
        nc_ref[k] = near
        turned = jnp.concatenate([theirs, mine] + blank, axis=0).astype(BF)
        p = nt(wr_ref[:c], near)
        spread(rscr, k, half, rows, p[:half] * sigm(p[half:]))
        p = nt(wr_ref[c:], turned)
        spread(rscr, half * rows + k, half, rows, p[:half] * sigm(p[half:]))
        cscr[pl.ds(k, cols, stride=rows), :] = xscr[k, pl.ds(own, cols), :]
        cscr[pl.ds(cols * rows + k, cols, stride=rows), :] = xscr[k, pl.ds(other, cols), :]
    cut = half * rows
    for ref, span in ((keep_ref, slice(0, cut)), (send_ref, slice(cut, None))):
        both = jnp.concatenate([joined(lscr, span), joined(rscr, span)], axis=1)
        ref[...] = both.astype(BF).reshape(ref.shape)
    xc_ref[...] = cscr[:cols * rows].astype(BF).reshape(xc_ref.shape)
    xs_ref[...] = cscr[cols * rows:].astype(BF).reshape(xs_ref.shape)


def operands(offs, parts, wl, wr, cols, start, total, bufs):
    n, c = parts[0].shape[1:]
    count = sum(p.shape[0] for p in parts)
    half = c // 2
    wide = padded(2 * cols)
    g = GROUP
    at = start // g
    shapes = [
        ((half, count, n + wide), (half, g, n + wide), lambda b, o: (0, b, 0)),
        ((half, count, n + wide), (half, g, n + wide), lambda b, o: (0, b, 0)),
        ((total, n, c), (g, n, c), lambda b, o: (at + b, 0, 0)),
        ((total, wide, c), (g, wide, c), lambda b, o: (at + b, 0, 0)),
        ((cols, total, c), (cols, g, c), lambda b, o: (0, o[2 + b], 0)),
        ((cols, total, c), (cols, g, c), lambda b, o: (0, o[2 + b], 0)),
    ]
    full = lambda v: pl.BlockSpec(v.shape, lambda b, o: (0,) * v.ndim)
    ins = [*parts, wl, wr]
    rows = [pl.BlockSpec((g, n, c), lambda b, o: (b, 0, 0))] if len(parts) == 1 else [full(p) for p in parts]
    specs = rows + [full(wl), full(wr)]
    alias = {}
    if bufs is not None:
        alias = {1 + len(ins) + i: 2 + i for i in range(4)}
        ins += list(bufs)
        specs += [pl.BlockSpec(memory_space=pl.ANY)] * 4
    got = pl.pallas_call(
        functools.partial(operand_kernel, cols, tuple(p.shape[0] for p in parts)),
        grid_spec=pltpu.PrefetchScalarGridSpec(
            num_scalar_prefetch=1,
            grid=(count // g,),
            in_specs=specs,
            out_specs=[pl.BlockSpec(b, m) for _, b, m in shapes],
            scratch_shapes=[
                pltpu.VMEM((n // 128, c * g, 128), F32),
                pltpu.VMEM((wide // 128, c * g, 128), F32),
                pltpu.VMEM((g, n, c), F32),
                pltpu.VMEM((g, n, c), F32),
                pltpu.VMEM((2 * cols * g, c), F32),
                pltpu.VMEM((g, n, c), BF),
            ],
        ),
        out_shape=[jax.ShapeDtypeStruct(s, BF) for s, _, _ in shapes],
        input_output_aliases=alias,
        compiler_params=pltpu.CompilerParams(vmem_limit_bytes=60 << 20),
        cost_estimate=cost(3e9 * count, 8 * count * n * c),
        name="operands",
    )(offs, *ins)
    return got[0], got[1], got[2:]


def product_kernel(groups, *refs):
    mine_ref, theirs_ref, scr = refs[groups:]
    g = refs[0].shape[0]
    cols, _, n = mine_ref.shape
    for e in range(g):
        both = jnp.concatenate([r[e] for r in refs[:groups]], axis=0)
        part = lax.dot_general(
            both[:, n:], both[:, :n], (((0,), (0,)), ((), ())), preferred_element_type=F32
        )
        spread(scr, e, 2 * cols, g, part[: 2 * cols])
    mine_ref[...] = joined(scr, slice(0, cols * g)).astype(mine_ref.dtype).reshape(mine_ref.shape)
    theirs_ref[...] = joined(scr, slice(cols * g, None)).astype(theirs_ref.dtype).reshape(theirs_ref.shape)


def products(sets, cols, n):
    half, _, wide = sets[0].shape
    wide -= n
    g = GROUP
    out = jax.ShapeDtypeStruct((cols, half, n), BF)
    return pl.pallas_call(
        functools.partial(product_kernel, len(sets)),
        grid=(half // g,),
        in_specs=[pl.BlockSpec((g,) + v.shape[1:], lambda b: (b, 0, 0)) for v in sets],
        out_specs=[pl.BlockSpec((cols, g, n), lambda b: (0, b, 0))] * 2,
        out_shape=[out, out],
        scratch_shapes=[pltpu.VMEM((n // 128, 2 * cols * g, 128), F32)],
        compiler_params=pltpu.CompilerParams(vmem_limit_bytes=56 << 20),
        cost_estimate=cost(2 * half * n * n * wide, 4 * half * n * n),
        name="products",
    )(*sets)


def batch(count, most):
    return max(b for b in range(1, most + 1) if count % b == 0)


def product_rows(mine_ref, theirs_ref):
    return jnp.concatenate(
        [
            jnp.concatenate([mine_ref[b].astype(F32), theirs_ref[b].astype(F32)], axis=0).T
            for b in range(mine_ref.shape[0])
        ],
        axis=0,
    )


def after_kernel(heads, core_ref, xm_ref, xo_ref, mine_ref, theirs_ref, w4_ref, wout_ref, wb_ref, vec_ref,
                 after_ref, bias_ref, xc_ref, bscr):
    cb, n, c = xc_ref.shape
    first = core_ref[0] == 0
    span = core_ref.shape[0]
    parts = []
    for b in range(cb):
        near, far = xm_ref[b].astype(F32), xo_ref[b].astype(F32)
        low, high = jnp.where(first, near, far), jnp.where(first, far, near)
        for r in range(0, n // 2, span):
            parts += [low[r:r + span], high[r:r + span]]
    x = jnp.concatenate(parts, axis=0)
    xc_ref[...] = x.astype(BF).reshape(xc_ref.shape)
    n0, _ = norm(x)
    gate = sigm(nn(n0.astype(BF), w4_ref[...]))
    nc, _ = norm(product_rows(mine_ref, theirs_ref))
    lin = nn((nc * vec_ref[1:2, :]).astype(BF), wout_ref[...])
    after = x + (gate * lin).astype(BF).astype(F32)
    after_ref[...] = after.reshape(after_ref.shape)
    n3, _ = norm(after)
    bias = nt(wb_ref[...], (n3 * vec_ref[2:3, :]).astype(BF))
    for b in range(cb):
        for h in range(heads):
            at = pl.program_id(0) * cb + b
            bscr[pl.ds(at, 1), h * n:(h + 1) * n] = bias[h:h + 1, b * n:(b + 1) * n]

    @pl.when(pl.program_id(0) == pl.num_programs(0) - 1)
    def _():
        bias_ref[...] = bscr[...].astype(BF)


def afters(core, xm, xo, mine, theirs, w4, wout, wb, vec, heads):
    cols, rows, c = xm.shape
    n = 2 * rows
    half = mine.shape[1]
    cb = batch(cols, AFTER_BATCH)
    full = lambda v: pl.BlockSpec(v.shape, lambda b: (0,) * v.ndim)
    col = lambda a, b: pl.BlockSpec((cb, a, b), lambda j: (j, 0, 0))
    return pl.pallas_call(
        functools.partial(after_kernel, heads),
        grid=(cols // cb,),
        in_specs=[pl.BlockSpec(memory_space=pltpu.SMEM), col(rows, c), col(rows, c), col(half, n), col(half, n)]
        + [full(v) for v in (w4, wout, wb, vec)],
        out_specs=[col(n, c), pl.BlockSpec((cols, heads * n), lambda j: (0, 0)), col(n, c)],
        out_shape=[
            jax.ShapeDtypeStruct((cols, n, c), F32),
            jax.ShapeDtypeStruct((cols, heads * n), BF),
            jax.ShapeDtypeStruct((cols, n, c), BF),
        ],
        scratch_shapes=[pltpu.VMEM((cols, heads * n), F32)],
        compiler_params=pltpu.CompilerParams(vmem_limit_bytes=56 << 20),
        cost_estimate=cost(8 * cols * n * c * c, 10 * cols * n * c, cols * n * c),
        name="afters",
    )(core, xm, xo, mine, theirs, w4, wout, wb, vec)


def back_kernel(after_ref, gx_ref, gmid_ref, gb_ref, xc_ref, mine_ref, theirs_ref, w4_ref, wout_ref, wb_ref, vec_ref,
                gmine_ref, gtheirs_ref, gwb_ref, gwout_ref, gw4_ref, small_ref):
    @pl.when(pl.program_id(0) == 0)
    def _():
        for ref in (gwb_ref, gwout_ref, gw4_ref, small_ref):
            ref[...] = jnp.zeros_like(ref)

    cb, n, c = xc_ref.shape
    half = mine_ref.shape[1]
    heads = gb_ref.shape[2]
    flat = lambda ref: ref[...].reshape(cb * n, c)
    g1 = vec_ref[1:2, :]
    g2 = vec_ref[2:3, :]
    n3, s3 = norm(flat(after_ref))
    x3 = (n3 * g2).astype(BF)
    parts = []
    for b in range(cb):
        gb = gb_ref[0, b].astype(F32)
        for d in range(1, gb_ref.shape[0]):
            gb = gb + gb_ref[d, b].astype(F32)
        parts.append(jnp.concatenate([gb, jnp.zeros((wb_ref.shape[0] - heads, n), F32)], axis=0))
    gb = jnp.concatenate(parts, axis=1)
    gwb_ref[...] += nn(gb.astype(BF), x3)
    gx = (flat(gx_ref) + nn(gb.T.astype(BF), wb_ref[...])).astype(BF).astype(F32)
    small_ref[0:1, :] += jnp.sum(gx * n3, axis=0, keepdims=True)
    gafter = (flat(gmid_ref) + norm_back(gx, g2, n3, s3)).astype(BF).astype(F32)

    n0, _ = norm(flat(xc_ref).astype(F32))
    n0 = n0.astype(BF)
    gate = sigm(nn(n0, w4_ref[...]))
    nc, sc = norm(product_rows(mine_ref, theirs_ref))
    centre = (nc * g1).astype(BF)
    lin = nn(centre, wout_ref[...])
    glin = (gafter * gate).astype(BF)
    gp4 = (gafter * lin * gate * (1.0 - gate)).astype(BF)
    gwout_ref[...] += nn(centre.astype(F32).T.astype(BF), glin)
    gw4_ref[...] += nn(n0.astype(F32).T.astype(BF), gp4)
    gc = nt(glin, wout_ref[...]).astype(BF).astype(F32)
    small_ref[1:2, :] += jnp.sum(gc * nc, axis=0, keepdims=True)
    gprod = norm_back(gc, g1, nc, sc)
    for b in range(cb):
        part = gprod[b * n:(b + 1) * n].T.astype(BF)
        gmine_ref[b] = part[:half]
        gtheirs_ref[b] = part[half:]


def back_pass(after, gx, gmid, gb, xc, mine, theirs, w4, wout, wb, vec):
    cols, n, c = xc.shape
    half = mine.shape[1]
    heads = gb.shape[2]
    cb = batch(cols, BACK_BATCH)
    full = lambda shape: pl.BlockSpec(shape, lambda b: (0,) * len(shape))
    col = lambda a, b: pl.BlockSpec((cb, a, b), lambda j: (j, 0, 0))
    accs = [wb.shape, (c, c), (c, c), (8, c)]
    return pl.pallas_call(
        back_kernel,
        grid=(cols // cb,),
        in_specs=[col(n, c)] * 3
        + [pl.BlockSpec((gb.shape[0], cb, heads, n), lambda j: (0, j, 0, 0)), col(n, c), col(half, n), col(half, n)]
        + [full(v.shape) for v in (w4, wout, wb, vec)],
        out_specs=[col(half, n)] * 2 + [full(s) for s in accs],
        out_shape=[jax.ShapeDtypeStruct((cols, half, n), BF)] * 2 + [jax.ShapeDtypeStruct(s, F32) for s in accs],
        compiler_params=pltpu.CompilerParams(vmem_limit_bytes=56 << 20),
        cost_estimate=cost(16 * cols * n * c * c, 24 * cols * n * c, cols * n * c),
        name="back",
    )(after, gx, gmid, gb, xc, mine, theirs, w4, wout, wb, vec)


def operand_grads_kernel(groups, *refs):
    sets = [refs[:groups], refs[groups:2 * groups]]
    gm_ref, gt_ref, keep_ref, send_ref, scr, lscr, rscr = refs[2 * groups:]
    cols, g, n = gm_ref.shape
    rows = keep_ref.shape[0]
    wide = keep_ref.shape[2] - n
    gm = gm_ref[...].astype(F32).reshape(cols * g, n)
    gt = gt_ref[...].astype(F32).reshape(cols * g, n)
    for t in range(n // 128):
        scr[t, : cols * g] = gm[:, t * 128 : (t + 1) * 128]
        scr[t, cols * g :] = gt[:, t * 128 : (t + 1) * 128]
    blank = [jnp.zeros((wide - 2 * cols, n), F32)] if wide > 2 * cols else []
    fetch = lambda at: jnp.concatenate([scr[t, pl.ds(at, cols, stride=g), :] for t in range(n // 128)], axis=1)
    for part, out_ref in enumerate((keep_ref, send_ref)):
        for e in range(g):
            pieces = [fetch(e), fetch(cols * g + e)]
            gp = jnp.concatenate(pieces + blank, axis=0).astype(BF)
            seen = gp if part == 0 else jnp.concatenate(pieces[::-1] + blank, axis=0).astype(BF)
            both = jnp.concatenate([r[e] for r in sets[part]], axis=0)
            spread(rscr, e, rows, g, nt(both[:, :n], seen))
            spread(lscr, e, rows, g, nn(both[:, n:], gp))
        both = jnp.concatenate([joined(lscr), joined(rscr)], axis=1)
        out_ref[...] = both.astype(BF).reshape(out_ref.shape)


def operand_grads(keep, recv, gmine, gtheirs):
    half, _, lanes = keep[0].shape
    rows = sum(v.shape[1] for v in keep)
    cols, _, n = gmine.shape
    wide = lanes - n
    g = GROUP
    out = jax.ShapeDtypeStruct((rows, half, lanes), BF)
    return pl.pallas_call(
        functools.partial(operand_grads_kernel, len(keep)),
        grid=(half // g,),
        in_specs=[pl.BlockSpec((g,) + v.shape[1:], lambda b: (b, 0, 0)) for v in keep + recv]
        + [pl.BlockSpec((cols, g, n), lambda b: (0, b, 0))] * 2,
        out_specs=[pl.BlockSpec((rows, g, lanes), lambda b: (0, b, 0))] * 2,
        out_shape=[out, out],
        scratch_shapes=[
            pltpu.VMEM((n // 128, 2 * cols * g, 128), F32),
            pltpu.VMEM((n // 128, rows * g, 128), F32),
            pltpu.VMEM((wide // 128, rows * g, 128), F32),
        ],
        compiler_params=pltpu.CompilerParams(vmem_limit_bytes=60 << 20),
        cost_estimate=cost(4 * half * n * n * wide, 8 * half * n * n),
        name="operand_grads",
    )(*keep, *recv, gmine, gtheirs)


def tri_grads_kernel(n_ref, nc_ref, g_ref, wl_ref, wr_ref, al_ref, ar_ref, lg, rg):
    @pl.when(pl.program_id(0) == 0)
    def _():
        al_ref[...] = jnp.zeros_like(al_ref)
        ar_ref[...] = jnp.zeros_like(ar_ref)
    rows, n, c = n_ref.shape
    wide = nc_ref.shape[1]
    half = g_ref.shape[1]
    def one(low, grad, w):
        p = nt(w, low)
        s = sigm(p[half:])
        first = grad.astype(F32) * s
        return first.astype(BF), (first * p[:half] * (1.0 - s)).astype(BF)
    for k in range(rows):
        a, b = one(n_ref[k], g_ref[k, :, :n], wl_ref[...])
        lg[:half, k*n:(k+1)*n] = a
        lg[half:, k*n:(k+1)*n] = b
        a, b = one(nc_ref[k], g_ref[k, :, n:], wr_ref[...])
        rg[:half, k*wide:(k+1)*wide] = a
        rg[half:, k*wide:(k+1)*wide] = b
    al_ref[...] += nn(lg[...], n_ref[...].reshape(rows*n, c))
    ar_ref[...] += nn(rg[...], nc_ref[...].reshape(rows*wide, c))


def tri_grads(nrm, near, grad, wl, wr):
    count, n, c = nrm.shape
    half = grad.shape[1]
    wide = near.shape[1]
    rows = batch(count, 24)
    full = lambda v: pl.BlockSpec(v.shape, lambda b: (0,) * v.ndim)
    row = lambda a, b: pl.BlockSpec((rows, a, b), lambda k: (k, 0, 0))
    out = jax.ShapeDtypeStruct((2 * half, c), F32)
    return pl.pallas_call(
        tri_grads_kernel,
        grid=(count // rows,),
        in_specs=[row(n, c), row(wide, c), row(half, n + wide), full(wl), full(wr)],
        out_specs=[pl.BlockSpec(out.shape, lambda k: (0, 0))] * 2,
        out_shape=[out] * 2,
        scratch_shapes=[pltpu.VMEM((2*half, rows*n), BF), pltpu.VMEM((2*half, rows*wide), BF)],
        compiler_params=pltpu.CompilerParams(vmem_limit_bytes=56 << 20),
        cost_estimate=cost(8 * count * n * c * c, 8 * count * n * c, count * n * half),
        name="tri_grads",
    )(nrm, near, grad, wl, wr)


def adam_kernel(scale_ref, sum_ref, shrink_ref, bias_ref, vec_ref, *refs):
    masters, firsts, seconds = refs[:8], refs[8:16], refs[16:24]
    new_masters, new_firsts, new_seconds = refs[24:32], refs[32:40], refs[40:]
    at = [0]

    def take(ref):
        at[0] += ref.shape[-1]
        return sum_ref[:, at[0] - ref.shape[-1] : at[0]]

    grads = {slot: take(masters[slot]) for slot in (2, 4, 5, 1, 0)}
    grads.update({3: bias_ref[...], 6: shrink_ref[...], 7: vec_ref[...]})
    for slot in range(8):
        whole = (lambda ref: ref[...]) if slot == 7 else (lambda ref: ref[0])
        clipped = grads[slot] * scale_ref[0]
        master = whole(masters[slot])
        moment = beta_first * whole(firsts[slot]) + (1 - beta_first) * clipped
        square = beta_second * whole(seconds[slot]) + (1 - beta_second) * clipped * clipped
        stride = (
            moment
            / (1 - beta_first**STEP)
            / (jnp.sqrt(square / (1 - beta_second**STEP)) + adam_epsilon)
        )
        rate = vector_rate if slot == 7 else learn_rate
        fresh = (master - rate * (stride + weight_decay * master), moment, square)
        for refs_out, value in zip((new_masters, new_firsts, new_seconds), fresh):
            if slot == 7:
                refs_out[slot][...] = value
            else:
                refs_out[slot][0] = value


def adam(scale, total, shrink, bias, vec, masters, firsts, seconds):
    ins = [total, shrink, bias, vec, *masters, *firsts, *seconds]
    vmem = pl.BlockSpec(memory_space=pltpu.VMEM)
    return pl.pallas_call(
        adam_kernel,
        in_specs=[pl.BlockSpec(memory_space=pltpu.SMEM)] + [vmem] * len(ins),
        out_specs=[vmem] * 24,
        out_shape=[jax.ShapeDtypeStruct(v.shape, F32) for v in [*masters, *firsts, *seconds]],
        compiler_params=pltpu.CompilerParams(vmem_limit_bytes=40 << 20),
        name="adam",
    )(scale, *ins)


def gather_weights(tri, tri_out, attn, bias, outp, expand, shrink, vectors):
    rows = tri.shape[1]
    pieces = [tri[0], tri_out[0], attn[0], outp[0], expand[0], shrink[0].reshape(rows, -1), bias[0], vectors.T]
    widths = [p.shape[1] for p in pieces]
    packed = jnp.concatenate(all_item(jnp.concatenate([p.astype(BF) for p in pieces], axis=1)))
    got, at = [], 0
    for w in widths:
        got.append(packed[:, at : at + w])
        at += w
    tri, tri_out, attn, outp, expand, shr, bias, vec = got
    return tri, tri_out, attn, bias, outp, expand, shr.reshape(-1, shrink.shape[2]), vec.T


def project_rows(rows, project, size, first):
    here = lax.axis_index("pair")
    count = rows.shape[0]
    if size != 8 or count % 48:
        sets = [list(range(c, size, 2)) for c in range(2)]
        got = lax.all_gather(rows, "pair", axis=0, tiled=True, axis_index_groups=sets)
        return [project([got], list(range(got.shape[0] // GROUP)))], first
    stages = 3
    step = count // stages
    per = step // GROUP
    x = [rows[s * step : (s + 1) * step] for s in range(stages)] + [None]
    spot = lambda device, s: [device // 2 * (stages * per) + s * per + u for u in range(per)]
    send = lambda value: [exchange(value, "pair", 2), exchange(value, "pair", 4)]
    near, late = send(x[0]), []
    done = [project([rows], [p for s in range(stages) for p in spot(here, s)])]
    for s in range(stages):
        waits = [x[s + 1], near, late, done[-1][0]]
        if s == 1:
            waits.append(first)
        if s:
            waits.append(done[-2][1])
        held = lax.optimization_barrier(tuple(waits))
        following, near, arrived, done[-1][0] = held[:4]
        if s == 1:
            first = held[4]
        if s:
            done[-2][1] = held[-1]
        late = [exchange(near[0][: step // 2], "pair", 4), exchange(near[1][step // 2 :], "pair", 2)]
        places = spot(here ^ 2, s) + spot(here ^ 4, s) + (spot(here ^ 6, s - 1) if arrived else [])
        group = list(near) + list(arrived)
        if s + 1 < stages:
            near = send(following)
        done.append(project(group, places))
    late, done[-1][0], done[-2][1] = lax.optimization_barrier((late, done[-1][0], done[-2][1]))
    done.append(project(list(late), spot(here ^ 6, stages - 1)))
    return done, first


def swap_cores(value):
    size = lax.axis_size("pair")
    return lax.ppermute(value, "pair", [(d, d ^ 1) for d in range(size)])


def exchange(value, axis, bit):
    size = lax.axis_size(axis)
    return lax.ppermute(value, axis, [(d, d ^ bit) for d in range(size)])


def sum_axis(value, axis):
    bit = 1
    while bit < lax.axis_size(axis):
        value = value + exchange(value, axis, bit)
        bit *= 2
    return value


def sum_item(part, beside=()):
    bit = lax.axis_size("item") // 2
    here = lax.axis_index("item")
    beside = list(beside)
    while bit:
        upper = (here // bit) % 2
        rows = part.shape[0] // 2
        kept = lax.dynamic_slice_in_dim(part, upper * rows, rows, 0)
        sent = lax.dynamic_slice_in_dim(part, (1 - upper) * rows, rows, 0)
        got = exchange(sent.astype(BF), "item", bit)
        if beside:
            work = beside.pop(0)
            got, work[0] = lax.optimization_barrier((got, work[0]))
        part = kept + got.astype(F32)
        bit //= 2
    return part


def all_item(value):
    size = lax.axis_size("item")
    here = lax.axis_index("item")
    got = jnp.stack([value] + [exchange(value, "item", bit) for bit in range(1, size)])
    return [lax.dynamic_index_in_dim(got, here ^ t, 0, keepdims=False) for t in range(size)]


def on_device(
    pair_act,
    targets,
    pair_mask,
    tri_proj,
    tri_out,
    attention_proj,
    bias_proj,
    output_proj,
    expand_proj,
    shrink_proj,
    vectors,
    first_tri,
    first_tri_out,
    first_attention,
    first_bias,
    first_output,
    first_expand,
    first_shrink,
    first_vectors,
    second_tri,
    second_tri_out,
    second_attention,
    second_bias,
    second_output,
    second_expand,
    second_shrink,
    second_vectors,
):
    layers = attention_proj.shape[0]
    assert layers == 1
    cols, tokens, width = pair_act.shape[1:]
    half = width // 2
    heads = bias_proj.shape[2]
    here = lax.axis_index("pair")
    core = here % 2
    weight = gather_weights(
        tri_proj, tri_out, attention_proj, bias_proj, output_proj, expand_proj, shrink_proj, vectors
    )
    tri_w, tri_out_w, project_w, pairbias_w, output_w, expand_w, shrink_w, vector_low = weight
    vec = vector_low.astype(F32)
    weighting_rows = pair_mask.astype(F32)
    both = lax.all_gather(
        jnp.concatenate([targets, weighting_rows]), "pair", axis=1, tiled=True
    )
    both = lax.dynamic_slice_in_dim(both, here * cols, cols, 2)

    scaled = (tri_w.astype(F32) * vec[0][:, None]).astype(BF).T
    tri_half = lambda s, c: lax.dynamic_slice_in_dim(scaled, width * s + half * c, half, 0)
    near_w = [tri_half(s, core) for s in range(4)]
    far_w = [tri_half(s, 1 - core) for s in range(4)]
    w_left = jnp.concatenate([near_w[0], far_w[0], near_w[1], far_w[1]])
    w_right = jnp.concatenate([near_w[2], near_w[3], far_w[2], far_w[3]])
    w_gate = scaled[4 * width :].T
    wout = jnp.roll(tri_out_w, -half * core, axis=0)
    gain_c = jnp.roll(vec[1], -half * core)
    vec8 = jnp.concatenate([vec[:1], gain_c[None], vec[2:], jnp.zeros((3, width), F32)])
    wb = jnp.concatenate([pairbias_w.T, jnp.zeros((16 - heads, width), BF)])

    state = {"bufs": None, "start": 0}

    def project(rows, places):
        offs = jnp.stack([here * cols, (here + 1 - 2 * core) * cols, *places]).astype(jnp.int32)
        mine, sent, state["bufs"] = operands(
            offs, rows, w_left, w_right, cols, state["start"], tokens // 2, state["bufs"]
        )
        state["start"] += sum(r.shape[0] for r in rows)
        return [mine, swap_cores(sent)]

    done, both = project_rows(pair_act[0], project, lax.axis_size("pair"), both)
    keep, recv = [v[0] for v in done], [v[1] for v in done]
    bufs = state["bufs"]
    nrm, near, xm, xs = bufs
    xo = swap_cores(xs)
    mine, send = products(keep + recv, cols, tokens)
    theirs = swap_cores(send)
    cores = jnp.full((cols,), core, jnp.int32)
    after_c, bias_part, xc = afters(cores, xm, xo, mine, theirs, w_gate, wout, wb, vec8, heads)
    bias_full = lax.all_gather(bias_part, "pair", axis=0, tiled=True)
    hidden = expand_w.shape[1] // 2
    z = jnp.sum(shrink_w.astype(F32) * vec[4], axis=1)[None]
    gx, gmid, gb, gkv_w, gqg_w, gow, gew, svec, small = column_pass(
        after_c, both[0], both[1], bias_full, project_w, project_w.T, output_w, expand_w, vec8, z
    )
    bias_cols = lax.all_to_all(gb, "pair", split_axis=0, concat_axis=0, tiled=True)
    gmine, gsend, gwb, gwout, gw4, small2 = back_pass(
        after_c, gx, gmid, bias_cols.reshape(-1, cols, heads, tokens), xc, mine, theirs,
        w_gate, wout, wb, vec8,
    )
    early = jnp.concatenate(
            [
                gqg_w[:width].T,
                gkv_w,
                gqg_w[width:].T,
                gow,
                gew,
                jnp.roll(gwout, half * core, axis=0),
                gw4 * vec[0][:, None],
                gwb[:heads].T,
                jnp.roll(small2[1], half * core)[:, None],
                small2[0][:, None],
                small[1][:, None],
                (small[0] + jnp.sum(svec[0][:, None] * shrink_w.astype(F32), axis=0))[:, None],
                svec.reshape(width, -1),
            ],
            axis=1,
        )
    gtheirs = swap_cores(gsend)
    grad_keep, grad_sent = operand_grads(keep, recv, gmine, gtheirs)
    grad_far = swap_cores(grad_sent)
    w_l = [jnp.concatenate([w[0], w[1]]) for w in (near_w, far_w)]
    w_r = [jnp.concatenate([w[2], w[3]]) for w in (near_w, far_w)]
    near_a = list(tri_grads(nrm, near, grad_keep, w_l[0], w_r[0]))
    far_a = list(tri_grads(nrm, near, grad_far, w_l[1], w_r[1]))
    early = sum_item(early, (near_a, far_a))
    a_tri = []
    for near_part, far_part in zip(near_a, far_a):
        for s in range(2):
            parts = [p[s * half : (s + 1) * half] for p in (near_part, far_part)]
            a_tri += [jnp.where(core == 0, parts[0], parts[1]), jnp.where(core == 0, parts[1], parts[0])]
    a_tri = jnp.concatenate(a_tri + [gw4.T]).T
    g_gain = jnp.sum(a_tri * tri_w.astype(F32), axis=1)[:, None]
    late = sum_item(jnp.concatenate([a_tri[:, : 4 * width] * vec[0][:, None], g_gain], axis=1))
    cut = 8 * width + 2 * hidden - width
    joint = sum_axis(
        jnp.concatenate(
            [
                early[:, : cut - width],
                late[:, : 4 * width],
                early[:, cut - width :],
                late[:, 4 * width :],
                jnp.pad(jnp.stack([jnp.sum(small[2]), jnp.sum(weighting_rows)]), (0, late.shape[0] - 2))[:, None],
            ],
            axis=1,
        ),
        "pair",
    )
    total = joint[:, : cut + 4 * width]
    rest = joint[:, cut + 4 * width :]
    g_bias, g_vec, g_svec = rest[:, :heads], rest[:, heads : heads + 4], rest[:, heads + 4 : -2]
    g_gain = rest[:, -2:-1]
    g_vec = jnp.concatenate([g_gain, g_vec], axis=1).T
    g_shrink = g_svec.reshape(-1, 1) * vec[4][None, :]
    squares = (
        jnp.sum(total * total)
        + jnp.sum(g_bias * g_bias)
        + jnp.sum(g_vec * g_vec)
        + jnp.sum(g_svec * g_svec) * jnp.sum(vec[4] * vec[4])
    )
    sums = sum(all_item(jnp.stack([squares, rest[0, -1], rest[1, -1]])))
    loss_sum, count = sums[1], sums[2]
    grad_norm = jnp.sqrt(sums[0]) / count
    factor = jnp.minimum(1.0, clip_limit / (grad_norm + 1e-06))
    masters = (
        tri_proj,
        tri_out,
        attention_proj,
        bias_proj,
        output_proj,
        expand_proj,
        shrink_proj,
        vectors,
    )
    firsts = (
        first_tri,
        first_tri_out,
        first_attention,
        first_bias,
        first_output,
        first_expand,
        first_shrink,
        first_vectors,
    )
    seconds = (
        second_tri,
        second_tri_out,
        second_attention,
        second_bias,
        second_output,
        second_expand,
        second_shrink,
        second_vectors,
    )
    outs = adam(
        (factor / count)[None], total, g_shrink, g_bias, g_vec, masters, firsts, seconds
    )
    return (loss_sum, count, grad_norm) + tuple(outs)


def solution(mesh):
    in_specs = (
        P("item", "pair", None, None),
        P("item", "pair", None),
        P("item", "pair", None),
        P(None, "item", None),
        P(None, "item", None),
        P(None, "item", None),
        P(None, "item", None),
        P(None, "item", None),
        P(None, "item", None),
        P(None, "item", None),
        P(None, "item"),
        P(None, "item", None),
        P(None, "item", None),
        P(None, "item", None),
        P(None, "item", None),
        P(None, "item", None),
        P(None, "item", None),
        P(None, "item", None),
        P(None, "item"),
        P(None, "item", None),
        P(None, "item", None),
        P(None, "item", None),
        P(None, "item", None),
        P(None, "item", None),
        P(None, "item", None),
        P(None, "item", None),
        P(None, "item"),
    )
    out_specs = (
        P(),
        P(),
        P(),
        P(None, "item", None),
        P(None, "item", None),
        P(None, "item", None),
        P(None, "item", None),
        P(None, "item", None),
        P(None, "item", None),
        P(None, "item", None),
        P(None, "item"),
        P(None, "item", None),
        P(None, "item", None),
        P(None, "item", None),
        P(None, "item", None),
        P(None, "item", None),
        P(None, "item", None),
        P(None, "item", None),
        P(None, "item"),
        P(None, "item", None),
        P(None, "item", None),
        P(None, "item", None),
        P(None, "item", None),
        P(None, "item", None),
        P(None, "item", None),
        P(None, "item", None),
        P(None, "item"),
    )
    return jax.shard_map(
        on_device, mesh=mesh, in_specs=in_specs, out_specs=out_specs, check_vma=False
    )
```
